32 devices in a mesh: gx: 8 (over z, x), gy: 4 (over y, core).
Axes of the slice: x: 2, y: 2, z: 4, core: 2. Of those that a mesh axis runs over, the one named last changes fastest.
Arguments:
- point_counts: int32 [128, 64, 128], P('gx', 'gy'), may hold values from 0 to 16
- face_counts: int32 [3, 128, 64, 128], P(None, 'gx', 'gy'), may hold values from -12 to 12, as said below
Outputs:
- solution: float32 [128, 64, 128], P('gx', 'gy')
- residual: float32 [128, 64, 128], P('gx', 'gy')
The draws below stay inside these ranges and needn't reach their ends.
Inputs may be any that keep to these rules, and one draw needn't show every extreme that they name: `face_counts`: signed count of oriented points splatted onto each upper face.
All inputs are finite; a program needn't handle non-finite values.
Results may differ from the reference program's by a relative error of at most 0.0003.
Values may be sent and summed in bfloat16 or wider, within the bound.
No kernel may reach another device: no remote copies, remote signals or barrier semaphores. Data moves between devices by JAX's collectives and lax.ppermute only.
A program may use at most 64 MiB of HBM per device.

```python
import jax
import jax.numpy as jnp

NZ = 128
LEVELS = 3
CYCLES = 2
PRE = 2
POST = 2
COARSE_ITERS = 6
NX = 128
NY = 64


def draw_point_counts(key, part):
    pos_x = jnp.arange(NX, dtype=jnp.int32)[:, None, None]
    pos_y = jnp.arange(NY, dtype=jnp.int32)[None, :, None]
    pos_z = jnp.arange(NZ, dtype=jnp.int32)[None, None, :]
    spread_sq = (NX // 2) ** 2 + (NY // 2) ** 2
    height = NZ // 4 + NZ // 2 * ((pos_x - NX // 2) ** 2 + (pos_y - NY // 2) ** 2) // spread_sq
    inside = jnp.abs(pos_z - height) <= 1
    key_band, key_noise = jax.random.split(key)
    band_counts = jax.random.randint(key_band, (NX, NY, NZ), 1, 17, dtype=jnp.int32)
    stray_points = (jax.random.randint(key_noise, (NX, NY, NZ), 0, 64, dtype=jnp.int32) == 0).astype(jnp.int32)
    counts = jnp.where(inside, band_counts, stray_points)
    return counts.at[0, 0, 3 * NZ // 4].set(16)


def draw_face_counts(key, part):
    pos_x = jnp.arange(NX, dtype=jnp.int32)[None, :, None, None]
    pos_y = jnp.arange(NY, dtype=jnp.int32)[None, None, :, None]
    amplitude = 2 + 6 * pos_x // NX + 6 * pos_y // NY
    amplitude = jnp.broadcast_to(amplitude, (3, NX, NY, NZ))
    values = jax.random.randint(key, (3, NX, NY, NZ), -amplitude, amplitude + 1, dtype=jnp.int32)
    values = values.at[0, NX - 1, NY - 1, 0].set(12)
    return values.at[1, NX - 1, NY - 1, 0].set(-12)


def setup_inputs(seed: int = 0) -> dict:
    splits = jax.random.split(jax.random.key(seed), 3)
    return {
        "point_counts": draw_point_counts(jax.random.fold_in(splits[2], 71), 0),
        "face_counts": draw_face_counts(jax.random.fold_in(splits[2], 71), 0),
    }


screen_weight = 0.25
flux_scale = 0.125
low_edge = 0.3
high_edge = 2.0


def neighbour_sum(padded):
    total = padded[2:, 1:-1, 1:-1] + padded[:-2, 1:-1, 1:-1]
    total = total + padded[1:-1, 2:, 1:-1] + padded[1:-1, :-2, 1:-1]
    total = total + padded[1:-1, 1:-1, 2:] + padded[1:-1, 1:-1, :-2]
    return total


def operate(field, screen, factor):
    return (6.0 * field - neighbour_sum(jnp.pad(field, 1))) * factor + screen * field


def restrict(field):
    size_x, size_y, size_z = field.shape
    blocks = field.reshape(size_x // 2, 2, size_y // 2, 2, size_z // 2, 2)
    return blocks.sum(axis=(1, 3, 5)) * 0.125


def prolong(field):
    size_x, size_y, size_z = field.shape
    spread_out = jnp.broadcast_to(field[:, None, :, None, :, None], (size_x, 2, size_y, 2, size_z, 2))
    return spread_out.reshape(2 * size_x, 2 * size_y, 2 * size_z)


def smooth(iterate, target, screen, inv_diag, factor, step_count):
    centre = 0.5 * (high_edge + low_edge)
    radius = 0.5 * (high_edge - low_edge)
    spread_ratio = centre / radius
    momentum = 1.0 / spread_ratio
    correction = (target - operate(iterate, screen, factor)) * inv_diag
    update = correction * (1.0 / centre)
    iterate = iterate + update
    for step in range(1, step_count):
        momentum_next = 1.0 / (2.0 * spread_ratio - momentum)
        correction = (target - operate(iterate, screen, factor)) * inv_diag
        update = (momentum_next * momentum) * update + (2.0 * momentum_next / radius) * correction
        iterate = iterate + update
        momentum = momentum_next
    return iterate


def coarse_solve(target, screen, factor):
    iterate = jnp.zeros_like(target)
    remain = target
    search = target
    norm_now = jnp.sum(remain * remain)
    for step in range(COARSE_ITERS):
        image = operate(search, screen, factor)
        step_length = norm_now / jnp.sum(search * image)
        iterate = iterate + step_length * search
        if step + 1 < COARSE_ITERS:
            remain = remain - step_length * image
            norm_next = jnp.sum(remain * remain)
            search = remain + (norm_next / norm_now) * search
            norm_now = norm_next
    return iterate


def vcycle(iterate, target, level_index, screens, inv_diags, factors):
    iterate = smooth(iterate, target, screens[level_index], inv_diags[level_index], factors[level_index], PRE)
    remain = target - operate(iterate, screens[level_index], factors[level_index])
    coarse_target = restrict(remain)
    if level_index + 1 == LEVELS:
        coarse_error = coarse_solve(coarse_target, screens[LEVELS], factors[LEVELS])
    else:
        coarse_error = vcycle(jnp.zeros_like(coarse_target), coarse_target, level_index + 1, screens, inv_diags, factors)
    iterate = iterate + prolong(coarse_error)
    return smooth(iterate, target, screens[level_index], inv_diags[level_index], factors[level_index], POST)


def reference(point_counts, face_counts):
    fluxes = face_counts.astype(jnp.float32) * flux_scale
    lower_x = jnp.pad(fluxes[0], ((1, 0), (0, 0), (0, 0)))[:-1]
    lower_y = jnp.pad(fluxes[1], ((0, 0), (1, 0), (0, 0)))[:, :-1]
    lower_z = jnp.pad(fluxes[2], ((0, 0), (0, 0), (1, 0)))[:, :, :-1]
    source = (lower_x - fluxes[0]) + (lower_y - fluxes[1]) + (lower_z - fluxes[2])
    screens = [point_counts.astype(jnp.float32) * screen_weight]
    for level_index in range(LEVELS):
        screens.append(restrict(screens[-1]))
    factors = [0.25 ** level_index for level_index in range(LEVELS + 1)]
    inv_diags = [1.0 / (6.0 * factors[level_index] + screens[level_index]) for level_index in range(LEVELS)]
    solution = jnp.zeros_like(source)
    for cycle_index in range(CYCLES):
        solution = vcycle(solution, source, 0, screens, inv_diags, factors)
    residual = source - operate(solution, screens[0], factors[0])
    return solution, residual
```

```python
import numpy as np
import jax
import jax.numpy as jnp
from jax import lax
from jax.experimental import pallas as pl
from jax.experimental.pallas import tpu as pltpu
from jax.sharding import Mesh, PartitionSpec as P

F32 = jnp.float32
BF16 = jnp.bfloat16
LANES = 128
HALO = 8
COARSE_ITERS = 6

screen_weight = 0.25
flux_scale = 0.125
low_edge = 0.3
high_edge = 2.0
centre = 0.5 * (high_edge + low_edge)
radius = 0.5 * (high_edge - low_edge)
ratio = centre / radius
mom_first = 1.0 / ratio
mom_second = 1.0 / (2.0 * ratio - mom_first)
keep = mom_second * mom_first
gain = 2.0 * mom_second / radius

VMEM = pl.BlockSpec(memory_space=pltpu.VMEM)
SMEM = pl.BlockSpec(memory_space=pltpu.SMEM)


def transfer_matrix(level):
    pack, size_z = 1 << level, LANES >> level
    planes = 2 if level == 0 else 4
    out = np.zeros((planes * LANES, LANES), np.float32)
    for j in range(planes):
        for q in range(pack):
            coarse = j if level == 0 else (j * pack + q) // 2
            for z in range(size_z):
                out[j * LANES + q * size_z + z, coarse * (size_z // 2) + z // 2] = 1.0
    return jnp.asarray(out, BF16)


def two_parts(value):
    high = value.astype(BF16)
    return high, (value - high.astype(F32)).astype(BF16)


def gather_lanes(value, matrix):
    high, low = two_parts(value)
    return jnp.dot(high, matrix, preferred_element_type=F32) + jnp.dot(low, matrix, preferred_element_type=F32)


def spread_lanes(value, matrix):
    dims = (((1,), (1,)), ((), ()))
    high, low = two_parts(value)
    return lax.dot_general(high, matrix, dims, preferred_element_type=F32) + lax.dot_general(
        low, matrix, dims, preferred_element_type=F32
    )


def lane_index(rows):
    return lax.broadcasted_iota(jnp.int32, (rows, LANES), 1)


def z_sum(value, size_z):
    lane = lane_index(value.shape[0]) & (size_z - 1)
    return jnp.where(lane != 0, pltpu.roll(value, 1, 1), 0.0) + jnp.where(
        lane != size_z - 1, pltpu.roll(value, LANES - 1, 1), 0.0
    )


def x_sum(before, here, after, size_z):
    if size_z == LANES:
        return before + after
    lane = lane_index(here.shape[0])
    if 2 * size_z == LANES:
        return pltpu.roll(here + jnp.where(lane < size_z, after, before), size_z, 1)
    up = pltpu.roll(jnp.where(lane < size_z, after, here), LANES - size_z, 1)
    down = pltpu.roll(jnp.where(lane >= LANES - size_z, before, here), size_z, 1)
    return up + down


def neighbours(ref, base, rows, stride, size_z):
    here = ref[pl.ds(base, rows), :]
    total = x_sum(ref[pl.ds(base - stride, rows), :], here, ref[pl.ds(base + stride, rows), :], size_z)
    total = total + (ref[pl.ds(base - 1, rows), :] + ref[pl.ds(base + 1, rows), :])
    return here, total + z_sum(here, size_z)


def for_planes(count, body, limit=64):
    if count <= limit:
        for i in range(count):
            body(i)
    else:
        step = 8

        def block(k, carry):
            for j in range(step):
                body(k * step + j)
            return carry

        lax.fori_loop(0, count // step, block, 0)


def pair_rows(ref, start, rows):
    return ref[pl.ds(start, rows // 2, stride=2), :] + ref[pl.ds(start + 1, rows // 2, stride=2), :]


def cells_kernel(place, faces, points, first, second, part, count, edge):
    size_x, size_y = points.shape[:2]
    lane = lane_index(size_y)
    row = lax.broadcasted_iota(jnp.int32, (size_y, LANES), 0)
    last_x = None
    for i in range(size_x):
        along_x = faces[0, i]
        along_y = faces[1, i]
        along_z = faces[2, i]
        total = jnp.where(row != 0, pltpu.roll(along_y, 1, 0), 0) - along_y
        total = total + (jnp.where(lane != 0, pltpu.roll(along_z, 1, 1), 0) - along_z) - along_x
        if last_x is not None:
            total = total + last_x
        last_x = along_x
        part[i] = total.astype(F32).astype(BF16)
        count[i] = (points[i] + 1).astype(F32).astype(BF16)
    edge[0] = last_x.astype(F32).astype(BF16)
    edge[1] = faces[1, :, size_y - 1, :].astype(F32).astype(BF16)

    def write(up, down):
        for target, start in ((up, size_x - HALO), (down, 0)):
            target[0:HALO] = part[start : start + HALO]
            target[HALO : 2 * HALO] = count[start : start + HALO]
            target[2 * HALO : 2 * HALO + 2] = edge[...]

    odd = place[0] % 2

    @pl.when(odd == 0)
    def _():
        write(first, second)

    @pl.when(odd == 1)
    def _():
        write(second, first)


def wide_kernel(place, got_first, got_second, part, count, edge, first, second, part_x, count_x, edge_x):
    size_x, size_y = part.shape[:2]
    wide = size_x + 2 * HALO

    def fill(below, above):
        part_x[0:HALO] = below[0:HALO]
        part_x[HALO + size_x :] = above[0:HALO]
        count_x[0:HALO] = below[HALO : 2 * HALO]
        count_x[HALO + size_x :] = above[HALO : 2 * HALO]
        part_x[HALO : HALO + size_x] = part[...]
        count_x[HALO : HALO + size_x] = count[...]
        part_x[HALO] = (part[0].astype(F32) + below[2 * HALO].astype(F32)).astype(BF16)
        part_x[HALO + size_x] = (above[0].astype(F32) + edge[0].astype(F32)).astype(BF16)
        edge_x[0:HALO] = below[2 * HALO + 1].astype(F32)[size_x - HALO :]
        edge_x[HALO : HALO + size_x] = edge[1].astype(F32)
        edge_x[HALO + size_x :] = above[2 * HALO + 1].astype(F32)[:HALO]

    odd = place[0] % 2

    @pl.when(odd == 0)
    def _():
        fill(got_second, got_first)

    @pl.when(odd == 1)
    def _():
        fill(got_first, got_second)

    def write(up, down):
        for i in range(wide):
            cells = part_x[i].astype(F32)
            points = count_x[i].astype(F32)
            up[i] = jnp.concatenate([cells[size_y - HALO :], points[size_y - HALO :]], 0).astype(BF16)
            down[i] = jnp.concatenate([cells[:HALO], points[:HALO]], 0).astype(BF16)
        for target in (up, down):
            for j in range(wide // size_y):
                target[wide + j] = edge_x[j * size_y : (j + 1) * size_y].astype(BF16)

    odd_y = place[1] % 2

    @pl.when(odd_y == 0)
    def _():
        write(first, second)

    @pl.when(odd_y == 1)
    def _():
        write(second, first)


def finest_step_one(source, target, field, scaled, start, end, plane):
    for i in range(start, end, 2):
        base = 8 + i * plane
        rows = 2 * plane
        here, total = neighbours(source, base, rows, plane, LANES)
        fit = (field[pl.ds(base, rows), :] + total) * scaled[pl.ds(base, rows), :]
        target[pl.ds(base, rows), :] = here + (fit - here) * (1.0 / centre)


def finest_step_two(source, old, field, scaled, start, end, plane):
    for i in range(start, end, 2):
        base = 8 + i * plane
        rows = 2 * plane
        here, total = neighbours(source, base, rows, plane, LANES)
        fit = (field[pl.ds(base, rows), :] + total) * scaled[pl.ds(base, rows), :]
        before = old[pl.ds(base, rows), :]
        old[pl.ds(base, rows), :] = here + (keep * (here - before) + gain * (fit - here))


def finest_residual(iterate, field, count, size_x, size_y, write):
    plane = size_y + 2 * HALO
    for i in range(size_x):
        base = 8 + (HALO + i) * plane + HALO
        here, total = neighbours(iterate, base, size_y, plane, LANES)
        diag = 6.0 + screen_weight * (count[HALO + i].astype(F32) - 1.0)
        write(i, here, field[pl.ds(base, size_y), :] + total - diag * here)


def restrict_finest(rows_ref, size_x, size_y, matrix):
    half = pair_rows(rows_ref, 0, size_x * size_y).reshape(size_x // 4, 4, size_y // 2, LANES)
    even = (half[:, 0] + half[:, 1]).reshape(-1, LANES)
    odd = (half[:, 2] + half[:, 3]).reshape(-1, LANES)
    return even, odd


def start_kernel(
    place, got_first, got_second, part_x, count_x, edge_x, matrix, iterate, field, inverse, packet, rows_ref, low, high
):
    wide, size_y = part_x.shape[:2]
    size_x = wide - 2 * HALO
    plane = size_y + 2 * HALO
    odd_y = place[1] % 2

    @pl.when(odd_y == 0)
    def _():
        low[...] = got_second[...]
        high[...] = got_first[...]

    @pl.when(odd_y == 1)
    def _():
        low[...] = got_first[...]
        high[...] = got_second[...]

    top = lax.broadcasted_iota(jnp.int32, (HALO, LANES), 0) == 0
    zero = jnp.zeros((8, LANES), F32)
    for ref in (iterate, field, inverse):
        ref[0:8] = zero
        ref[8 + wide * plane :] = zero
    low_edge_rows = [low[wide + j].astype(F32) for j in range(wide // size_y)]
    for i in range(wide):
        below = low[i].astype(F32)
        above = high[i].astype(F32)
        own = part_x[i].astype(F32)
        under = low_edge_rows[i // size_y][i % size_y : i % size_y + 1]
        over = edge_x[i : i + 1]
        cells = jnp.concatenate(
            [
                below[:HALO],
                own[:HALO] + jnp.where(top, under, 0.0),
                own[HALO:],
                above[:HALO] + jnp.where(top, over, 0.0),
            ],
            0,
        )
        points = jnp.concatenate([below[HALO:], count_x[i].astype(F32), above[HALO:]], 0)
        given = flux_scale * cells
        inv = jnp.where(points > 0.0, 1.0 / (6.0 - screen_weight + screen_weight * points), 0.0)
        base = 8 + i * plane
        field[pl.ds(base, plane), :] = given
        inverse[pl.ds(base, plane), :] = inv
        iterate[pl.ds(base, plane), :] = (given * inv) * (1.0 / centre)

    scratch = rows_ref
    for i in range(1, wide - 1, 2):
        base = 8 + i * plane
        rows = 2 * plane
        here, total = neighbours(iterate, base, rows, plane, LANES)
        fit = (field[pl.ds(base, rows), :] + total) * inverse[pl.ds(base, rows), :]
        scratch[pl.ds(base, rows), :] = here + (keep * here + gain * (fit - here))
    for i in range(1, wide - 1, 2):
        base = 8 + i * plane
        iterate[pl.ds(base, 2 * plane), :] = scratch[pl.ds(base, 2 * plane), :]

    def write(i, here, value):
        scratch[pl.ds(i * size_y, size_y), :] = value

    finest_residual(iterate, field, count_x, size_x, size_y, write)
    even, odd = restrict_finest(scratch, size_x, size_y, matrix)
    coarse = 0.125 * gather_lanes(jnp.concatenate([even, odd], 1), matrix[...])
    for i in range(size_x):
        scratch[pl.ds(i * size_y, size_y), :] = count_x[HALO + i].astype(F32) - 1.0
    even, odd = restrict_finest(scratch, size_x, size_y, matrix)
    points = jnp.dot(jnp.concatenate([even, odd], 1).astype(BF16), matrix[...], preferred_element_type=F32)
    send_coarse(packet, coarse, points, size_y // 2)


def send_coarse(packet, coarse, points, size_y):
    copies = packet.shape[0]
    planes = coarse.shape[0] // size_y
    high = coarse.astype(BF16).astype(F32)
    low = coarse - high
    for i in range(planes):
        at = slice(i * size_y, (i + 1) * size_y)
        tile = jnp.concatenate([high[at], low[at]], 0).astype(BF16)
        for k in range(copies):
            packet[k, i] = tile
    if points is not None:
        for i in range(planes // 2):
            tile = points[2 * i * size_y : 2 * (i + 1) * size_y].astype(BF16)
            for k in range(copies):
                packet[k, planes + i] = tile


def packed_apply(value, screen, factor, size_z):
    planes, size_y, _ = value.shape
    flat = value.reshape(planes * size_y, LANES)
    empty = jnp.zeros((1, size_y, LANES), F32)
    if planes > 1:
        before = jnp.concatenate([empty, value[:-1]], 0).reshape(flat.shape)
        after = jnp.concatenate([value[1:], empty], 0).reshape(flat.shape)
    else:
        before = after = jnp.zeros_like(flat)
    row = lax.broadcasted_iota(jnp.int32, value.shape, 1)
    along_y = jnp.where(row != 0, pltpu.roll(value, 1, 1), 0.0) + jnp.where(
        row != size_y - 1, pltpu.roll(value, size_y - 1, 1), 0.0
    )
    total = x_sum(before, flat, after, size_z) + z_sum(flat, size_z)
    return (6.0 * value - (total.reshape(value.shape) + along_y)) * factor + screen * value


def total_of(value):
    return jnp.sum(jnp.sum(value, 0), keepdims=True)[None]


def conjugate_gradients(target, screen, factor, size_z):
    iterate = jnp.zeros_like(target)
    remain = target
    search = target
    norm_now = total_of(remain * remain)
    for step in range(COARSE_ITERS):
        image = packed_apply(search, screen, factor, size_z)
        length = norm_now / total_of(search * image)
        iterate = iterate + length * search
        if step + 1 < COARSE_ITERS:
            remain = remain - length * image
            norm_next = total_of(remain * remain)
            search = remain + (norm_next / norm_now) * search
            norm_now = norm_next
    return iterate


def smooth_packed(iterate, target, screen, inv, factor, size_z):
    step = (target - packed_apply(iterate, screen, factor, size_z)) * inv * (1.0 / centre)
    iterate = iterate + step
    again = (target - packed_apply(iterate, screen, factor, size_z)) * inv
    return iterate + (keep * step + gain * again)


def smooth_packed_zero(target, screen, inv, factor, size_z):
    step = target * inv * (1.0 / centre)
    again = (target - packed_apply(step, screen, factor, size_z)) * inv
    return step + (keep * step + gain * again)


def add_lanes(rows_ref, planes, size_y, matrix):
    half = pair_rows(rows_ref, 0, planes * size_y).reshape(planes // 4, 4, size_y // 2, LANES)
    wide = jnp.concatenate([half[:, j].reshape(-1, LANES) for j in range(4)], 1)
    return gather_lanes(wide, matrix[...]).reshape(planes // 4, size_y // 2, LANES)


def copy_level(value, matrix):
    planes, size_y, _ = value.shape
    wide = spread_lanes(value.reshape(-1, LANES), matrix[...]).reshape(planes, size_y, 4 * LANES)
    return jnp.stack([wide[:, :, j * LANES : (j + 1) * LANES] for j in range(4)], 1).reshape(
        4 * planes, size_y, LANES
    )


class Sizes:
    def __init__(self, mesh_x, mesh_y, size_x, size_y):
        self.mesh_x, self.mesh_y = mesh_x, mesh_y
        self.own_x, self.own_y = size_x // 4, size_y // 2
        self.planes, self.rows = mesh_x * self.own_x, mesh_y * self.own_y
        self.stride = self.rows + 8
        self.flat = (self.planes + 8) * self.stride + 8
        self.pad_x = 4


def level_one(place, gathered, sizes, mats, refs, first):
    mat_1, mat_2 = mats
    given, inverse, diag, step, iterate, rows_ref, level_two, local_a, local_b = refs
    size_z = LANES // 2
    factor = 0.25
    planes, rows, stride, pad = sizes.planes, sizes.rows, sizes.stride, sizes.pad_x
    own_x, own_y = sizes.own_x, sizes.own_y

    def clear(ref):
        ref[0 : pad * stride + 8] = jnp.zeros((pad * stride + 8, LANES), F32)
        ref[(pad + planes) * stride :] = jnp.zeros((pad * stride + 8, LANES), F32)

        def gap(i):
            ref[pl.ds((pad + i) * stride, 8), :] = jnp.zeros((8, LANES), F32)

        for_planes(planes, gap)

    for ref in (given, step, iterate) + ((inverse, diag) if first else ()):
        clear(ref)

    def block(b):
        gx = b // sizes.mesh_y
        gy = b % sizes.mesh_y
        source = gathered.at[gy % 2, gx * (sizes.mesh_y // 2) + gy // 2]
        for i in range(own_x):
            at = pl.ds((pad + gx * own_x + i) * stride + 8 + gy * own_y, own_y)
            tile = source[i].astype(F32)
            value = tile[:own_y] + tile[own_y:]
            if first:
                points = source[own_x + i // 2].astype(F32)[(i % 2) * own_y : (i % 2 + 1) * own_y]
                d = 6.0 * factor + (screen_weight * 0.125) * points
                diag[at, :] = d
                inv = 1.0 / d
                inverse[at, :] = inv
            else:
                inv = inverse[at, :]
            given[at, :] = value
            step[at, :] = value * inv * (1.0 / centre)

    for_planes(sizes.mesh_x * sizes.mesh_y, block)

    def second(i):
        base = (pad + i) * stride + 8
        at = pl.ds(base, rows)
        here, total = neighbours(step, base, rows, stride, size_z)
        fit = (given[at, :] + factor * total) * inverse[at, :]
        iterate[at, :] = here + (keep * here + gain * (fit - here))

    for_planes(planes, second)

    def residual(i):
        base = (pad + i) * stride + 8
        at = pl.ds(base, rows)
        here, total = neighbours(iterate, base, rows, stride, size_z)
        rows_ref[pl.ds(i * rows, rows), :] = given[at, :] + factor * total - diag[at, :] * here

    for_planes(planes, residual)
    target = 0.125 * add_lanes(rows_ref, planes, rows, mat_1)

    screen_two, screen_three = level_two
    if first:

        def screens(i):
            at = pl.ds((pad + i) * stride + 8, rows)
            rows_ref[pl.ds(i * rows, rows), :] = diag[at, :] - 6.0 * factor

        for_planes(planes, screens)
        screen_two[...] = 0.125 * add_lanes(rows_ref, planes, rows, mat_1)
    planes_2, rows_2 = planes // 4, rows // 2
    screen = screen_two[...]
    inv = 1.0 / (6.0 * factor**2 + screen)
    if first:
        rows_ref[0 : planes_2 * rows_2] = screen.reshape(-1, LANES)
        screen_three[...] = 0.125 * add_lanes(rows_ref, planes_2, rows_2, mat_2)
    value = smooth_packed_zero(target, screen, inv, factor**2, LANES // 4)
    remain = target - packed_apply(value, screen, factor**2, LANES // 4)
    rows_ref[0 : planes_2 * rows_2] = remain.reshape(-1, LANES)
    target_3 = 0.125 * add_lanes(rows_ref, planes_2, rows_2, mat_2)
    error = conjugate_gradients(target_3, screen_three[...], factor**3, LANES // 8)
    error = copy_level(error, mat_2).reshape(-1, LANES)
    count = planes_2 * rows_2
    rows_ref[pl.ds(0, count // 2, stride=2), :] = error
    rows_ref[pl.ds(1, count // 2, stride=2), :] = error
    value = value + rows_ref[0:count].reshape(value.shape)
    value = smooth_packed(value, target, screen, inv, factor**2, LANES // 4)

    rows_ref[0:rows_2] = jnp.zeros((rows_2, LANES), F32)
    rows_ref[(planes_2 + 1) * rows_2 : (planes_2 + 2) * rows_2] = jnp.zeros((rows_2, LANES), F32)
    rows_ref[rows_2 : (planes_2 + 1) * rows_2] = value.reshape(-1, LANES)
    near_2 = own_x // 4 + 2
    start = pl.multiple_of(place[0] * (own_x // 4) * rows_2, 8)
    near = rows_ref[pl.ds(start, near_2 * rows_2), :].reshape(near_2, rows_2, LANES)
    error = copy_level(near, mat_1)
    near_x, near_y = 4 * near_2, own_y + 16
    first_plane = place[0] * own_x
    for i in range(near_x):
        base = (first_plane + i) * stride + 8
        even, odd = pl.ds(base, rows_2, stride=2), pl.ds(base + 1, rows_2, stride=2)
        iterate[even, :] = iterate[even, :] + error[i]
        iterate[odd, :] = iterate[odd, :] + error[i]
    for i in range(near_x):
        at = pl.ds(pl.multiple_of((first_plane + i) * stride + place[1] * own_y, 8), near_y)
        local_a[pl.ds(8 + i * near_y, near_y), :] = iterate[at, :]
    for ref in (local_a, local_b):
        ref[0:8] = jnp.zeros((8, LANES), F32)
        ref[8 + near_x * near_y :] = jnp.zeros((8, LANES), F32)
    ends = pl.ds(8, near_y), pl.ds(8 + (near_x - 1) * near_y, near_y)
    for at in ends:
        local_b[at, :] = jnp.zeros((near_y, LANES), F32)

    def fit_of(ref, i):
        at = pl.ds(pl.multiple_of((first_plane + i) * stride + place[1] * own_y, 8), near_y)
        here, total = neighbours(ref, 8 + i * near_y, near_y, near_y, size_z)
        return here, (given[at, :] + factor * total) * inverse[at, :]

    for i in range(1, near_x - 1):
        here, fit = fit_of(local_a, i)
        local_b[pl.ds(8 + i * near_y, near_y), :] = here + (fit - here) * (1.0 / centre)
    for i in range(2, near_x - 2):
        here, fit = fit_of(local_b, i)
        at = pl.ds(8 + i * near_y, near_y)
        local_a[at, :] = here + (keep * (here - local_a[at, :]) + gain * (fit - here))


def add_correction(iterate, local, sizes, mat_0, plane):
    near_y = sizes.own_y + 16
    half_y = plane // 2
    planes = sizes.own_x + 4
    value = jnp.concatenate(
        [local[pl.ds(8 + (2 + i) * near_y + 4, half_y), :] for i in range(planes)], 0
    )
    wide = spread_lanes(value, mat_0[...])
    for i in range(planes):
        for j in range(4):
            error = wide[i * half_y : (i + 1) * half_y, (j // 2) * LANES : (j // 2 + 1) * LANES]
            for side in (0, 1):
                at = pl.ds(8 + (4 * i + j) * plane + side, half_y, stride=2)
                iterate[at, :] = iterate[at, :] + error


def middle_kernel(sizes, place, gathered, start, field, scaled, count_x, mat_0, mat_1, mat_2, *rest):
    iterate, packet, inverse, diag, screen_two, screen_three = rest[:6]
    given, step, coarse, rows_ref, local_a, local_b, other, fine_rows = rest[6:]
    wide, size_y = count_x.shape[:2]
    size_x = wide - 2 * HALO
    plane = size_y + 2 * HALO
    refs = (given, inverse, diag, step, coarse, rows_ref, (screen_two, screen_three), local_a, local_b)
    iterate[...] = start[...]
    level_one(place, gathered, sizes, (mat_1, mat_2), refs, True)
    add_correction(iterate, local_a, sizes, mat_0, plane)
    other[...] = jnp.zeros_like(other)
    finest_step_one(iterate, other, field, scaled, 2, wide - 2, plane)
    finest_step_two(other, iterate, field, scaled, 3, wide - 3, plane)
    finest_step_one(iterate, other, field, scaled, 4, wide - 4, plane)
    finest_step_two(other, iterate, field, scaled, 5, wide - 5, plane)

    def write(i, here, value):
        fine_rows[pl.ds(i * size_y, size_y), :] = value

    finest_residual(iterate, field, count_x, size_x, size_y, write)
    even, odd = restrict_finest(fine_rows, size_x, size_y, mat_0)
    send_coarse(packet, 0.125 * gather_lanes(jnp.concatenate([even, odd], 1), mat_0[...]), None, size_y // 2)


def last_kernel(sizes, place, gathered, start, field, scaled, count_x, inverse, diag, screen_two, screen_three, *rest):
    mat_0, mat_1, mat_2, solution_out, residual_out = rest[:5]
    given, step, coarse, rows_ref, local_a, local_b, iterate, other = rest[5:]
    wide, size_y = count_x.shape[:2]
    size_x = wide - 2 * HALO
    plane = size_y + 2 * HALO
    refs = (given, inverse, diag, step, coarse, rows_ref, (screen_two, screen_three), local_a, local_b)
    iterate[...] = start[...]
    level_one(place, gathered, sizes, (mat_1, mat_2), refs, False)
    add_correction(iterate, local_a, sizes, mat_0, plane)
    other[...] = jnp.zeros_like(other)
    finest_step_one(iterate, other, field, scaled, HALO - 2, wide - HALO + 2, plane)
    finest_step_two(other, iterate, field, scaled, HALO - 1, wide - HALO + 1, plane)

    def write(i, here, value):
        solution_out[i] = here
        residual_out[i] = value

    finest_residual(iterate, field, count_x, size_x, size_y, write)


def exchange(first, second, axis):
    count = lax.axis_size(axis)

    def pairs(start):
        found = []
        for i in range(start, count - 1, 2):
            found += [(i, i + 1), (i + 1, i)]
        return found

    return lax.ppermute(first, axis, pairs(0)), lax.ppermute(second, axis, pairs(1))


def gather(packet):
    spread = lax.all_to_all(packet, ("gx", "gy_chip"), 0, 0, tiled=True)
    return lax.all_gather(spread, "gy_core", axis=0)


def per_device(point_counts, face_counts):
    size_x, size_y, size_z = point_counts.shape
    assert size_z == LANES and size_x == 16 and size_y == 16
    mesh_x = lax.axis_size("gx")
    mesh_y = lax.axis_size("gy_chip") * lax.axis_size("gy_core")
    gx = lax.axis_index("gx")
    gy = lax.axis_index("gy_chip") * 2 + lax.axis_index("gy_core")
    place = jnp.stack([gx, gy]).astype(jnp.int32)
    wide, plane = size_x + 2 * HALO, size_y + 2 * HALO
    flat = 16 + wide * plane
    sizes = Sizes(mesh_x, mesh_y, size_x, size_y)
    copies = mesh_x * mesh_y // 2
    mats = [transfer_matrix(level) for level in range(3)]
    params = pltpu.CompilerParams(vmem_limit_bytes=(24 if sizes.flat < 4096 else 56) * 2**20)

    def call(kernel, outs, scratch, *args):
        return pl.pallas_call(
            kernel,
            out_shape=[jax.ShapeDtypeStruct(shape, dtype) for shape, dtype in outs],
            in_specs=[SMEM] + [VMEM] * (len(args) - 1),
            out_specs=[VMEM] * len(outs),
            scratch_shapes=[pltpu.VMEM(shape, dtype) for shape, dtype in scratch],
            compiler_params=params,
        )(*args)

    cells = (size_x, size_y, LANES)
    packet = (2 * HALO + 2, size_y, LANES)
    first, second, part, count, edge = call(
        cells_kernel,
        [(packet, BF16), (packet, BF16), (cells, BF16), (cells, BF16), ((2, size_y, LANES), BF16)],
        [],
        place,
        face_counts,
        point_counts,
    )
    first, second = exchange(first, second, "gx")
    packet = (wide + wide // size_y, size_y, LANES)
    strip = (wide, size_y, LANES)
    first, second, part_x, count_x, edge_x = call(
        wide_kernel,
        [(packet, BF16), (packet, BF16), (strip, BF16), (strip, BF16), ((wide, LANES), F32)],
        [],
        place,
        first,
        second,
        part,
        count,
        edge,
    )
    first, second = exchange(first, second, ("gy_chip", "gy_core"))
    own = sizes.own_x
    iterate, field, scaled, packet = call(
        start_kernel,
        [((flat, LANES), F32)] * 3 + [((copies, own + own // 2, 2 * sizes.own_y, LANES), BF16)],
        [((flat, LANES), F32), (packet, BF16), (packet, BF16)],
        place,
        first,
        second,
        part_x,
        count_x,
        edge_x,
        mats[0],
    )
    level = (sizes.flat, LANES)
    near = (16 + (own + 8) * (sizes.own_y + 16), LANES)
    scratch = [
        (level, F32),
        (level, F32),
        (level, F32),
        ((sizes.planes * sizes.rows, LANES), F32),
        (near, F32),
        (near, F32),
        ((flat, LANES), F32),
    ]
    level_two = (sizes.planes // 4, sizes.rows // 2, LANES)
    level_three = (sizes.planes // 16, sizes.rows // 4, LANES)
    iterate, packet, inverse, diag, screen_two, screen_three = call(
        lambda *refs: middle_kernel(sizes, *refs),
        [
            ((flat, LANES), F32),
            ((copies, own, 2 * sizes.own_y, LANES), BF16),
            (level, F32),
            (level, F32),
            (level_two, F32),
            (level_three, F32),
        ],
        scratch + [((size_x * size_y, LANES), F32)],
        place,
        gather(packet),
        iterate,
        field,
        scaled,
        count_x,
        *mats,
    )
    solution_own, residual_own = call(
        lambda *refs: last_kernel(sizes, *refs),
        [(cells, F32), (cells, F32)],
        scratch + [((flat, LANES), F32)],
        place,
        gather(packet),
        iterate,
        field,
        scaled,
        count_x,
        inverse,
        diag,
        screen_two,
        screen_three,
        *mats,
    )
    return solution_own, residual_own


def solution(mesh):
    mesh_x, mesh_y = mesh.shape["gx"], mesh.shape["gy"]
    split = Mesh(mesh.devices.reshape(mesh_x, mesh_y // 2, 2), ("gx", "gy_chip", "gy_core"))
    rows = ("gy_chip", "gy_core")

    def run(point_counts, face_counts):
        return jax.shard_map(
            per_device,
            mesh=split,
            in_specs=(P("gx", rows, None), P(None, "gx", rows, None)),
            out_specs=(P("gx", rows, None), P("gx", rows, None)),
            check_vma=False,
        )(point_counts, face_counts)

    return run
```

```python
import numpy as np
import jax
import jax.numpy as jnp
from jax import lax
from jax.experimental import pallas as pl
from jax.experimental.pallas import tpu as pltpu
from jax.sharding import Mesh, PartitionSpec as P

F32 = jnp.float32
BF16 = jnp.bfloat16
LANES = 128
HALO = 8
COARSE_ITERS = 6

screen_weight = 0.25
flux_scale = 0.125
low_edge = 0.3
high_edge = 2.0
centre = 0.5 * (high_edge + low_edge)
radius = 0.5 * (high_edge - low_edge)
ratio = centre / radius
mom_first = 1.0 / ratio
mom_second = 1.0 / (2.0 * ratio - mom_first)
keep = mom_second * mom_first
gain = 2.0 * mom_second / radius

VMEM = pl.BlockSpec(memory_space=pltpu.VMEM)
SMEM = pl.BlockSpec(memory_space=pltpu.SMEM)
FAR = pl.BlockSpec(memory_space=pltpu.HBM)


def transfer_matrix(level):
    pack, size_z = 1 << level, LANES >> level
    planes = 2 if level == 0 else 4
    out = np.zeros((planes * LANES, LANES), np.float32)
    for j in range(planes):
        for q in range(pack):
            coarse = j if level == 0 else (j * pack + q) // 2
            for z in range(size_z):
                out[j * LANES + q * size_z + z, coarse * (size_z // 2) + z // 2] = 1.0
    return jnp.asarray(out, BF16)


def two_parts(value):
    high = value.astype(BF16)
    return jnp.concatenate([high, (value - high.astype(F32)).astype(BF16)], 0)


def gather_lanes(value, matrix):
    both = jnp.dot(two_parts(value), matrix, preferred_element_type=F32)
    return both[: value.shape[0]] + both[value.shape[0] :]


def spread_lanes(value, matrix):
    dims = (((1,), (1,)), ((), ()))
    both = lax.dot_general(two_parts(value), matrix, dims, preferred_element_type=F32)
    return both[: value.shape[0]] + both[value.shape[0] :]


def lane_index():
    return lax.broadcasted_iota(jnp.int32, (1, LANES), 1)


def z_sum(value, size_z):
    lane = lane_index() & (size_z - 1)
    inner_low = (lane != 0).astype(F32)
    inner_high = (lane != size_z - 1).astype(F32)
    return pltpu.roll(value, 1, 1) * inner_low + pltpu.roll(value, LANES - 1, 1) * inner_high


def x_sum(before, here, after, size_z):
    if size_z == LANES:
        return before + after
    lane = lax.broadcasted_iota(jnp.int32, here.shape, 1)
    if 2 * size_z == LANES:
        return pltpu.roll(here + jnp.where(lane < size_z, after, before), size_z, 1)
    up = pltpu.roll(jnp.where(lane < size_z, after, here), LANES - size_z, 1)
    down = pltpu.roll(jnp.where(lane >= LANES - size_z, before, here), size_z, 1)
    return up + down


def neighbours(ref, base, rows, stride, size_z):
    here = ref[pl.ds(base, rows), :]
    total = x_sum(ref[pl.ds(base - stride, rows), :], here, ref[pl.ds(base + stride, rows), :], size_z)
    total = total + (ref[pl.ds(base - 1, rows), :] + ref[pl.ds(base + 1, rows), :])
    return here, total + z_sum(here, size_z)


def for_planes(count, body, limit=64):
    if count <= limit:
        for i in range(count):
            body(i)
    else:
        step = 8

        def block(k, carry):
            for j in range(step):
                body(k * step + j)
            return carry

        lax.fori_loop(0, count // step, block, 0)


def pair_rows(ref, start, rows):
    return ref[pl.ds(start, rows // 2, stride=2), :] + ref[pl.ds(start + 1, rows // 2, stride=2), :]


def cells_kernel(place, faces, points, first, second, part, count, edge):
    size_x, size_y = points.shape[:2]
    lane = lax.broadcasted_iota(jnp.int32, (size_y, LANES), 1)
    row = lax.broadcasted_iota(jnp.int32, (size_y, LANES), 0)
    last_x = None
    for i in range(size_x):
        along_x = faces[0, i]
        along_y = faces[1, i]
        along_z = faces[2, i]
        total = jnp.where(row != 0, pltpu.roll(along_y, 1, 0), 0) - along_y
        total = total + (jnp.where(lane != 0, pltpu.roll(along_z, 1, 1), 0) - along_z) - along_x
        if last_x is not None:
            total = total + last_x
        last_x = along_x
        part[i] = total.astype(F32).astype(BF16)
        count[i] = (points[i] + 1).astype(F32).astype(BF16)
    edge[0] = last_x.astype(F32).astype(BF16)
    edge[1] = faces[1, :, size_y - 1, :].astype(F32).astype(BF16)

    def write(up, down):
        for target, start in ((up, size_x - HALO), (down, 0)):
            target[0:HALO] = part[start : start + HALO]
            target[HALO : 2 * HALO] = count[start : start + HALO]
            target[2 * HALO : 2 * HALO + 2] = edge[...]

    odd = place[0] % 2

    @pl.when(odd == 0)
    def _():
        write(first, second)

    @pl.when(odd == 1)
    def _():
        write(second, first)


def wide_kernel(place, got_first, got_second, part, count, edge, first, second, part_x, count_x, edge_x):
    size_x, size_y = part.shape[:2]
    wide = size_x + 2 * HALO

    def fill(below, above):
        part_x[0:HALO] = below[0:HALO]
        part_x[HALO + size_x :] = above[0:HALO]
        count_x[0:HALO] = below[HALO : 2 * HALO]
        count_x[HALO + size_x :] = above[HALO : 2 * HALO]
        part_x[HALO : HALO + size_x] = part[...]
        count_x[HALO : HALO + size_x] = count[...]
        part_x[HALO] = (part[0].astype(F32) + below[2 * HALO].astype(F32)).astype(BF16)
        part_x[HALO + size_x] = (above[0].astype(F32) + edge[0].astype(F32)).astype(BF16)
        edge_x[0:HALO] = below[2 * HALO + 1].astype(F32)[size_x - HALO :]
        edge_x[HALO : HALO + size_x] = edge[1].astype(F32)
        edge_x[HALO + size_x :] = above[2 * HALO + 1].astype(F32)[:HALO]

    odd = place[0] % 2

    @pl.when(odd == 0)
    def _():
        fill(got_second, got_first)

    @pl.when(odd == 1)
    def _():
        fill(got_first, got_second)

    def write(up, down):
        for i in range(wide):
            cells = part_x[i].astype(F32)
            points = count_x[i].astype(F32)
            up[i] = jnp.concatenate([cells[size_y - HALO :], points[size_y - HALO :]], 0).astype(BF16)
            down[i] = jnp.concatenate([cells[:HALO], points[:HALO]], 0).astype(BF16)
        for target in (up, down):
            for j in range(wide // size_y):
                target[wide + j] = edge_x[j * size_y : (j + 1) * size_y].astype(BF16)

    odd_y = place[1] % 2

    @pl.when(odd_y == 0)
    def _():
        write(first, second)

    @pl.when(odd_y == 1)
    def _():
        write(second, first)


def finest_step_one(source, target, field, scaled, start, end, plane):
    for i in range(start, end, 2):
        base = 8 + i * plane
        rows = 2 * plane
        here, total = neighbours(source, base, rows, plane, LANES)
        fit = (field[pl.ds(base, rows), :] + total) * scaled[pl.ds(base, rows), :]
        target[pl.ds(base, rows), :] = here + (fit - here) * (1.0 / centre)


def finest_step_two(source, old, field, scaled, start, end, plane):
    for i in range(start, end, 2):
        base = 8 + i * plane
        rows = 2 * plane
        here, total = neighbours(source, base, rows, plane, LANES)
        fit = (field[pl.ds(base, rows), :] + total) * scaled[pl.ds(base, rows), :]
        before = old[pl.ds(base, rows), :]
        old[pl.ds(base, rows), :] = here + (keep * (here - before) + gain * (fit - here))


def finest_residual(iterate, field, count, size_x, size_y, write):
    plane = size_y + 2 * HALO
    for i in range(size_x):
        base = 8 + (HALO + i) * plane + HALO
        here, total = neighbours(iterate, base, size_y, plane, LANES)
        diag = 6.0 + screen_weight * (count[HALO + i].astype(F32) - 1.0)
        write(i, here, field[pl.ds(base, size_y), :] + total - diag * here)


def restrict_finest(rows_ref, size_x, size_y, matrix):
    half = pair_rows(rows_ref, 0, size_x * size_y).reshape(size_x // 4, 4, size_y // 2, LANES)
    even = (half[:, 0] + half[:, 1]).reshape(-1, LANES)
    odd = (half[:, 2] + half[:, 3]).reshape(-1, LANES)
    return even, odd


def start_kernel(
    place, got_first, got_second, part_x, count_x, edge_x, matrix, iterate, field, inverse, packet, rows_ref, low, high
):
    wide, size_y = part_x.shape[:2]
    size_x = wide - 2 * HALO
    plane = size_y + 2 * HALO
    odd_y = place[1] % 2

    @pl.when(odd_y == 0)
    def _():
        low[...] = got_second[...]
        high[...] = got_first[...]

    @pl.when(odd_y == 1)
    def _():
        low[...] = got_first[...]
        high[...] = got_second[...]

    top = lax.broadcasted_iota(jnp.int32, (HALO, LANES), 0) == 0
    zero = jnp.zeros((8, LANES), F32)
    for ref in (iterate, field, inverse):
        ref[0:8] = zero
        ref[8 + wide * plane :] = zero
    low_edge_rows = [low[wide + j].astype(F32) for j in range(wide // size_y)]
    for i in range(wide):
        below = low[i].astype(F32)
        above = high[i].astype(F32)
        own = part_x[i].astype(F32)
        under = low_edge_rows[i // size_y][i % size_y : i % size_y + 1]
        over = edge_x[i : i + 1]
        cells = jnp.concatenate(
            [
                below[:HALO],
                own[:HALO] + jnp.where(top, under, 0.0),
                own[HALO:],
                above[:HALO] + jnp.where(top, over, 0.0),
            ],
            0,
        )
        points = jnp.concatenate([below[HALO:], count_x[i].astype(F32), above[HALO:]], 0)
        given = flux_scale * cells
        inv = jnp.where(points > 0.0, 1.0 / (6.0 - screen_weight + screen_weight * points), 0.0)
        base = 8 + i * plane
        field[pl.ds(base, plane), :] = given
        inverse[pl.ds(base, plane), :] = inv
        iterate[pl.ds(base, plane), :] = (given * inv) * (1.0 / centre)

    scratch = rows_ref
    for i in range(1, wide - 1, 2):
        base = 8 + i * plane
        rows = 2 * plane
        here, total = neighbours(iterate, base, rows, plane, LANES)
        fit = (field[pl.ds(base, rows), :] + total) * inverse[pl.ds(base, rows), :]
        scratch[pl.ds(base, rows), :] = here + (keep * here + gain * (fit - here))
    for i in range(1, wide - 1, 2):
        base = 8 + i * plane
        iterate[pl.ds(base, 2 * plane), :] = scratch[pl.ds(base, 2 * plane), :]

    def write(i, here, value):
        scratch[pl.ds(i * size_y, size_y), :] = value

    finest_residual(iterate, field, count_x, size_x, size_y, write)
    even, odd = restrict_finest(scratch, size_x, size_y, matrix)
    coarse = 0.125 * gather_lanes(jnp.concatenate([even, odd], 1), matrix[...])
    for i in range(size_x):
        scratch[pl.ds(i * size_y, size_y), :] = count_x[HALO + i].astype(F32) - 1.0
    even, odd = restrict_finest(scratch, size_x, size_y, matrix)
    points = jnp.dot(jnp.concatenate([even, odd], 1).astype(BF16), matrix[...], preferred_element_type=F32)
    send_coarse(packet, coarse, points, size_y // 2)


def send_coarse(packet, coarse, points, size_y):
    copies = packet.shape[0]
    planes = coarse.shape[0] // size_y
    high = coarse.astype(BF16).astype(F32)
    low = coarse - high
    for i in range(planes):
        at = slice(i * size_y, (i + 1) * size_y)
        tile = jnp.concatenate([high[at], low[at]], 0).astype(BF16)
        for k in range(copies):
            packet[k, i] = tile
    if points is not None:
        for i in range(planes // 2):
            tile = points[2 * i * size_y : 2 * (i + 1) * size_y].astype(BF16)
            for k in range(copies):
                packet[k, planes + i] = tile


def packed_apply(value, screen, factor, size_z):
    planes, size_y, _ = value.shape
    flat = value.reshape(planes * size_y, LANES)
    empty = jnp.zeros((1, size_y, LANES), F32)
    if planes > 1:
        before = jnp.concatenate([empty, value[:-1]], 0).reshape(flat.shape)
        after = jnp.concatenate([value[1:], empty], 0).reshape(flat.shape)
    else:
        before = after = jnp.zeros_like(flat)
    row = lax.broadcasted_iota(jnp.int32, value.shape, 1)
    along_y = jnp.where(row != 0, pltpu.roll(value, 1, 1), 0.0) + jnp.where(
        row != size_y - 1, pltpu.roll(value, size_y - 1, 1), 0.0
    )
    total = x_sum(before, flat, after, size_z) + z_sum(flat, size_z)
    return (6.0 * value - (total.reshape(value.shape) + along_y)) * factor + screen * value


def totals_of(*values):
    rows = jnp.concatenate([jnp.sum(value, 0) for value in values], 0)
    sums = jnp.sum(rows, 1, keepdims=True).reshape(len(values), -1, 1)
    sums = jnp.sum(sums, 1, keepdims=True)
    return [sums[i : i + 1] for i in range(len(values))]


def conjugate_gradients(target, screen, factor, size_z):
    iterate = jnp.zeros_like(target)
    remain = target
    search = target
    for step in range(COARSE_ITERS):
        image = packed_apply(search, screen, factor, size_z)
        if step + 1 == COARSE_ITERS:
            norm_now, bent = totals_of(remain * remain, search * image)
            return iterate + (norm_now / bent) * search
        norm_now, bent, mixed, norm_image = totals_of(
            remain * remain, search * image, remain * image, image * image
        )
        length = norm_now / bent
        iterate = iterate + length * search
        remain = remain - length * image
        norm_next = norm_now - 2.0 * length * mixed + length * length * norm_image
        search = remain + (norm_next / norm_now) * search


def smooth_packed(iterate, target, screen, inv, factor, size_z):
    step = (target - packed_apply(iterate, screen, factor, size_z)) * inv * (1.0 / centre)
    iterate = iterate + step
    again = (target - packed_apply(iterate, screen, factor, size_z)) * inv
    return iterate + (keep * step + gain * again)


def smooth_packed_zero(target, screen, inv, factor, size_z):
    step = target * inv * (1.0 / centre)
    again = (target - packed_apply(step, screen, factor, size_z)) * inv
    return step + (keep * step + gain * again)


def add_lanes(rows_ref, planes, size_y, matrix):
    half = pair_rows(rows_ref, 0, planes * size_y).reshape(planes // 4, 4, size_y // 2, LANES)
    wide = jnp.concatenate([half[:, j].reshape(-1, LANES) for j in range(4)], 1)
    return gather_lanes(wide, matrix[...]).reshape(planes // 4, size_y // 2, LANES)


def copy_level(value, matrix):
    planes, size_y, _ = value.shape
    wide = spread_lanes(value.reshape(-1, LANES), matrix[...]).reshape(planes, size_y, 4 * LANES)
    return jnp.stack([wide[:, :, j * LANES : (j + 1) * LANES] for j in range(4)], 1).reshape(
        4 * planes, size_y, LANES
    )


class Sizes:
    def __init__(self, mesh_x, mesh_y, size_x, size_y):
        self.mesh_x, self.mesh_y = mesh_x, mesh_y
        self.own_x, self.own_y = size_x // 4, size_y // 2
        self.planes, self.rows = mesh_x * self.own_x, mesh_y * self.own_y
        self.stride = self.rows + 8
        self.flat = (self.planes + 8) * self.stride + 8
        self.pad_x = 4


def level_one(place, gathered, sizes, mats, refs, first):
    mat_1, mat_2 = mats
    given, inverse, diag, step, iterate, rows_ref, level_two, local_a, local_b = refs
    size_z = LANES // 2
    factor = 0.25
    planes, rows, stride, pad = sizes.planes, sizes.rows, sizes.stride, sizes.pad_x
    own_x, own_y = sizes.own_x, sizes.own_y

    def clear(ref):
        ref[0 : pad * stride + 8] = jnp.zeros((pad * stride + 8, LANES), F32)
        ref[(pad + planes) * stride :] = jnp.zeros((pad * stride + 8, LANES), F32)

        def gap(i):
            ref[pl.ds((pad + i) * stride, 8), :] = jnp.zeros((8, LANES), F32)

        for_planes(planes, gap)

    for ref in (given, step, iterate) + ((inverse, diag) if first else ()):
        clear(ref)

    def block(b):
        gx = b // sizes.mesh_y
        gy = b % sizes.mesh_y
        source = gathered.at[gy % 2, gx * (sizes.mesh_y // 2) + gy // 2]
        for i in range(own_x):
            at = pl.ds((pad + gx * own_x + i) * stride + 8 + gy * own_y, own_y)
            tile = source[i].astype(F32)
            value = tile[:own_y] + tile[own_y:]
            if first:
                points = source[own_x + i // 2].astype(F32)[(i % 2) * own_y : (i % 2 + 1) * own_y]
                d = 6.0 * factor + (screen_weight * 0.125) * points
                diag[at, :] = d
                inv = 1.0 / d
                inverse[at, :] = inv
            else:
                inv = inverse[at, :]
            given[at, :] = value
            step[at, :] = value * inv * (1.0 / centre)

    for_planes(sizes.mesh_x * sizes.mesh_y, block)

    def second(i):
        base = (pad + i) * stride + 8
        at = pl.ds(base, rows)
        here, total = neighbours(step, base, rows, stride, size_z)
        fit = (given[at, :] + factor * total) * inverse[at, :]
        iterate[at, :] = here + (keep * here + gain * (fit - here))

    for_planes(planes, second)

    def residual(i):
        base = (pad + i) * stride + 8
        at = pl.ds(base, rows)
        here, total = neighbours(iterate, base, rows, stride, size_z)
        rows_ref[pl.ds(i * rows, rows), :] = given[at, :] + factor * total - diag[at, :] * here

    for_planes(planes, residual)
    target = 0.125 * add_lanes(rows_ref, planes, rows, mat_1)

    screen_two, screen_three = level_two
    if first:

        def screens(i):
            at = pl.ds((pad + i) * stride + 8, rows)
            rows_ref[pl.ds(i * rows, rows), :] = diag[at, :] - 6.0 * factor

        for_planes(planes, screens)
        screen_two[...] = 0.125 * add_lanes(rows_ref, planes, rows, mat_1)
    planes_2, rows_2 = planes // 4, rows // 2
    screen = screen_two[...]
    inv = 1.0 / (6.0 * factor**2 + screen)
    if first:
        rows_ref[0 : planes_2 * rows_2] = screen.reshape(-1, LANES)
        screen_three[...] = 0.125 * add_lanes(rows_ref, planes_2, rows_2, mat_2)
    value = smooth_packed_zero(target, screen, inv, factor**2, LANES // 4)
    remain = target - packed_apply(value, screen, factor**2, LANES // 4)
    rows_ref[0 : planes_2 * rows_2] = remain.reshape(-1, LANES)
    target_3 = 0.125 * add_lanes(rows_ref, planes_2, rows_2, mat_2)
    error = conjugate_gradients(target_3, screen_three[...], factor**3, LANES // 8)
    error = copy_level(error, mat_2).reshape(-1, LANES)
    count = planes_2 * rows_2
    rows_ref[pl.ds(0, count // 2, stride=2), :] = error
    rows_ref[pl.ds(1, count // 2, stride=2), :] = error
    value = value + rows_ref[0:count].reshape(value.shape)
    value = smooth_packed(value, target, screen, inv, factor**2, LANES // 4)

    rows_ref[0:rows_2] = jnp.zeros((rows_2, LANES), F32)
    rows_ref[(planes_2 + 1) * rows_2 : (planes_2 + 2) * rows_2] = jnp.zeros((rows_2, LANES), F32)
    rows_ref[rows_2 : (planes_2 + 1) * rows_2] = value.reshape(-1, LANES)
    near_2 = own_x // 4 + 2
    start = pl.multiple_of(place[0] * (own_x // 4) * rows_2, 8)
    near = rows_ref[pl.ds(start, near_2 * rows_2), :].reshape(near_2, rows_2, LANES)
    error = copy_level(near, mat_1)
    near_x, near_y = 4 * near_2, own_y + 16
    first_plane = place[0] * own_x
    for i in range(near_x):
        base = (first_plane + i) * stride + 8
        even, odd = pl.ds(base, rows_2, stride=2), pl.ds(base + 1, rows_2, stride=2)
        iterate[even, :] = iterate[even, :] + error[i]
        iterate[odd, :] = iterate[odd, :] + error[i]
    for i in range(near_x):
        at = pl.ds(pl.multiple_of((first_plane + i) * stride + place[1] * own_y, 8), near_y)
        local_a[pl.ds(8 + i * near_y, near_y), :] = iterate[at, :]
    for ref in (local_a, local_b):
        ref[0:8] = jnp.zeros((8, LANES), F32)
        ref[8 + near_x * near_y :] = jnp.zeros((8, LANES), F32)
    ends = pl.ds(8, near_y), pl.ds(8 + (near_x - 1) * near_y, near_y)
    for at in ends:
        local_b[at, :] = jnp.zeros((near_y, LANES), F32)

    def fit_of(ref, i):
        at = pl.ds(pl.multiple_of((first_plane + i) * stride + place[1] * own_y, 8), near_y)
        here, total = neighbours(ref, 8 + i * near_y, near_y, near_y, size_z)
        return here, (given[at, :] + factor * total) * inverse[at, :]

    for i in range(1, near_x - 1):
        here, fit = fit_of(local_a, i)
        local_b[pl.ds(8 + i * near_y, near_y), :] = here + (fit - here) * (1.0 / centre)
    for i in range(2, near_x - 2):
        here, fit = fit_of(local_b, i)
        at = pl.ds(8 + i * near_y, near_y)
        local_a[at, :] = here + (keep * (here - local_a[at, :]) + gain * (fit - here))


def add_correction(start, iterate, local, sizes, mat_0, plane):
    ends = pl.ds(0, 8), pl.ds(start.shape[0] - 8, 8)
    for at in ends:
        iterate[at, :] = start[at, :]
    near_y = sizes.own_y + 16
    half_y = plane // 2
    planes = sizes.own_x + 4
    value = jnp.concatenate(
        [local[pl.ds(8 + (2 + i) * near_y + 4, half_y), :] for i in range(planes)], 0
    )
    wide = spread_lanes(value, mat_0[...])
    for i in range(planes):
        for j in range(4):
            error = wide[i * half_y : (i + 1) * half_y, (j // 2) * LANES : (j // 2 + 1) * LANES]
            for side in (0, 1):
                at = pl.ds(8 + (4 * i + j) * plane + side, half_y, stride=2)
                iterate[at, :] = start[at, :] + error


def middle_kernel(sizes, place, gathered, start, field, scaled, count_x, mat_0, mat_1, mat_2, *rest):
    iterate, packet, inverse, diag, screen_two, screen_three = rest[:6]
    given, step, coarse, rows_ref, local_a, local_b, other, fine_rows = rest[6:]
    wide, size_y = count_x.shape[:2]
    size_x = wide - 2 * HALO
    plane = size_y + 2 * HALO
    refs = (given, inverse, diag, step, coarse, rows_ref, (screen_two, screen_three), local_a, local_b)
    level_one(place, gathered, sizes, (mat_1, mat_2), refs, True)
    add_correction(start, iterate, local_a, sizes, mat_0, plane)
    finest_step_one(iterate, other, field, scaled, 2, wide - 2, plane)
    finest_step_two(other, iterate, field, scaled, 3, wide - 3, plane)
    finest_step_one(iterate, other, field, scaled, 4, wide - 4, plane)
    finest_step_two(other, iterate, field, scaled, 5, wide - 5, plane)

    def write(i, here, value):
        fine_rows[pl.ds(i * size_y, size_y), :] = value

    finest_residual(iterate, field, count_x, size_x, size_y, write)
    even, odd = restrict_finest(fine_rows, size_x, size_y, mat_0)
    send_coarse(packet, 0.125 * gather_lanes(jnp.concatenate([even, odd], 1), mat_0[...]), None, size_y // 2)


def last_kernel(sizes, place, gathered, start, field, scaled, count_x, inverse, diag, screen_two, screen_three, *rest):
    mat_0, mat_1, mat_2, solution_far, residual_far = rest[:5]
    given, step, coarse, rows_ref, local_a, local_b, iterate, other, solution_out, residual_out, left = rest[5:]
    wide, size_y = count_x.shape[:2]
    size_x = wide - 2 * HALO
    plane = size_y + 2 * HALO
    refs = (given, inverse, diag, step, coarse, rows_ref, (screen_two, screen_three), local_a, local_b)
    level_one(place, gathered, sizes, (mat_1, mat_2), refs, False)
    add_correction(start, iterate, local_a, sizes, mat_0, plane)
    finest_step_one(iterate, other, field, scaled, HALO - 2, wide - HALO + 2, plane)
    finest_step_two(other, iterate, field, scaled, HALO - 1, wide - HALO + 1, plane)

    def send(source, target, which):
        copy = pltpu.make_async_copy(source, target, left.at[which])
        copy.start()
        return copy

    for i in range(size_x):
        solution_out[i] = iterate[pl.ds(8 + (HALO + i) * plane + HALO, size_y), :]
    copies = [send(solution_out, solution_far, 0)]

    def write(i, here, value):
        residual_out[i] = value
        if (2 * i + 2) % size_x == 0:
            half = pl.ds(i + 1 - size_x // 2, size_x // 2)
            copies.append(send(residual_out.at[half], residual_far.at[half], 1 + (i + 1) * 2 // size_x))

    finest_residual(iterate, field, count_x, size_x, size_y, write)
    for copy in copies:
        copy.wait()


def exchange(first, second, axis):
    count = lax.axis_size(axis)

    def pairs(start):
        found = []
        for i in range(start, count - 1, 2):
            found += [(i, i + 1), (i + 1, i)]
        return found

    return lax.ppermute(first, axis, pairs(0)), lax.ppermute(second, axis, pairs(1))


def gather(packet):
    spread = lax.all_to_all(packet, ("gx", "gy_chip"), 0, 0, tiled=True)
    return lax.all_gather(spread, "gy_core", axis=0)


def per_device(point_counts, face_counts):
    size_x, size_y, size_z = point_counts.shape
    assert size_z == LANES and size_x == 16 and size_y == 16
    mesh_x = lax.axis_size("gx")
    mesh_y = lax.axis_size("gy_chip") * lax.axis_size("gy_core")
    gx = lax.axis_index("gx")
    gy = lax.axis_index("gy_chip") * 2 + lax.axis_index("gy_core")
    place = jnp.stack([gx, gy]).astype(jnp.int32)
    wide, plane = size_x + 2 * HALO, size_y + 2 * HALO
    flat = 16 + wide * plane
    sizes = Sizes(mesh_x, mesh_y, size_x, size_y)
    copies = mesh_x * mesh_y // 2
    mats = [transfer_matrix(level) for level in range(3)]
    params = pltpu.CompilerParams(vmem_limit_bytes=(24 if sizes.flat < 4096 else 56) * 2**20)

    def call(kernel, outs, scratch, *args, copies=0, far_out=False):
        return pl.pallas_call(
            kernel,
            out_shape=[jax.ShapeDtypeStruct(shape, dtype) for shape, dtype in outs],
            in_specs=[SMEM] + [VMEM] * (len(args) - 1),
            out_specs=[FAR if far_out else VMEM] * len(outs),
            scratch_shapes=[pltpu.VMEM(shape, dtype) for shape, dtype in scratch]
            + ([pltpu.SemaphoreType.DMA((copies,))] if copies else []),
            compiler_params=params,
        )(*args)

    cells = (size_x, size_y, LANES)
    packet = (2 * HALO + 2, size_y, LANES)
    first, second, part, count, edge = call(
        cells_kernel,
        [(packet, BF16), (packet, BF16), (cells, BF16), (cells, BF16), ((2, size_y, LANES), BF16)],
        [],
        place,
        face_counts,
        point_counts,
    )
    first, second = exchange(first, second, "gx")
    packet = (wide + wide // size_y, size_y, LANES)
    strip = (wide, size_y, LANES)
    first, second, part_x, count_x, edge_x = call(
        wide_kernel,
        [(packet, BF16), (packet, BF16), (strip, BF16), (strip, BF16), ((wide, LANES), F32)],
        [],
        place,
        first,
        second,
        part,
        count,
        edge,
    )
    first, second = exchange(first, second, ("gy_chip", "gy_core"))
    own = sizes.own_x
    iterate, field, scaled, packet = call(
        start_kernel,
        [((flat, LANES), F32)] * 3 + [((copies, own + own // 2, 2 * sizes.own_y, LANES), BF16)],
        [((flat, LANES), F32), (packet, BF16), (packet, BF16)],
        place,
        first,
        second,
        part_x,
        count_x,
        edge_x,
        mats[0],
    )
    level = (sizes.flat, LANES)
    near = (16 + (own + 8) * (sizes.own_y + 16), LANES)
    scratch = [
        (level, F32),
        (level, F32),
        (level, F32),
        ((sizes.planes * sizes.rows, LANES), F32),
        (near, F32),
        (near, F32),
        ((flat, LANES), F32),
    ]
    level_two = (sizes.planes // 4, sizes.rows // 2, LANES)
    level_three = (sizes.planes // 16, sizes.rows // 4, LANES)
    iterate, packet, inverse, diag, screen_two, screen_three = call(
        lambda *refs: middle_kernel(sizes, *refs),
        [
            ((flat, LANES), F32),
            ((copies, own, 2 * sizes.own_y, LANES), BF16),
            (level, F32),
            (level, F32),
            (level_two, F32),
            (level_three, F32),
        ],
        scratch + [((size_x * size_y, LANES), F32)],
        place,
        gather(packet),
        iterate,
        field,
        scaled,
        count_x,
        *mats,
    )
    solution_own, residual_own = call(
        lambda *refs: last_kernel(sizes, *refs),
        [(cells, F32), (cells, F32)],
        scratch + [((flat, LANES), F32), (cells, F32), (cells, F32)],
        place,
        gather(packet),
        iterate,
        field,
        scaled,
        count_x,
        inverse,
        diag,
        screen_two,
        screen_three,
        *mats,
        copies=4,
        far_out=True,
    )
    return solution_own, residual_own


def solution(mesh):
    mesh_x, mesh_y = mesh.shape["gx"], mesh.shape["gy"]
    split = Mesh(mesh.devices.reshape(mesh_x, mesh_y // 2, 2), ("gx", "gy_chip", "gy_core"))
    rows = ("gy_chip", "gy_core")

    def run(point_counts, face_counts):
        return jax.shard_map(
            per_device,
            mesh=split,
            in_specs=(P("gx", rows, None), P(None, "gx", rows, None)),
            out_specs=(P("gx", rows, None), P("gx", rows, None)),
            check_vma=False,
        )(point_counts, face_counts)

    return run
```

```python
import numpy as np
import jax
import jax.numpy as jnp
from jax import lax
from jax.experimental import pallas as pl
from jax.experimental.pallas import tpu as pltpu
from jax.sharding import Mesh, PartitionSpec as P

F32 = jnp.float32
BF16 = jnp.bfloat16
LANES = 128
HALO = 8
COARSE_ITERS = 6

screen_weight = 0.25
flux_scale = 0.125
low_edge = 0.3
high_edge = 2.0
centre = 0.5 * (high_edge + low_edge)
radius = 0.5 * (high_edge - low_edge)
ratio = centre / radius
mom_first = 1.0 / ratio
mom_second = 1.0 / (2.0 * ratio - mom_first)
keep = mom_second * mom_first
gain = 2.0 * mom_second / radius

VMEM = pl.BlockSpec(memory_space=pltpu.VMEM)
SMEM = pl.BlockSpec(memory_space=pltpu.SMEM)
FAR = pl.BlockSpec(memory_space=pltpu.HBM)


def transfer_matrix(level):
    pack, size_z = 1 << level, LANES >> level
    planes = 2 if level == 0 else 4
    out = np.zeros((planes * LANES, LANES), np.float32)
    for j in range(planes):
        for q in range(pack):
            coarse = j if level == 0 else (j * pack + q) // 2
            for z in range(size_z):
                out[j * LANES + q * size_z + z, coarse * (size_z // 2) + z // 2] = 1.0
    return jnp.asarray(out, BF16)


def two_parts(value):
    high = value.astype(BF16)
    return jnp.concatenate([high, (value - high.astype(F32)).astype(BF16)], 0)


def gather_lanes(value, matrix):
    both = jnp.dot(two_parts(value), matrix, preferred_element_type=F32)
    return both[: value.shape[0]] + both[value.shape[0] :]


def spread_lanes(value, matrix):
    dims = (((1,), (1,)), ((), ()))
    both = lax.dot_general(two_parts(value), matrix, dims, preferred_element_type=F32)
    return both[: value.shape[0]] + both[value.shape[0] :]


def lane_index():
    return lax.broadcasted_iota(jnp.int32, (1, LANES), 1)


def z_sum(value, size_z):
    lane = lane_index() & (size_z - 1)
    inner_low = (lane != 0).astype(F32)
    inner_high = (lane != size_z - 1).astype(F32)
    return pltpu.roll(value, 1, 1) * inner_low + pltpu.roll(value, LANES - 1, 1) * inner_high


def x_sum(before, here, after, size_z):
    if size_z == LANES:
        return before + after
    lane = lax.broadcasted_iota(jnp.int32, here.shape, 1)
    if 2 * size_z == LANES:
        return pltpu.roll(here + jnp.where(lane < size_z, after, before), size_z, 1)
    up = pltpu.roll(jnp.where(lane < size_z, after, here), LANES - size_z, 1)
    down = pltpu.roll(jnp.where(lane >= LANES - size_z, before, here), size_z, 1)
    return up + down


def neighbours(ref, base, rows, stride, size_z):
    here = ref[pl.ds(base, rows), :]
    total = x_sum(ref[pl.ds(base - stride, rows), :], here, ref[pl.ds(base + stride, rows), :], size_z)
    total = total + (ref[pl.ds(base - 1, rows), :] + ref[pl.ds(base + 1, rows), :])
    return here, total + z_sum(here, size_z)


def for_planes(count, body, limit=64):
    if count <= limit:
        for i in range(count):
            body(i)
    else:
        step = 8

        def block(k, carry):
            for j in range(step):
                body(k * step + j)
            return carry

        lax.fori_loop(0, count // step, block, 0)


def pair_rows(ref, start, rows):
    return ref[pl.ds(start, rows // 2, stride=2), :] + ref[pl.ds(start + 1, rows // 2, stride=2), :]


def pack_cell(faces, points):
    word = points << 18
    for c in range(3):
        word = word + ((faces[c] + 32) << (6 * c))
    return word


def cells_kernel(place, words, first, second, part, count, edge):
    size_x, size_y = words.shape[:2]
    lane = lax.broadcasted_iota(jnp.int32, (size_y, LANES), 1)
    row = lax.broadcasted_iota(jnp.int32, (size_y, LANES), 0)
    last_x = None
    for i in range(size_x):
        word = words[i]
        along_x, along_y, along_z = [((word >> (6 * c)) & 63) - 32 for c in range(3)]
        total = jnp.where(row != 0, pltpu.roll(along_y, 1, 0), 0) - along_y
        total = total + (jnp.where(lane != 0, pltpu.roll(along_z, 1, 1), 0) - along_z) - along_x
        if last_x is not None:
            total = total + last_x
        last_x = along_x
        part[i] = total.astype(F32).astype(BF16)
        count[i] = ((word >> 18) + 1).astype(F32).astype(BF16)
    edge[0] = last_x.astype(F32).astype(BF16)
    edge[1] = (((words[:, size_y - 1, :] >> 6) & 63) - 32).astype(F32).astype(BF16)

    def write(up, down):
        for target, start in ((up, size_x - HALO), (down, 0)):
            target[0:HALO] = part[start : start + HALO]
            target[HALO : 2 * HALO] = count[start : start + HALO]
            target[2 * HALO : 2 * HALO + 2] = edge[...]

    odd = place[0] % 2

    @pl.when(odd == 0)
    def _():
        write(first, second)

    @pl.when(odd == 1)
    def _():
        write(second, first)


def wide_kernel(place, got_first, got_second, part, count, edge, first, second, part_x, count_x, edge_x):
    size_x, size_y = part.shape[:2]
    wide = size_x + 2 * HALO

    def fill(below, above):
        part_x[0:HALO] = below[0:HALO]
        part_x[HALO + size_x :] = above[0:HALO]
        count_x[0:HALO] = below[HALO : 2 * HALO]
        count_x[HALO + size_x :] = above[HALO : 2 * HALO]
        part_x[HALO : HALO + size_x] = part[...]
        count_x[HALO : HALO + size_x] = count[...]
        part_x[HALO] = (part[0].astype(F32) + below[2 * HALO].astype(F32)).astype(BF16)
        part_x[HALO + size_x] = (above[0].astype(F32) + edge[0].astype(F32)).astype(BF16)
        edge_x[0:HALO] = below[2 * HALO + 1].astype(F32)[size_x - HALO :]
        edge_x[HALO : HALO + size_x] = edge[1].astype(F32)
        edge_x[HALO + size_x :] = above[2 * HALO + 1].astype(F32)[:HALO]

    odd = place[0] % 2

    @pl.when(odd == 0)
    def _():
        fill(got_second, got_first)

    @pl.when(odd == 1)
    def _():
        fill(got_first, got_second)

    def write(up, down):
        for i in range(wide):
            cells = part_x[i].astype(F32)
            points = count_x[i].astype(F32)
            up[i] = jnp.concatenate([cells[size_y - HALO :], points[size_y - HALO :]], 0).astype(BF16)
            down[i] = jnp.concatenate([cells[:HALO], points[:HALO]], 0).astype(BF16)
        for target in (up, down):
            for j in range(wide // size_y):
                target[wide + j] = edge_x[j * size_y : (j + 1) * size_y].astype(BF16)

    odd_y = place[1] % 2

    @pl.when(odd_y == 0)
    def _():
        write(first, second)

    @pl.when(odd_y == 1)
    def _():
        write(second, first)


def finest_parts(margin, wide, plane):
    planes = range(HALO - margin, wide - HALO + margin)
    if margin > 4:
        return [(8 + i * plane, 2 * plane) for i in planes[::2]]
    return [(8 + i * plane + HALO - 4, plane - 2 * HALO + 8) for i in planes]


def finest_step_one(source, target, field, scaled, margin, wide, plane):
    for base, rows in finest_parts(margin, wide, plane):
        at = pl.ds(base, rows)
        here, total = neighbours(source, base, rows, plane, LANES)
        fit = (field[at, :] + total) * scaled[at, :]
        target[at, :] = here + (fit - here) * (1.0 / centre)


def finest_step_two(source, old, field, scaled, margin, wide, plane):
    for base, rows in finest_parts(margin, wide, plane):
        at = pl.ds(base, rows)
        here, total = neighbours(source, base, rows, plane, LANES)
        fit = (field[at, :] + total) * scaled[at, :]
        old[at, :] = here + (keep * (here - old[at, :]) + gain * (fit - here))


def finest_step_two_from_zero(source, target, field, scaled, margin, wide, plane):
    for base, rows in finest_parts(margin, wide, plane):
        at = pl.ds(base, rows)
        here, total = neighbours(source, base, rows, plane, LANES)
        fit = (field[at, :] + total) * scaled[at, :]
        target[at, :] = here + (keep * here + gain * (fit - here))


def finest_residual(iterate, field, count, size_x, size_y, write):
    plane = size_y + 2 * HALO
    for i in range(size_x):
        base = 8 + (HALO + i) * plane + HALO
        here, total = neighbours(iterate, base, size_y, plane, LANES)
        diag = 6.0 + screen_weight * (count[HALO + i].astype(F32) - 1.0)
        write(i, here, field[pl.ds(base, size_y), :] + total - diag * here)


def restrict_finest(rows_ref, size_x, size_y, matrix):
    half = pair_rows(rows_ref, 0, size_x * size_y).reshape(size_x // 4, 4, size_y // 2, LANES)
    even = (half[:, 0] + half[:, 1]).reshape(-1, LANES)
    odd = (half[:, 2] + half[:, 3]).reshape(-1, LANES)
    return even, odd


def first_step(place, got, part_x, count_x, edge_x, iterate, field, inverse, margin):
    wide, size_y = part_x.shape[:2]
    plane = size_y + 2 * HALO
    even = place[1] % 2 == 0
    top = lax.broadcasted_iota(jnp.int32, (HALO, LANES), 0) == 0
    under_rows = [jnp.where(even, got[1][wide + j], got[0][wide + j]).astype(F32) for j in range(wide // size_y)]
    for i in range(HALO - margin, wide - HALO + margin):
        below = jnp.where(even, got[1][i], got[0][i]).astype(F32)
        above = jnp.where(even, got[0][i], got[1][i]).astype(F32)
        own = part_x[i].astype(F32)
        under = under_rows[i // size_y][i % size_y : i % size_y + 1]
        over = edge_x[i : i + 1]
        cells = jnp.concatenate(
            [
                below[:HALO],
                own[:HALO] + jnp.where(top, under, 0.0),
                own[HALO:],
                above[:HALO] + jnp.where(top, over, 0.0),
            ],
            0,
        )
        points = jnp.concatenate([below[HALO:], count_x[i].astype(F32), above[HALO:]], 0)
        given = flux_scale * cells
        inv = jnp.where(points > 0.0, 1.0 / (6.0 - screen_weight + screen_weight * points), 0.0)
        at = pl.ds(8 + i * plane, plane)
        field[at, :] = given
        inverse[at, :] = inv
        iterate[at, :] = (given * inv) * (1.0 / centre)


def start_kernel(
    place, got_first, got_second, part_x, count_x, edge_x, matrix, packet, first, second, field, inverse, rows_ref
):
    wide, size_y = part_x.shape[:2]
    size_x = wide - 2 * HALO
    plane = size_y + 2 * HALO
    first_step(place, (got_first, got_second), part_x, count_x, edge_x, first, field, inverse, 2)
    finest_step_two_from_zero(first, second, field, inverse, 1, wide, plane)

    def write(i, here, value):
        rows_ref[pl.ds(i * size_y, size_y), :] = value

    finest_residual(second, field, count_x, size_x, size_y, write)
    even, odd = restrict_finest(rows_ref, size_x, size_y, matrix)
    coarse = 0.125 * gather_lanes(jnp.concatenate([even, odd], 1), matrix[...])
    for i in range(size_x):
        rows_ref[pl.ds(i * size_y, size_y), :] = count_x[HALO + i].astype(F32) - 1.0
    even, odd = restrict_finest(rows_ref, size_x, size_y, matrix)
    points = jnp.dot(jnp.concatenate([even, odd], 1).astype(BF16), matrix[...], preferred_element_type=F32)
    send_coarse(packet, coarse, points, size_y // 2)


def surroundings_kernel(
    place, after, got_first, got_second, part_x, count_x, edge_x, iterate, field, inverse, first
):
    wide, size_y = part_x.shape[:2]
    plane = size_y + 2 * HALO
    zero = jnp.zeros((8, LANES), F32)
    for ref in (iterate, field, inverse, first):
        ref[0:8] = zero
        ref[8 + wide * plane :] = zero
    first_step(place, (got_first, got_second), part_x, count_x, edge_x, first, field, inverse, HALO)
    for base, rows in ((8, plane), (8 + (wide - 1) * plane, plane)):
        iterate[pl.ds(base, rows), :] = first[pl.ds(base, rows), :]
    finest_step_two_from_zero(first, iterate, field, inverse, HALO - 1, wide, plane)


def send_coarse(packet, coarse, points, size_y):
    copies = packet.shape[0]
    planes = coarse.shape[0] // size_y
    high = coarse.astype(BF16).astype(F32)
    low = coarse - high
    for i in range(planes):
        at = slice(i * size_y, (i + 1) * size_y)
        tile = jnp.concatenate([high[at], low[at]], 0).astype(BF16)
        for k in range(copies):
            packet[k, i] = tile
    if points is not None:
        for i in range(planes // 2):
            tile = points[2 * i * size_y : 2 * (i + 1) * size_y].astype(BF16)
            for k in range(copies):
                packet[k, planes + i] = tile


def packed_apply(value, screen, factor, size_z):
    planes, size_y, _ = value.shape
    flat = value.reshape(planes * size_y, LANES)
    empty = jnp.zeros((1, size_y, LANES), F32)
    if planes > 1:
        before = jnp.concatenate([empty, value[:-1]], 0).reshape(flat.shape)
        after = jnp.concatenate([value[1:], empty], 0).reshape(flat.shape)
    else:
        before = after = jnp.zeros_like(flat)
    row = lax.broadcasted_iota(jnp.int32, value.shape, 1)
    along_y = jnp.where(row != 0, pltpu.roll(value, 1, 1), 0.0) + jnp.where(
        row != size_y - 1, pltpu.roll(value, size_y - 1, 1), 0.0
    )
    total = x_sum(before, flat, after, size_z) + z_sum(flat, size_z)
    return (6.0 * value - (total.reshape(value.shape) + along_y)) * factor + screen * value


def totals_of(*values):
    rows = jnp.concatenate([jnp.sum(value, 0) for value in values], 0)
    sums = jnp.sum(rows, 1, keepdims=True).reshape(len(values), -1, 1)
    sums = jnp.sum(sums, 1, keepdims=True)
    return [sums[i : i + 1] for i in range(len(values))]


def conjugate_gradients(target, screen, factor, size_z):
    iterate = jnp.zeros_like(target)
    remain = target
    search = target
    for step in range(COARSE_ITERS):
        image = packed_apply(search, screen, factor, size_z)
        if step + 1 == COARSE_ITERS:
            norm_now, bent = totals_of(remain * remain, search * image)
            return iterate + (norm_now / bent) * search
        norm_now, bent, mixed, norm_image = totals_of(
            remain * remain, search * image, remain * image, image * image
        )
        length = norm_now / bent
        iterate = iterate + length * search
        remain = remain - length * image
        norm_next = norm_now - 2.0 * length * mixed + length * length * norm_image
        search = remain + (norm_next / norm_now) * search


def smooth_packed(iterate, target, screen, inv, factor, size_z):
    step = (target - packed_apply(iterate, screen, factor, size_z)) * inv * (1.0 / centre)
    iterate = iterate + step
    again = (target - packed_apply(iterate, screen, factor, size_z)) * inv
    return iterate + (keep * step + gain * again)


def smooth_packed_zero(target, screen, inv, factor, size_z):
    step = target * inv * (1.0 / centre)
    again = (target - packed_apply(step, screen, factor, size_z)) * inv
    return step + (keep * step + gain * again)


def add_lanes(rows_ref, planes, size_y, matrix):
    half = pair_rows(rows_ref, 0, planes * size_y).reshape(planes // 4, 4, size_y // 2, LANES)
    wide = jnp.concatenate([half[:, j].reshape(-1, LANES) for j in range(4)], 1)
    return gather_lanes(wide, matrix[...]).reshape(planes // 4, size_y // 2, LANES)


def copy_level(value, matrix):
    planes, size_y, _ = value.shape
    wide = spread_lanes(value.reshape(-1, LANES), matrix[...]).reshape(planes, size_y, 4 * LANES)
    return jnp.stack([wide[:, :, j * LANES : (j + 1) * LANES] for j in range(4)], 1).reshape(
        4 * planes, size_y, LANES
    )


class Sizes:
    def __init__(self, mesh_x, mesh_y, size_x, size_y):
        self.mesh_x, self.mesh_y = mesh_x, mesh_y
        self.own_x, self.own_y = size_x // 4, size_y // 2
        self.planes, self.rows = mesh_x * self.own_x, mesh_y * self.own_y
        self.stride = self.rows + 8
        self.flat = (self.planes + 8) * self.stride + 8
        self.pad_x = 4


def level_one(place, gathered, sizes, mats, refs, first):
    mat_1, mat_2 = mats
    given, inverse, diag, step, iterate, rows_ref, level_two, local_a, local_b = refs
    size_z = LANES // 2
    factor = 0.25
    planes, rows, stride, pad = sizes.planes, sizes.rows, sizes.stride, sizes.pad_x
    own_x, own_y = sizes.own_x, sizes.own_y

    def clear(ref):
        ref[0 : pad * stride + 8] = jnp.zeros((pad * stride + 8, LANES), F32)
        ref[(pad + planes) * stride :] = jnp.zeros((pad * stride + 8, LANES), F32)

        def gap(i):
            ref[pl.ds((pad + i) * stride, 8), :] = jnp.zeros((8, LANES), F32)

        for_planes(planes, gap)

    for ref in (given, step, iterate) + ((inverse, diag) if first else ()):
        clear(ref)

    core = place[1] % 2
    per_core = sizes.mesh_x * sizes.mesh_y // 2

    def block(b):
        source, side = (gathered[0], core) if b < per_core else (gathered[1], 1 - core)
        gx = b % per_core // (sizes.mesh_y // 2)
        gy = 2 * (b % (sizes.mesh_y // 2)) + side
        source = source.at[b % per_core]
        for i in range(own_x):
            start = (pad + gx * own_x + i) * stride + 8 + gy * own_y
            at = pl.ds(pl.multiple_of(start, 8), own_y)
            tile = source[i].astype(F32)
            value = tile[:own_y] + tile[own_y:]
            if first:
                points = source[own_x + i // 2].astype(F32)[(i % 2) * own_y : (i % 2 + 1) * own_y]
                d = 6.0 * factor + (screen_weight * 0.125) * points
                diag[at, :] = d
                inv = 1.0 / d
                inverse[at, :] = inv
            else:
                inv = inverse[at, :]
            given[at, :] = value
            step[at, :] = value * inv * (1.0 / centre)

    for b in range(sizes.mesh_x * sizes.mesh_y):
        block(b)

    def second(i):
        base = (pad + i) * stride + 8
        at = pl.ds(base, rows)
        here, total = neighbours(step, base, rows, stride, size_z)
        fit = (given[at, :] + factor * total) * inverse[at, :]
        iterate[at, :] = here + (keep * here + gain * (fit - here))

    for_planes(planes, second)

    def residual(i):
        base = (pad + i) * stride + 8
        at = pl.ds(base, rows)
        here, total = neighbours(iterate, base, rows, stride, size_z)
        rows_ref[pl.ds(i * rows, rows), :] = given[at, :] + factor * total - diag[at, :] * here

    for_planes(planes, residual)
    target = 0.125 * add_lanes(rows_ref, planes, rows, mat_1)

    screen_two, screen_three = level_two
    if first:

        def screens(i):
            at = pl.ds((pad + i) * stride + 8, rows)
            rows_ref[pl.ds(i * rows, rows), :] = diag[at, :] - 6.0 * factor

        for_planes(planes, screens)
        screen_two[...] = 0.125 * add_lanes(rows_ref, planes, rows, mat_1)
    planes_2, rows_2 = planes // 4, rows // 2
    screen = screen_two[...]
    inv = 1.0 / (6.0 * factor**2 + screen)
    if first:
        rows_ref[0 : planes_2 * rows_2] = screen.reshape(-1, LANES)
        screen_three[...] = 0.125 * add_lanes(rows_ref, planes_2, rows_2, mat_2)
    value = smooth_packed_zero(target, screen, inv, factor**2, LANES // 4)
    remain = target - packed_apply(value, screen, factor**2, LANES // 4)
    rows_ref[0 : planes_2 * rows_2] = remain.reshape(-1, LANES)
    target_3 = 0.125 * add_lanes(rows_ref, planes_2, rows_2, mat_2)
    error = conjugate_gradients(target_3, screen_three[...], factor**3, LANES // 8)
    error = copy_level(error, mat_2).reshape(-1, LANES)
    count = planes_2 * rows_2
    rows_ref[pl.ds(0, count // 2, stride=2), :] = error
    rows_ref[pl.ds(1, count // 2, stride=2), :] = error
    value = value + rows_ref[0:count].reshape(value.shape)
    value = smooth_packed(value, target, screen, inv, factor**2, LANES // 4)

    rows_ref[0:rows_2] = jnp.zeros((rows_2, LANES), F32)
    rows_ref[(planes_2 + 1) * rows_2 : (planes_2 + 2) * rows_2] = jnp.zeros((rows_2, LANES), F32)
    rows_ref[rows_2 : (planes_2 + 1) * rows_2] = value.reshape(-1, LANES)
    near_2 = own_x // 4 + 2
    start = pl.multiple_of(place[0] * (own_x // 4) * rows_2, 8)
    near = rows_ref[pl.ds(start, near_2 * rows_2), :].reshape(near_2, rows_2, LANES)
    error = copy_level(near, mat_1)
    near_x, near_y = 4 * near_2, own_y + 16
    first_plane = place[0] * own_x
    for i in range(near_x):
        base = (first_plane + i) * stride + 8
        even, odd = pl.ds(base, rows_2, stride=2), pl.ds(base + 1, rows_2, stride=2)
        iterate[even, :] = iterate[even, :] + error[i]
        iterate[odd, :] = iterate[odd, :] + error[i]
    for i in range(near_x):
        at = pl.ds(pl.multiple_of((first_plane + i) * stride + place[1] * own_y, 8), near_y)
        local_a[pl.ds(8 + i * near_y, near_y), :] = iterate[at, :]
    for ref in (local_a, local_b):
        ref[0:8] = jnp.zeros((8, LANES), F32)
        ref[8 + near_x * near_y :] = jnp.zeros((8, LANES), F32)
    ends = pl.ds(8, near_y), pl.ds(8 + (near_x - 1) * near_y, near_y)
    for at in ends:
        local_b[at, :] = jnp.zeros((near_y, LANES), F32)

    def fit_of(ref, i):
        at = pl.ds(pl.multiple_of((first_plane + i) * stride + place[1] * own_y, 8), near_y)
        here, total = neighbours(ref, 8 + i * near_y, near_y, near_y, size_z)
        return here, (given[at, :] + factor * total) * inverse[at, :]

    for i in range(1, near_x - 1):
        here, fit = fit_of(local_a, i)
        local_b[pl.ds(8 + i * near_y, near_y), :] = here + (fit - here) * (1.0 / centre)
    for i in range(2, near_x - 2):
        here, fit = fit_of(local_b, i)
        at = pl.ds(8 + i * near_y, near_y)
        local_a[at, :] = here + (keep * (here - local_a[at, :]) + gain * (fit - here))


def add_correction(start, iterate, local, sizes, mat_0, plane):
    ends = pl.ds(0, 8), pl.ds(start.shape[0] - 8, 8)
    for at in ends:
        iterate[at, :] = start[at, :]
    near_y = sizes.own_y + 16
    half_y = plane // 2
    planes = sizes.own_x + 4
    value = jnp.concatenate(
        [local[pl.ds(8 + (2 + i) * near_y + 4, half_y), :] for i in range(planes)], 0
    )
    wide = spread_lanes(value, mat_0[...])
    for i in range(planes):
        for j in range(4):
            error = wide[i * half_y : (i + 1) * half_y, (j // 2) * LANES : (j // 2 + 1) * LANES]
            for side in (0, 1):
                at = pl.ds(8 + (4 * i + j) * plane + side, half_y, stride=2)
                iterate[at, :] = start[at, :] + error


def middle_kernel(sizes, place, near, far, start, field, scaled, count_x, mat_0, mat_1, mat_2, *rest):
    iterate, packet, inverse, diag, screen_two, screen_three = rest[:6]
    given, step, coarse, rows_ref, local_a, local_b, other, fine_rows = rest[6:]
    wide, size_y = count_x.shape[:2]
    size_x = wide - 2 * HALO
    plane = size_y + 2 * HALO
    refs = (given, inverse, diag, step, coarse, rows_ref, (screen_two, screen_three), local_a, local_b)
    level_one(place, (near, far), sizes, (mat_1, mat_2), refs, True)
    add_correction(start, iterate, local_a, sizes, mat_0, plane)
    finest_step_one(iterate, other, field, scaled, 6, wide, plane)
    finest_step_two(other, iterate, field, scaled, 5, wide, plane)
    finest_step_one(iterate, other, field, scaled, 4, wide, plane)
    finest_step_two(other, iterate, field, scaled, 3, wide, plane)

    def write(i, here, value):
        fine_rows[pl.ds(i * size_y, size_y), :] = value

    finest_residual(iterate, field, count_x, size_x, size_y, write)
    even, odd = restrict_finest(fine_rows, size_x, size_y, mat_0)
    send_coarse(packet, 0.125 * gather_lanes(jnp.concatenate([even, odd], 1), mat_0[...]), None, size_y // 2)


def last_kernel(sizes, place, near, far, start, field, scaled, count_x, inverse, diag, screen_two, screen_three, *rest):
    mat_0, mat_1, mat_2, solution_far, residual_far = rest[:5]
    given, step, coarse, rows_ref, local_a, local_b, iterate, other, solution_out, residual_out, left = rest[5:]
    wide, size_y = count_x.shape[:2]
    size_x = wide - 2 * HALO
    plane = size_y + 2 * HALO
    refs = (given, inverse, diag, step, coarse, rows_ref, (screen_two, screen_three), local_a, local_b)
    level_one(place, (near, far), sizes, (mat_1, mat_2), refs, False)
    add_correction(start, iterate, local_a, sizes, mat_0, plane)
    finest_step_one(iterate, other, field, scaled, 2, wide, plane)
    finest_step_two(other, iterate, field, scaled, 1, wide, plane)

    def send(source, target, which):
        copy = pltpu.make_async_copy(source, target, left.at[which])
        copy.start()
        return copy

    for i in range(size_x):
        solution_out[i] = iterate[pl.ds(8 + (HALO + i) * plane + HALO, size_y), :]
    copies = [send(solution_out, solution_far, 0)]

    def write(i, here, value):
        residual_out[i] = value
        if (2 * i + 2) % size_x == 0:
            half = pl.ds(i + 1 - size_x // 2, size_x // 2)
            copies.append(send(residual_out.at[half], residual_far.at[half], 1 + (i + 1) * 2 // size_x))

    finest_residual(iterate, field, count_x, size_x, size_y, write)
    for copy in copies:
        copy.wait()


def exchange(first, second, axis):
    count = lax.axis_size(axis)

    def pairs(start):
        found = []
        for i in range(start, count - 1, 2):
            found += [(i, i + 1), (i + 1, i)]
        return found

    return lax.ppermute(first, axis, pairs(0)), lax.ppermute(second, axis, pairs(1))


def gather(packet):
    near = lax.all_to_all(packet, ("gx", "gy_chip"), 0, 0, tiled=True)
    return near, lax.ppermute(near, "gy_core", [(0, 1), (1, 0)])


def per_device(point_counts, face_counts):
    size_x, size_y, size_z = point_counts.shape
    assert size_z == LANES and size_x == 16 and size_y == 16
    mesh_x = lax.axis_size("gx")
    mesh_y = lax.axis_size("gy_chip") * lax.axis_size("gy_core")
    gx = lax.axis_index("gx")
    gy = lax.axis_index("gy_chip") * 2 + lax.axis_index("gy_core")
    place = jnp.stack([gx, gy]).astype(jnp.int32)
    wide, plane = size_x + 2 * HALO, size_y + 2 * HALO
    flat = 16 + wide * plane
    sizes = Sizes(mesh_x, mesh_y, size_x, size_y)
    copies = mesh_x * mesh_y // 2
    mats = [transfer_matrix(level) for level in range(3)]
    params = pltpu.CompilerParams(vmem_limit_bytes=(24 if sizes.flat < 4096 else 56) * 2**20)

    def call(kernel, outs, scratch, *args, copies=0, far_out=False, cost=None):
        return pl.pallas_call(
            kernel,
            out_shape=[jax.ShapeDtypeStruct(shape, dtype) for shape, dtype in outs],
            in_specs=[SMEM] + [VMEM] * (len(args) - 1),
            out_specs=[FAR if far_out else VMEM] * len(outs),
            scratch_shapes=[pltpu.VMEM(shape, dtype) for shape, dtype in scratch]
            + ([pltpu.SemaphoreType.DMA((copies,))] if copies else []),
            compiler_params=params,
            cost_estimate=cost,
        )(*args)

    cells = (size_x, size_y, LANES)
    packet = (2 * HALO + 2, size_y, LANES)
    first, second, part, count, edge = call(
        cells_kernel,
        [(packet, BF16), (packet, BF16), (cells, BF16), (cells, BF16), ((2, size_y, LANES), BF16)],
        [],
        place,
        pack_cell(face_counts, point_counts),
    )
    first, second = exchange(first, second, "gx")
    packet = (wide + wide // size_y, size_y, LANES)
    strip = (wide, size_y, LANES)
    first, second, part_x, count_x, edge_x = call(
        wide_kernel,
        [(packet, BF16), (packet, BF16), (strip, BF16), (strip, BF16), ((wide, LANES), F32)],
        [],
        place,
        first,
        second,
        part,
        count,
        edge,
    )
    first, second = exchange(first, second, ("gy_chip", "gy_core"))
    own = sizes.own_x
    received = (first, second, part_x, count_x, edge_x)
    flat_f32 = ((flat, LANES), F32)
    (packet,) = call(
        start_kernel,
        [((copies, own + own // 2, 2 * sizes.own_y, LANES), BF16)],
        [flat_f32] * 4 + [((size_x * size_y, LANES), F32)],
        place,
        *received,
        mats[0],
    )
    near, far = gather(packet)
    iterate, field, scaled = call(
        surroundings_kernel,
        [flat_f32] * 3,
        [flat_f32],
        place,
        near,
        *received,
        cost=pl.CostEstimate(flops=1 << 22, bytes_accessed=4 << 20, transcendentals=0),
    )
    level = (sizes.flat, LANES)
    around = (16 + (own + 8) * (sizes.own_y + 16), LANES)
    scratch = [
        (level, F32),
        (level, F32),
        (level, F32),
        ((sizes.planes * sizes.rows, LANES), F32),
        (around, F32),
        (around, F32),
        ((flat, LANES), F32),
    ]
    level_two = (sizes.planes // 4, sizes.rows // 2, LANES)
    level_three = (sizes.planes // 16, sizes.rows // 4, LANES)
    iterate, packet, inverse, diag, screen_two, screen_three = call(
        lambda *refs: middle_kernel(sizes, *refs),
        [
            ((flat, LANES), F32),
            ((copies, own, 2 * sizes.own_y, LANES), BF16),
            (level, F32),
            (level, F32),
            (level_two, F32),
            (level_three, F32),
        ],
        scratch + [((size_x * size_y, LANES), F32)],
        place,
        near,
        far,
        iterate,
        field,
        scaled,
        count_x,
        *mats,
    )
    solution_own, residual_own = call(
        lambda *refs: last_kernel(sizes, *refs),
        [(cells, F32), (cells, F32)],
        scratch + [((flat, LANES), F32), (cells, F32), (cells, F32)],
        place,
        *gather(packet),
        iterate,
        field,
        scaled,
        count_x,
        inverse,
        diag,
        screen_two,
        screen_three,
        *mats,
        copies=4,
        far_out=True,
    )
    return solution_own, residual_own


def solution(mesh):
    mesh_x, mesh_y = mesh.shape["gx"], mesh.shape["gy"]
    split = Mesh(mesh.devices.reshape(mesh_x, mesh_y // 2, 2), ("gx", "gy_chip", "gy_core"))
    rows = ("gy_chip", "gy_core")

    def run(point_counts, face_counts):
        return jax.shard_map(
            per_device,
            mesh=split,
            in_specs=(P("gx", rows, None), P(None, "gx", rows, None)),
            out_specs=(P("gx", rows, None), P("gx", rows, None)),
            check_vma=False,
        )(point_counts, face_counts)

    return run
```

```python
import numpy as np
import jax
import jax.numpy as jnp
from jax import lax
from jax.experimental import pallas as pl
from jax.experimental.pallas import tpu as pltpu
from jax.sharding import Mesh, PartitionSpec as P

F32 = jnp.float32
BF16 = jnp.bfloat16
LANES = 128
HALO = 8
COARSE_ITERS = 6

screen_weight = 0.25
flux_scale = 0.125
low_edge = 0.3
high_edge = 2.0
centre = 0.5 * (high_edge + low_edge)
radius = 0.5 * (high_edge - low_edge)
ratio = centre / radius
mom_first = 1.0 / ratio
mom_second = 1.0 / (2.0 * ratio - mom_first)
keep = mom_second * mom_first
gain = 2.0 * mom_second / radius

VMEM = pl.BlockSpec(memory_space=pltpu.VMEM)
SMEM = pl.BlockSpec(memory_space=pltpu.SMEM)
FAR = pl.BlockSpec(memory_space=pltpu.HBM)


def transfer_matrix(level):
    pack, size_z = 1 << level, LANES >> level
    planes = 2 if level == 0 else 4
    out = np.zeros((planes * LANES, LANES), np.float32)
    for j in range(planes):
        for q in range(pack):
            coarse = j if level == 0 else (j * pack + q) // 2
            for z in range(size_z):
                out[j * LANES + q * size_z + z, coarse * (size_z // 2) + z // 2] = 1.0
    return jnp.asarray(out, BF16)


def two_parts(value):
    high = value.astype(BF16)
    return jnp.concatenate([high, (value - high.astype(F32)).astype(BF16)], 0)


def gather_lanes(value, matrix):
    both = jnp.dot(two_parts(value), matrix, preferred_element_type=F32)
    return both[: value.shape[0]] + both[value.shape[0] :]


def spread_lanes(value, matrix):
    dims = (((1,), (1,)), ((), ()))
    both = lax.dot_general(two_parts(value), matrix, dims, preferred_element_type=F32)
    return both[: value.shape[0]] + both[value.shape[0] :]


def lane_index():
    return lax.broadcasted_iota(jnp.int32, (1, LANES), 1)


def z_sum(value, size_z):
    lane = lane_index() & (size_z - 1)
    inner_low = (lane != 0).astype(F32)
    inner_high = (lane != size_z - 1).astype(F32)
    return pltpu.roll(value, 1, 1) * inner_low + pltpu.roll(value, LANES - 1, 1) * inner_high


def x_sum(before, here, after, size_z):
    if size_z == LANES:
        return before + after
    lane = lax.broadcasted_iota(jnp.int32, here.shape, 1)
    if 2 * size_z == LANES:
        return pltpu.roll(here + jnp.where(lane < size_z, after, before), size_z, 1)
    up = pltpu.roll(jnp.where(lane < size_z, after, here), LANES - size_z, 1)
    down = pltpu.roll(jnp.where(lane >= LANES - size_z, before, here), size_z, 1)
    return up + down


def neighbours(ref, base, rows, stride, size_z):
    here = ref[pl.ds(base, rows), :]
    total = x_sum(ref[pl.ds(base - stride, rows), :], here, ref[pl.ds(base + stride, rows), :], size_z)
    total = total + (ref[pl.ds(base - 1, rows), :] + ref[pl.ds(base + 1, rows), :])
    return here, total + z_sum(here, size_z)


def for_planes(count, body, limit=64):
    if count <= limit:
        for i in range(count):
            body(i)
    else:
        step = 8

        def block(k, carry):
            for j in range(step):
                body(k * step + j)
            return carry

        lax.fori_loop(0, count // step, block, 0)


def pair_rows(ref, start, rows):
    return ref[pl.ds(start, rows // 2, stride=2), :] + ref[pl.ds(start + 1, rows // 2, stride=2), :]


def pack_cell(faces, points):
    word = points << 18
    for c in range(3):
        word = word + ((faces[c] + 32) << (6 * c))
    return word


def cells_kernel(place, words, first, second, part, count, edge):
    size_x, size_y = words.shape[:2]
    lane = lax.broadcasted_iota(jnp.int32, (size_y, LANES), 1)
    row = lax.broadcasted_iota(jnp.int32, (size_y, LANES), 0)
    last_x = None
    for i in range(size_x):
        word = words[i]
        along_x, along_y, along_z = [((word >> (6 * c)) & 63) - 32 for c in range(3)]
        total = jnp.where(row != 0, pltpu.roll(along_y, 1, 0), 0) - along_y
        total = total + (jnp.where(lane != 0, pltpu.roll(along_z, 1, 1), 0) - along_z) - along_x
        if last_x is not None:
            total = total + last_x
        last_x = along_x
        part[i] = total.astype(F32).astype(BF16)
        count[i] = ((word >> 18) + 1).astype(F32).astype(BF16)
    edge[0] = last_x.astype(F32).astype(BF16)
    edge[1] = (((words[:, size_y - 1, :] >> 6) & 63) - 32).astype(F32).astype(BF16)

    def write(up, down):
        for target, start in ((up, size_x - HALO), (down, 0)):
            target[0:HALO] = part[start : start + HALO]
            target[HALO : 2 * HALO] = count[start : start + HALO]
            target[2 * HALO : 2 * HALO + 2] = edge[...]

    odd = place[0] % 2

    @pl.when(odd == 0)
    def _():
        write(first, second)

    @pl.when(odd == 1)
    def _():
        write(second, first)


def wide_kernel(place, got_first, got_second, part, count, edge, first, second, part_x, count_x, edge_x):
    size_x, size_y = part.shape[:2]
    wide = size_x + 2 * HALO

    def fill(below, above):
        part_x[0:HALO] = below[0:HALO]
        part_x[HALO + size_x :] = above[0:HALO]
        count_x[0:HALO] = below[HALO : 2 * HALO]
        count_x[HALO + size_x :] = above[HALO : 2 * HALO]
        part_x[HALO : HALO + size_x] = part[...]
        count_x[HALO : HALO + size_x] = count[...]
        part_x[HALO] = (part[0].astype(F32) + below[2 * HALO].astype(F32)).astype(BF16)
        part_x[HALO + size_x] = (above[0].astype(F32) + edge[0].astype(F32)).astype(BF16)
        edge_x[0:HALO] = below[2 * HALO + 1].astype(F32)[size_x - HALO :]
        edge_x[HALO : HALO + size_x] = edge[1].astype(F32)
        edge_x[HALO + size_x :] = above[2 * HALO + 1].astype(F32)[:HALO]

    odd = place[0] % 2

    @pl.when(odd == 0)
    def _():
        fill(got_second, got_first)

    @pl.when(odd == 1)
    def _():
        fill(got_first, got_second)

    def write(up, down):
        for i in range(wide):
            cells = part_x[i].astype(F32)
            points = count_x[i].astype(F32)
            up[i] = jnp.concatenate([cells[size_y - HALO :], points[size_y - HALO :]], 0).astype(BF16)
            down[i] = jnp.concatenate([cells[:HALO], points[:HALO]], 0).astype(BF16)
        for target in (up, down):
            for j in range(wide // size_y):
                target[wide + j] = edge_x[j * size_y : (j + 1) * size_y].astype(BF16)

    odd_y = place[1] % 2

    @pl.when(odd_y == 0)
    def _():
        write(first, second)

    @pl.when(odd_y == 1)
    def _():
        write(second, first)


def finest_parts(margin, wide, plane):
    planes = range(HALO - margin, wide - HALO + margin)
    if margin > 4:
        return [(8 + i * plane, 2 * plane) for i in planes[::2]]
    return [(8 + i * plane + HALO - 4, plane - 2 * HALO + 8) for i in planes]


def finest_step_one(source, target, field, scaled, margin, wide, plane):
    for base, rows in finest_parts(margin, wide, plane):
        at = pl.ds(base, rows)
        here, total = neighbours(source, base, rows, plane, LANES)
        fit = (field[at, :] + total) * scaled[at, :]
        target[at, :] = here + (fit - here) * (1.0 / centre)


def finest_step_two(source, old, field, scaled, margin, wide, plane):
    for base, rows in finest_parts(margin, wide, plane):
        at = pl.ds(base, rows)
        here, total = neighbours(source, base, rows, plane, LANES)
        fit = (field[at, :] + total) * scaled[at, :]
        old[at, :] = here + (keep * (here - old[at, :]) + gain * (fit - here))


def finest_step_two_from_zero(source, target, field, scaled, margin, wide, plane):
    for base, rows in finest_parts(margin, wide, plane):
        at = pl.ds(base, rows)
        here, total = neighbours(source, base, rows, plane, LANES)
        fit = (field[at, :] + total) * scaled[at, :]
        target[at, :] = here + (keep * here + gain * (fit - here))


def finest_residual(iterate, field, count, size_x, size_y, write):
    plane = size_y + 2 * HALO
    for i in range(size_x):
        base = 8 + (HALO + i) * plane + HALO
        here, total = neighbours(iterate, base, size_y, plane, LANES)
        diag = 6.0 + screen_weight * (count[HALO + i].astype(F32) - 1.0)
        write(i, here, field[pl.ds(base, size_y), :] + total - diag * here)


def restrict_finest(rows_ref, size_x, size_y, matrix):
    half = pair_rows(rows_ref, 0, size_x * size_y).reshape(size_x // 4, 4, size_y // 2, LANES)
    even = (half[:, 0] + half[:, 1]).reshape(-1, LANES)
    odd = (half[:, 2] + half[:, 3]).reshape(-1, LANES)
    return even, odd


def first_step(place, got, part_x, count_x, edge_x, iterate, field, inverse, margin):
    wide, size_y = part_x.shape[:2]
    plane = size_y + 2 * HALO
    even = place[1] % 2 == 0
    top = lax.broadcasted_iota(jnp.int32, (HALO, LANES), 0) == 0
    under_rows = [jnp.where(even, got[1][wide + j], got[0][wide + j]).astype(F32) for j in range(wide // size_y)]
    for i in range(HALO - margin, wide - HALO + margin):
        below = jnp.where(even, got[1][i], got[0][i]).astype(F32)
        above = jnp.where(even, got[0][i], got[1][i]).astype(F32)
        own = part_x[i].astype(F32)
        under = under_rows[i // size_y][i % size_y : i % size_y + 1]
        over = edge_x[i : i + 1]
        cells = jnp.concatenate(
            [
                below[:HALO],
                own[:HALO] + jnp.where(top, under, 0.0),
                own[HALO:],
                above[:HALO] + jnp.where(top, over, 0.0),
            ],
            0,
        )
        points = jnp.concatenate([below[HALO:], count_x[i].astype(F32), above[HALO:]], 0)
        given = flux_scale * cells
        inv = jnp.where(points > 0.0, 1.0 / (6.0 - screen_weight + screen_weight * points), 0.0)
        at = pl.ds(8 + i * plane, plane)
        field[at, :] = given
        inverse[at, :] = inv
        iterate[at, :] = (given * inv) * (1.0 / centre)


def start_kernel(
    place, got_first, got_second, part_x, count_x, edge_x, matrix, packet, first, second, field, inverse, rows_ref
):
    wide, size_y = part_x.shape[:2]
    size_x = wide - 2 * HALO
    plane = size_y + 2 * HALO
    first_step(place, (got_first, got_second), part_x, count_x, edge_x, first, field, inverse, 2)
    finest_step_two_from_zero(first, second, field, inverse, 1, wide, plane)

    def write(i, here, value):
        rows_ref[pl.ds(i * size_y, size_y), :] = value

    finest_residual(second, field, count_x, size_x, size_y, write)
    even, odd = restrict_finest(rows_ref, size_x, size_y, matrix)
    coarse = 0.125 * gather_lanes(jnp.concatenate([even, odd], 1), matrix[...])
    for i in range(size_x):
        rows_ref[pl.ds(i * size_y, size_y), :] = count_x[HALO + i].astype(F32) - 1.0
    even, odd = restrict_finest(rows_ref, size_x, size_y, matrix)
    points = jnp.dot(jnp.concatenate([even, odd], 1).astype(BF16), matrix[...], preferred_element_type=F32)
    send_coarse(packet, coarse, points, size_y // 2)


def surroundings_kernel(
    place, after, got_first, got_second, part_x, count_x, edge_x, iterate, field, inverse, first
):
    wide, size_y = part_x.shape[:2]
    plane = size_y + 2 * HALO
    zero = jnp.zeros((8, LANES), F32)
    for ref in (iterate, field, inverse, first):
        ref[0:8] = zero
        ref[8 + wide * plane :] = zero
    first_step(place, (got_first, got_second), part_x, count_x, edge_x, first, field, inverse, HALO)
    for base, rows in ((8, plane), (8 + (wide - 1) * plane, plane)):
        iterate[pl.ds(base, rows), :] = first[pl.ds(base, rows), :]
    finest_step_two_from_zero(first, iterate, field, inverse, HALO - 1, wide, plane)


def scale_of(code):
    return jnp.exp2(code * (1.0 / 128.0))


def send_coarse(packet, coarse, points, size_y):
    copies = packet.shape[0]
    tiles = [coarse[i : i + size_y] for i in range(0, coarse.shape[0], size_y)]
    largest = jnp.abs(tiles[0])
    for tile in tiles[1:]:
        largest = jnp.maximum(largest, jnp.abs(tile))
    largest = jnp.maximum(jnp.max(largest, 1, keepdims=True), 1e-30)
    code = jnp.ceil(128.0 * jnp.log2(largest * (1.0 / 32766.0)))
    scale = scale_of(-code)
    rows = [jnp.round(tile * scale) for tile in tiles]
    rows += [jnp.broadcast_to(code, (size_y, LANES)), jnp.zeros((size_y, LANES), F32)]
    if points is not None:
        rows += [points[i : i + size_y] for i in range(0, points.shape[0], size_y)]
    for i in range(0, len(rows), 2):
        tile = jnp.concatenate(rows[i : i + 2], 0).astype(jnp.int32).astype(jnp.int16)
        for k in range(copies):
            packet[k, i // 2] = tile


def packed_apply(value, screen, factor, size_z):
    planes, size_y, _ = value.shape
    flat = value.reshape(planes * size_y, LANES)
    empty = jnp.zeros((1, size_y, LANES), F32)
    if planes > 1:
        before = jnp.concatenate([empty, value[:-1]], 0).reshape(flat.shape)
        after = jnp.concatenate([value[1:], empty], 0).reshape(flat.shape)
    else:
        before = after = jnp.zeros_like(flat)
    row = lax.broadcasted_iota(jnp.int32, value.shape, 1)
    along_y = jnp.where(row != 0, pltpu.roll(value, 1, 1), 0.0) + jnp.where(
        row != size_y - 1, pltpu.roll(value, size_y - 1, 1), 0.0
    )
    total = x_sum(before, flat, after, size_z) + z_sum(flat, size_z)
    return (6.0 * value - (total.reshape(value.shape) + along_y)) * factor + screen * value


def totals_of(*values):
    rows = jnp.concatenate([jnp.sum(value, 0) for value in values], 0)
    sums = jnp.sum(rows, 1, keepdims=True).reshape(len(values), -1, 1)
    sums = jnp.sum(sums, 1, keepdims=True)
    return [sums[i : i + 1] for i in range(len(values))]


def conjugate_gradients(target, screen, factor, size_z):
    iterate = jnp.zeros_like(target)
    remain = target
    search = target
    for step in range(COARSE_ITERS):
        image = packed_apply(search, screen, factor, size_z)
        if step + 1 == COARSE_ITERS:
            norm_now, bent = totals_of(remain * remain, search * image)
            return iterate + (norm_now / bent) * search
        norm_now, bent, mixed, norm_image = totals_of(
            remain * remain, search * image, remain * image, image * image
        )
        length = norm_now / bent
        iterate = iterate + length * search
        remain = remain - length * image
        norm_next = norm_now - 2.0 * length * mixed + length * length * norm_image
        search = remain + (norm_next / norm_now) * search


def smooth_packed(iterate, target, screen, inv, factor, size_z):
    step = (target - packed_apply(iterate, screen, factor, size_z)) * inv * (1.0 / centre)
    iterate = iterate + step
    again = (target - packed_apply(iterate, screen, factor, size_z)) * inv
    return iterate + (keep * step + gain * again)


def smooth_packed_zero(target, screen, inv, factor, size_z):
    step = target * inv * (1.0 / centre)
    again = (target - packed_apply(step, screen, factor, size_z)) * inv
    return step + (keep * step + gain * again)


def add_lanes(rows_ref, planes, size_y, matrix):
    half = pair_rows(rows_ref, 0, planes * size_y).reshape(planes // 4, 4, size_y // 2, LANES)
    wide = jnp.concatenate([half[:, j].reshape(-1, LANES) for j in range(4)], 1)
    return gather_lanes(wide, matrix[...]).reshape(planes // 4, size_y // 2, LANES)


def copy_level(value, matrix):
    planes, size_y, _ = value.shape
    wide = spread_lanes(value.reshape(-1, LANES), matrix[...]).reshape(planes, size_y, 4 * LANES)
    return jnp.stack([wide[:, :, j * LANES : (j + 1) * LANES] for j in range(4)], 1).reshape(
        4 * planes, size_y, LANES
    )


class Sizes:
    def __init__(self, mesh_x, mesh_y, size_x, size_y):
        self.mesh_x, self.mesh_y = mesh_x, mesh_y
        self.own_x, self.own_y = size_x // 4, size_y // 2
        self.planes, self.rows = mesh_x * self.own_x, mesh_y * self.own_y
        self.stride = self.rows + 8
        self.flat = (self.planes + 8) * self.stride + 8
        self.pad_x = 4


def level_one(place, gathered, sizes, mats, refs, first):
    mat_1, mat_2 = mats
    given, inverse, diag, step, iterate, rows_ref, level_two, local_a, local_b = refs
    size_z = LANES // 2
    factor = 0.25
    planes, rows, stride, pad = sizes.planes, sizes.rows, sizes.stride, sizes.pad_x
    own_x, own_y = sizes.own_x, sizes.own_y

    def clear(ref):
        ref[0 : pad * stride + 8] = jnp.zeros((pad * stride + 8, LANES), F32)
        ref[(pad + planes) * stride :] = jnp.zeros((pad * stride + 8, LANES), F32)

        def gap(i):
            ref[pl.ds((pad + i) * stride, 8), :] = jnp.zeros((8, LANES), F32)

        for_planes(planes, gap)

    for ref in (given, step, iterate) + ((inverse, diag) if first else ()):
        clear(ref)

    core = place[1] % 2
    per_core = sizes.mesh_x * sizes.mesh_y // 2

    def block(b):
        source, side = (gathered[0], core) if b < per_core else (gathered[1], 1 - core)
        gx = b % per_core // (sizes.mesh_y // 2)
        gy = 2 * (b % (sizes.mesh_y // 2)) + side
        tiles = []
        for i in range(source.shape[1]):
            tile = source[b % per_core, i].astype(jnp.int32).astype(F32)
            tiles += [tile[:own_y], tile[own_y:]]
        scale = scale_of(tiles[own_x])
        for i in range(own_x):
            start = (pad + gx * own_x + i) * stride + 8 + gy * own_y
            at = pl.ds(pl.multiple_of(start, 8), own_y)
            value = tiles[i] * scale
            if first:
                d = 6.0 * factor + (screen_weight * 0.125) * tiles[own_x + 2 + i]
                diag[at, :] = d
                inv = 1.0 / d
                inverse[at, :] = inv
            else:
                inv = inverse[at, :]
            given[at, :] = value
            step[at, :] = value * inv * (1.0 / centre)

    for b in range(sizes.mesh_x * sizes.mesh_y):
        block(b)

    def second(i):
        base = (pad + i) * stride + 8
        at = pl.ds(base, rows)
        here, total = neighbours(step, base, rows, stride, size_z)
        fit = (given[at, :] + factor * total) * inverse[at, :]
        iterate[at, :] = here + (keep * here + gain * (fit - here))

    for_planes(planes, second)

    def residual(i):
        base = (pad + i) * stride + 8
        at = pl.ds(base, rows)
        here, total = neighbours(iterate, base, rows, stride, size_z)
        rows_ref[pl.ds(i * rows, rows), :] = given[at, :] + factor * total - diag[at, :] * here

    for_planes(planes, residual)
    target = 0.125 * add_lanes(rows_ref, planes, rows, mat_1)

    screen_two, screen_three = level_two
    if first:

        def screens(i):
            at = pl.ds((pad + i) * stride + 8, rows)
            rows_ref[pl.ds(i * rows, rows), :] = diag[at, :] - 6.0 * factor

        for_planes(planes, screens)
        screen_two[...] = 0.125 * add_lanes(rows_ref, planes, rows, mat_1)
    planes_2, rows_2 = planes // 4, rows // 2
    screen = screen_two[...]
    inv = 1.0 / (6.0 * factor**2 + screen)
    if first:
        rows_ref[0 : planes_2 * rows_2] = screen.reshape(-1, LANES)
        screen_three[...] = 0.125 * add_lanes(rows_ref, planes_2, rows_2, mat_2)
    value = smooth_packed_zero(target, screen, inv, factor**2, LANES // 4)
    remain = target - packed_apply(value, screen, factor**2, LANES // 4)
    rows_ref[0 : planes_2 * rows_2] = remain.reshape(-1, LANES)
    target_3 = 0.125 * add_lanes(rows_ref, planes_2, rows_2, mat_2)
    error = conjugate_gradients(target_3, screen_three[...], factor**3, LANES // 8)
    error = copy_level(error, mat_2).reshape(-1, LANES)
    count = planes_2 * rows_2
    rows_ref[pl.ds(0, count // 2, stride=2), :] = error
    rows_ref[pl.ds(1, count // 2, stride=2), :] = error
    value = value + rows_ref[0:count].reshape(value.shape)
    value = smooth_packed(value, target, screen, inv, factor**2, LANES // 4)

    rows_ref[0:rows_2] = jnp.zeros((rows_2, LANES), F32)
    rows_ref[(planes_2 + 1) * rows_2 : (planes_2 + 2) * rows_2] = jnp.zeros((rows_2, LANES), F32)
    rows_ref[rows_2 : (planes_2 + 1) * rows_2] = value.reshape(-1, LANES)
    near_2 = own_x // 4 + 2
    start = pl.multiple_of(place[0] * (own_x // 4) * rows_2, 8)
    near = rows_ref[pl.ds(start, near_2 * rows_2), :].reshape(near_2, rows_2, LANES)
    error = copy_level(near, mat_1)
    near_x, near_y = 4 * near_2, own_y + 16
    first_plane = place[0] * own_x
    for i in range(near_x):
        base = (first_plane + i) * stride + 8
        even, odd = pl.ds(base, rows_2, stride=2), pl.ds(base + 1, rows_2, stride=2)
        iterate[even, :] = iterate[even, :] + error[i]
        iterate[odd, :] = iterate[odd, :] + error[i]
    for i in range(near_x):
        at = pl.ds(pl.multiple_of((first_plane + i) * stride + place[1] * own_y, 8), near_y)
        local_a[pl.ds(8 + i * near_y, near_y), :] = iterate[at, :]
    for ref in (local_a, local_b):
        ref[0:8] = jnp.zeros((8, LANES), F32)
        ref[8 + near_x * near_y :] = jnp.zeros((8, LANES), F32)
    ends = pl.ds(8, near_y), pl.ds(8 + (near_x - 1) * near_y, near_y)
    for at in ends:
        local_b[at, :] = jnp.zeros((near_y, LANES), F32)

    def fit_of(ref, i):
        at = pl.ds(pl.multiple_of((first_plane + i) * stride + place[1] * own_y, 8), near_y)
        here, total = neighbours(ref, 8 + i * near_y, near_y, near_y, size_z)
        return here, (given[at, :] + factor * total) * inverse[at, :]

    for i in range(1, near_x - 1):
        here, fit = fit_of(local_a, i)
        local_b[pl.ds(8 + i * near_y, near_y), :] = here + (fit - here) * (1.0 / centre)
    for i in range(2, near_x - 2):
        here, fit = fit_of(local_b, i)
        at = pl.ds(8 + i * near_y, near_y)
        local_a[at, :] = here + (keep * (here - local_a[at, :]) + gain * (fit - here))


def add_correction(start, iterate, local, sizes, mat_0, plane):
    ends = pl.ds(0, 8), pl.ds(start.shape[0] - 8, 8)
    for at in ends:
        iterate[at, :] = start[at, :]
    near_y = sizes.own_y + 16
    half_y = plane // 2
    planes = sizes.own_x + 4
    value = jnp.concatenate(
        [local[pl.ds(8 + (2 + i) * near_y + 4, half_y), :] for i in range(planes)], 0
    )
    wide = spread_lanes(value, mat_0[...])
    for i in range(planes):
        for j in range(4):
            error = wide[i * half_y : (i + 1) * half_y, (j // 2) * LANES : (j // 2 + 1) * LANES]
            for side in (0, 1):
                at = pl.ds(8 + (4 * i + j) * plane + side, half_y, stride=2)
                iterate[at, :] = start[at, :] + error


def middle_kernel(sizes, place, near, far, start, field, scaled, count_x, mat_0, mat_1, mat_2, *rest):
    iterate, packet, inverse, diag, screen_two, screen_three = rest[:6]
    given, step, coarse, rows_ref, local_a, local_b, other, fine_rows = rest[6:]
    wide, size_y = count_x.shape[:2]
    size_x = wide - 2 * HALO
    plane = size_y + 2 * HALO
    refs = (given, inverse, diag, step, coarse, rows_ref, (screen_two, screen_three), local_a, local_b)
    level_one(place, (near, far), sizes, (mat_1, mat_2), refs, True)
    add_correction(start, iterate, local_a, sizes, mat_0, plane)
    finest_step_one(iterate, other, field, scaled, 6, wide, plane)
    finest_step_two(other, iterate, field, scaled, 5, wide, plane)
    finest_step_one(iterate, other, field, scaled, 4, wide, plane)
    finest_step_two(other, iterate, field, scaled, 3, wide, plane)

    def write(i, here, value):
        fine_rows[pl.ds(i * size_y, size_y), :] = value

    finest_residual(iterate, field, count_x, size_x, size_y, write)
    even, odd = restrict_finest(fine_rows, size_x, size_y, mat_0)
    send_coarse(packet, 0.125 * gather_lanes(jnp.concatenate([even, odd], 1), mat_0[...]), None, size_y // 2)


def last_kernel(sizes, place, near, far, start, field, scaled, count_x, inverse, diag, screen_two, screen_three, *rest):
    mat_0, mat_1, mat_2, solution_far, residual_far = rest[:5]
    given, step, coarse, rows_ref, local_a, local_b, iterate, other, solution_out, residual_out, left = rest[5:]
    wide, size_y = count_x.shape[:2]
    size_x = wide - 2 * HALO
    plane = size_y + 2 * HALO
    refs = (given, inverse, diag, step, coarse, rows_ref, (screen_two, screen_three), local_a, local_b)
    level_one(place, (near, far), sizes, (mat_1, mat_2), refs, False)
    add_correction(start, iterate, local_a, sizes, mat_0, plane)
    finest_step_one(iterate, other, field, scaled, 2, wide, plane)
    finest_step_two(other, iterate, field, scaled, 1, wide, plane)

    def send(source, target, which):
        copy = pltpu.make_async_copy(source, target, left.at[which])
        copy.start()
        return copy

    for i in range(size_x):
        solution_out[i] = iterate[pl.ds(8 + (HALO + i) * plane + HALO, size_y), :]
    copies = [send(solution_out, solution_far, 0)]

    def write(i, here, value):
        residual_out[i] = value
        if (2 * i + 2) % size_x == 0:
            half = pl.ds(i + 1 - size_x // 2, size_x // 2)
            copies.append(send(residual_out.at[half], residual_far.at[half], 1 + (i + 1) * 2 // size_x))

    finest_residual(iterate, field, count_x, size_x, size_y, write)
    for copy in copies:
        copy.wait()


def exchange(first, second, axis):
    count = lax.axis_size(axis)

    def pairs(start):
        found = []
        for i in range(start, count - 1, 2):
            found += [(i, i + 1), (i + 1, i)]
        return found

    return lax.ppermute(first, axis, pairs(0)), lax.ppermute(second, axis, pairs(1))


def gather(packet):
    near = lax.all_to_all(packet, ("gx", "gy_chip"), 0, 0, tiled=True)
    return near, lax.ppermute(near, "gy_core", [(0, 1), (1, 0)])


def per_device(point_counts, face_counts):
    size_x, size_y, size_z = point_counts.shape
    assert size_z == LANES and size_x == 16 and size_y == 16
    mesh_x = lax.axis_size("gx")
    mesh_y = lax.axis_size("gy_chip") * lax.axis_size("gy_core")
    gx = lax.axis_index("gx")
    gy = lax.axis_index("gy_chip") * 2 + lax.axis_index("gy_core")
    place = jnp.stack([gx, gy]).astype(jnp.int32)
    wide, plane = size_x + 2 * HALO, size_y + 2 * HALO
    flat = 16 + wide * plane
    sizes = Sizes(mesh_x, mesh_y, size_x, size_y)
    copies = mesh_x * mesh_y // 2
    mats = [transfer_matrix(level) for level in range(3)]
    params = pltpu.CompilerParams(vmem_limit_bytes=(24 if sizes.flat < 4096 else 56) * 2**20)

    def call(kernel, outs, scratch, *args, copies=0, far_out=False, cost=None):
        return pl.pallas_call(
            kernel,
            out_shape=[jax.ShapeDtypeStruct(shape, dtype) for shape, dtype in outs],
            in_specs=[SMEM] + [VMEM] * (len(args) - 1),
            out_specs=[FAR if far_out else VMEM] * len(outs),
            scratch_shapes=[pltpu.VMEM(shape, dtype) for shape, dtype in scratch]
            + ([pltpu.SemaphoreType.DMA((copies,))] if copies else []),
            compiler_params=params,
            cost_estimate=cost,
        )(*args)

    cells = (size_x, size_y, LANES)
    packet = (2 * HALO + 2, size_y, LANES)
    first, second, part, count, edge = call(
        cells_kernel,
        [(packet, BF16), (packet, BF16), (cells, BF16), (cells, BF16), ((2, size_y, LANES), BF16)],
        [],
        place,
        pack_cell(face_counts, point_counts),
    )
    first, second = exchange(first, second, "gx")
    packet = (wide + wide // size_y, size_y, LANES)
    strip = (wide, size_y, LANES)
    first, second, part_x, count_x, edge_x = call(
        wide_kernel,
        [(packet, BF16), (packet, BF16), (strip, BF16), (strip, BF16), ((wide, LANES), F32)],
        [],
        place,
        first,
        second,
        part,
        count,
        edge,
    )
    first, second = exchange(first, second, ("gy_chip", "gy_core"))
    own = sizes.own_x
    received = (first, second, part_x, count_x, edge_x)
    flat_f32 = ((flat, LANES), F32)
    (packet,) = call(
        start_kernel,
        [((copies, own + 1, 2 * sizes.own_y, LANES), jnp.int16)],
        [flat_f32] * 4 + [((size_x * size_y, LANES), F32)],
        place,
        *received,
        mats[0],
    )
    near, far = gather(packet)
    iterate, field, scaled = call(
        surroundings_kernel,
        [flat_f32] * 3,
        [flat_f32],
        place,
        near,
        *received,
        cost=pl.CostEstimate(flops=1 << 22, bytes_accessed=4 << 20, transcendentals=0),
    )
    level = (sizes.flat, LANES)
    around = (16 + (own + 8) * (sizes.own_y + 16), LANES)
    scratch = [
        (level, F32),
        (level, F32),
        (level, F32),
        ((sizes.planes * sizes.rows, LANES), F32),
        (around, F32),
        (around, F32),
        ((flat, LANES), F32),
    ]
    level_two = (sizes.planes // 4, sizes.rows // 2, LANES)
    level_three = (sizes.planes // 16, sizes.rows // 4, LANES)
    iterate, packet, inverse, diag, screen_two, screen_three = call(
        lambda *refs: middle_kernel(sizes, *refs),
        [
            ((flat, LANES), F32),
            ((copies, own // 2 + 1, 2 * sizes.own_y, LANES), jnp.int16),
            (level, F32),
            (level, F32),
            (level_two, F32),
            (level_three, F32),
        ],
        scratch + [((size_x * size_y, LANES), F32)],
        place,
        near,
        far,
        iterate,
        field,
        scaled,
        count_x,
        *mats,
    )
    solution_own, residual_own = call(
        lambda *refs: last_kernel(sizes, *refs),
        [(cells, F32), (cells, F32)],
        scratch + [((flat, LANES), F32), (cells, F32), (cells, F32)],
        place,
        *gather(packet),
        iterate,
        field,
        scaled,
        count_x,
        inverse,
        diag,
        screen_two,
        screen_three,
        *mats,
        copies=4,
        far_out=True,
    )
    return solution_own, residual_own


def solution(mesh):
    mesh_x, mesh_y = mesh.shape["gx"], mesh.shape["gy"]
    split = Mesh(mesh.devices.reshape(mesh_x, mesh_y // 2, 2), ("gx", "gy_chip", "gy_core"))
    rows = ("gy_chip", "gy_core")

    def run(point_counts, face_counts):
        return jax.shard_map(
            per_device,
            mesh=split,
            in_specs=(P("gx", rows, None), P(None, "gx", rows, None)),
            out_specs=(P("gx", rows, None), P("gx", rows, None)),
            check_vma=False,
        )(point_counts, face_counts)

    return run
```

```python
import numpy as np
import jax
import jax.numpy as jnp
from jax import lax
from jax.experimental import pallas as pl
from jax.experimental.pallas import tpu as pltpu
from jax.sharding import Mesh, PartitionSpec as P

F32 = jnp.float32
BF16 = jnp.bfloat16
LANES = 128
HALO = 8
COARSE_ITERS = 6

screen_weight = 0.25
flux_scale = 0.125
low_edge = 0.3
high_edge = 2.0
centre = 0.5 * (high_edge + low_edge)
radius = 0.5 * (high_edge - low_edge)
ratio = centre / radius
mom_first = 1.0 / ratio
mom_second = 1.0 / (2.0 * ratio - mom_first)
keep = mom_second * mom_first
gain = 2.0 * mom_second / radius

VMEM = pl.BlockSpec(memory_space=pltpu.VMEM)
SMEM = pl.BlockSpec(memory_space=pltpu.SMEM)
FAR = pl.BlockSpec(memory_space=pltpu.HBM)


def transfer_matrix(level):
    pack, size_z = 1 << level, LANES >> level
    planes = 2 if level == 0 else 4
    out = np.zeros((planes * LANES, LANES), np.float32)
    for j in range(planes):
        for q in range(pack):
            coarse = j if level == 0 else (j * pack + q) // 2
            for z in range(size_z):
                out[j * LANES + q * size_z + z, coarse * (size_z // 2) + z // 2] = 1.0
    return jnp.asarray(out, BF16)


def in_parts(value):
    high = value.astype(BF16)
    rest = value - high.astype(F32)
    middle = rest.astype(BF16)
    return jnp.concatenate([high, middle, (rest - middle.astype(F32)).astype(BF16)], 0)


def add_parts(value, rows):
    return value[:rows] + (value[rows : 2 * rows] + value[2 * rows :])


def gather_lanes(value, matrix):
    return add_parts(jnp.dot(in_parts(value), matrix, preferred_element_type=F32), value.shape[0])


def spread_lanes(value, matrix):
    dims = (((1,), (1,)), ((), ()))
    return add_parts(lax.dot_general(in_parts(value), matrix, dims, preferred_element_type=F32), value.shape[0])


def lane_index():
    return lax.broadcasted_iota(jnp.int32, (1, LANES), 1)


def z_sum(value, size_z):
    lane = lane_index() & (size_z - 1)
    inner_low = (lane != 0).astype(F32)
    inner_high = (lane != size_z - 1).astype(F32)
    return pltpu.roll(value, 1, 1) * inner_low + pltpu.roll(value, LANES - 1, 1) * inner_high


def x_sum(before, here, after, size_z):
    if size_z == LANES:
        return before + after
    lane = lax.broadcasted_iota(jnp.int32, here.shape, 1)
    if 2 * size_z == LANES:
        return pltpu.roll(here + jnp.where(lane < size_z, after, before), size_z, 1)
    up = pltpu.roll(jnp.where(lane < size_z, after, here), LANES - size_z, 1)
    down = pltpu.roll(jnp.where(lane >= LANES - size_z, before, here), size_z, 1)
    return up + down


def neighbours(ref, base, rows, stride, size_z):
    here = ref[pl.ds(base, rows), :]
    total = x_sum(ref[pl.ds(base - stride, rows), :], here, ref[pl.ds(base + stride, rows), :], size_z)
    total = total + (ref[pl.ds(base - 1, rows), :] + ref[pl.ds(base + 1, rows), :])
    return here, total + z_sum(here, size_z)


def for_planes(count, body, limit=64):
    if count <= limit:
        for i in range(count):
            body(i)
    else:
        step = 8

        def block(k, carry):
            for j in range(step):
                body(k * step + j)
            return carry

        lax.fori_loop(0, count // step, block, 0)


def pair_rows(ref, start, rows):
    return ref[pl.ds(start, rows // 2, stride=2), :] + ref[pl.ds(start + 1, rows // 2, stride=2), :]


def pack_cell(faces, points):
    word = points << 18
    for c in range(3):
        word = word + ((faces[c] + 32) << (6 * c))
    return word


def cells_kernel(place, words, first, second, part, count, edge):
    size_x, size_y = words.shape[:2]
    lane = lax.broadcasted_iota(jnp.int32, (size_y, LANES), 1)
    row = lax.broadcasted_iota(jnp.int32, (size_y, LANES), 0)
    last_x = None
    for i in range(size_x):
        word = words[i]
        along_x, along_y, along_z = [((word >> (6 * c)) & 63) - 32 for c in range(3)]
        total = jnp.where(row != 0, pltpu.roll(along_y, 1, 0), 0) - along_y
        total = total + (jnp.where(lane != 0, pltpu.roll(along_z, 1, 1), 0) - along_z) - along_x
        if last_x is not None:
            total = total + last_x
        last_x = along_x
        part[i] = total.astype(F32).astype(BF16)
        count[i] = ((word >> 18) + 1).astype(F32).astype(BF16)
    edge[0] = last_x.astype(F32).astype(BF16)
    edge[1] = (((words[:, size_y - 1, :] >> 6) & 63) - 32).astype(F32).astype(BF16)

    def write(up, down):
        for target, start in ((up, size_x - HALO), (down, 0)):
            target[0:HALO] = part[start : start + HALO]
            target[HALO : 2 * HALO] = count[start : start + HALO]
            target[2 * HALO : 2 * HALO + 2] = edge[...]

    odd = place[0] % 2

    @pl.when(odd == 0)
    def _():
        write(first, second)

    @pl.when(odd == 1)
    def _():
        write(second, first)


def wide_kernel(place, got_first, got_second, part, count, edge, first, second, part_x, count_x, edge_x):
    size_x, size_y = part.shape[:2]
    wide = size_x + 2 * HALO

    def fill(below, above):
        part_x[0:HALO] = below[0:HALO]
        part_x[HALO + size_x :] = above[0:HALO]
        count_x[0:HALO] = below[HALO : 2 * HALO]
        count_x[HALO + size_x :] = above[HALO : 2 * HALO]
        part_x[HALO : HALO + size_x] = part[...]
        count_x[HALO : HALO + size_x] = count[...]
        part_x[HALO] = (part[0].astype(F32) + below[2 * HALO].astype(F32)).astype(BF16)
        part_x[HALO + size_x] = (above[0].astype(F32) + edge[0].astype(F32)).astype(BF16)
        edge_x[0:HALO] = below[2 * HALO + 1].astype(F32)[size_x - HALO :]
        edge_x[HALO : HALO + size_x] = edge[1].astype(F32)
        edge_x[HALO + size_x :] = above[2 * HALO + 1].astype(F32)[:HALO]

    odd = place[0] % 2

    @pl.when(odd == 0)
    def _():
        fill(got_second, got_first)

    @pl.when(odd == 1)
    def _():
        fill(got_first, got_second)

    def write(up, down):
        for i in range(wide):
            cells = part_x[i].astype(F32)
            points = count_x[i].astype(F32)
            up[i] = jnp.concatenate([cells[size_y - HALO :], points[size_y - HALO :]], 0).astype(BF16)
            down[i] = jnp.concatenate([cells[:HALO], points[:HALO]], 0).astype(BF16)
        for target in (up, down):
            for j in range(wide // size_y):
                target[wide + j] = edge_x[j * size_y : (j + 1) * size_y].astype(BF16)

    odd_y = place[1] % 2

    @pl.when(odd_y == 0)
    def _():
        write(first, second)

    @pl.when(odd_y == 1)
    def _():
        write(second, first)


def finest_parts(margin, wide, plane):
    planes = range(HALO - margin, wide - HALO + margin)
    if margin > 4:
        return [(8 + i * plane, 2 * plane) for i in planes[::2]]
    return [(8 + i * plane + HALO - 4, plane - 2 * HALO + 8) for i in planes]


def finest_step_one(source, target, field, scaled, margin, wide, plane):
    for base, rows in finest_parts(margin, wide, plane):
        at = pl.ds(base, rows)
        here, total = neighbours(source, base, rows, plane, LANES)
        fit = (field[at, :] + total) * scaled[at, :]
        target[at, :] = here + (fit - here) * (1.0 / centre)


def finest_step_two(source, old, field, scaled, margin, wide, plane):
    for base, rows in finest_parts(margin, wide, plane):
        at = pl.ds(base, rows)
        here, total = neighbours(source, base, rows, plane, LANES)
        fit = (field[at, :] + total) * scaled[at, :]
        old[at, :] = here + (keep * (here - old[at, :]) + gain * (fit - here))


def finest_step_two_from_zero(source, target, field, scaled, margin, wide, plane):
    for base, rows in finest_parts(margin, wide, plane):
        at = pl.ds(base, rows)
        here, total = neighbours(source, base, rows, plane, LANES)
        fit = (field[at, :] + total) * scaled[at, :]
        target[at, :] = here + (keep * here + gain * (fit - here))


def finest_residual(iterate, field, count, size_x, size_y, write):
    plane = size_y + 2 * HALO
    for i in range(size_x):
        base = 8 + (HALO + i) * plane + HALO
        here, total = neighbours(iterate, base, size_y, plane, LANES)
        diag = 6.0 + screen_weight * (count[HALO + i].astype(F32) - 1.0)
        write(i, here, field[pl.ds(base, size_y), :] + total - diag * here)


def restrict_finest(rows_ref, size_x, size_y, matrix):
    half = pair_rows(rows_ref, 0, size_x * size_y).reshape(size_x // 4, 4, size_y // 2, LANES)
    even = (half[:, 0] + half[:, 1]).reshape(-1, LANES)
    odd = (half[:, 2] + half[:, 3]).reshape(-1, LANES)
    return even, odd


def first_step(place, got, part_x, count_x, edge_x, iterate, field, inverse, margin):
    wide, size_y = part_x.shape[:2]
    plane = size_y + 2 * HALO
    even = place[1] % 2 == 0
    top = lax.broadcasted_iota(jnp.int32, (HALO, LANES), 0) == 0
    under_rows = [jnp.where(even, got[1][wide + j], got[0][wide + j]).astype(F32) for j in range(wide // size_y)]
    for i in range(HALO - margin, wide - HALO + margin):
        below = jnp.where(even, got[1][i], got[0][i]).astype(F32)
        above = jnp.where(even, got[0][i], got[1][i]).astype(F32)
        own = part_x[i].astype(F32)
        under = under_rows[i // size_y][i % size_y : i % size_y + 1]
        over = edge_x[i : i + 1]
        cells = jnp.concatenate(
            [
                below[:HALO],
                own[:HALO] + jnp.where(top, under, 0.0),
                own[HALO:],
                above[:HALO] + jnp.where(top, over, 0.0),
            ],
            0,
        )
        points = jnp.concatenate([below[HALO:], count_x[i].astype(F32), above[HALO:]], 0)
        given = flux_scale * cells
        inv = jnp.where(points > 0.0, 1.0 / (6.0 - screen_weight + screen_weight * points), 0.0)
        at = pl.ds(8 + i * plane, plane)
        field[at, :] = given
        inverse[at, :] = inv
        iterate[at, :] = (given * inv) * (1.0 / centre)


def start_kernel(
    place, got_first, got_second, part_x, count_x, edge_x, matrix, packet, first, second, field, inverse, rows_ref
):
    wide, size_y = part_x.shape[:2]
    size_x = wide - 2 * HALO
    plane = size_y + 2 * HALO
    first_step(place, (got_first, got_second), part_x, count_x, edge_x, first, field, inverse, 2)
    finest_step_two_from_zero(first, second, field, inverse, 1, wide, plane)

    def write(i, here, value):
        rows_ref[pl.ds(i * size_y, size_y), :] = value

    finest_residual(second, field, count_x, size_x, size_y, write)
    even, odd = restrict_finest(rows_ref, size_x, size_y, matrix)
    coarse = 0.125 * gather_lanes(jnp.concatenate([even, odd], 1), matrix[...])
    for i in range(size_x):
        rows_ref[pl.ds(i * size_y, size_y), :] = count_x[HALO + i].astype(F32) - 1.0
    even, odd = restrict_finest(rows_ref, size_x, size_y, matrix)
    points = jnp.dot(jnp.concatenate([even, odd], 1).astype(BF16), matrix[...], preferred_element_type=F32)
    send_coarse(packet, coarse, points, size_y // 2)


def surroundings_kernel(
    place, after, got_first, got_second, part_x, count_x, edge_x, iterate, field, inverse, first
):
    wide, size_y = part_x.shape[:2]
    plane = size_y + 2 * HALO
    zero = jnp.zeros((8, LANES), F32)
    for ref in (iterate, field, inverse, first):
        ref[0:8] = zero
        ref[8 + wide * plane :] = zero
    first_step(place, (got_first, got_second), part_x, count_x, edge_x, first, field, inverse, HALO)
    for base, rows in ((8, plane), (8 + (wide - 1) * plane, plane)):
        iterate[pl.ds(base, rows), :] = first[pl.ds(base, rows), :]
    finest_step_two_from_zero(first, iterate, field, inverse, HALO - 1, wide, plane)


def scale_of(code):
    return jnp.exp2(code * (1.0 / 128.0))


def send_coarse(packet, coarse, points, size_y):
    copies = packet.shape[0]
    tiles = [coarse[i : i + size_y] for i in range(0, coarse.shape[0], size_y)]
    largest = jnp.abs(tiles[0])
    for tile in tiles[1:]:
        largest = jnp.maximum(largest, jnp.abs(tile))
    largest = jnp.maximum(jnp.max(largest, 1, keepdims=True), 1e-30)
    code = jnp.ceil(128.0 * jnp.log2(largest * (1.0 / 32766.0)))
    scale = scale_of(-code)
    rows = [jnp.round(tile * scale) for tile in tiles]
    rows += [jnp.broadcast_to(code, (size_y, LANES)), jnp.zeros((size_y, LANES), F32)]
    if points is not None:
        rows += [points[i : i + size_y] for i in range(0, points.shape[0], size_y)]
    for i in range(0, len(rows), 2):
        tile = jnp.concatenate(rows[i : i + 2], 0).astype(jnp.int32).astype(jnp.int16)
        for k in range(copies):
            packet[k, i // 2] = tile


def packed_apply(value, screen, factor, size_z):
    planes, size_y, _ = value.shape
    flat = value.reshape(planes * size_y, LANES)
    empty = jnp.zeros((1, size_y, LANES), F32)
    if planes > 1:
        before = jnp.concatenate([empty, value[:-1]], 0).reshape(flat.shape)
        after = jnp.concatenate([value[1:], empty], 0).reshape(flat.shape)
    else:
        before = after = jnp.zeros_like(flat)
    row = lax.broadcasted_iota(jnp.int32, value.shape, 1)
    along_y = jnp.where(row != 0, pltpu.roll(value, 1, 1), 0.0) + jnp.where(
        row != size_y - 1, pltpu.roll(value, size_y - 1, 1), 0.0
    )
    total = x_sum(before, flat, after, size_z) + z_sum(flat, size_z)
    return (6.0 * value - (total.reshape(value.shape) + along_y)) * factor + screen * value


def totals_of(*values):
    rows = jnp.concatenate([jnp.sum(value, 0) for value in values], 0)
    sums = jnp.sum(rows, 1, keepdims=True).reshape(len(values), -1, 1)
    sums = jnp.sum(sums, 1, keepdims=True)
    return [sums[i : i + 1] for i in range(len(values))]


def conjugate_gradients(target, screen, factor, size_z):
    planes, size_y, _ = target.shape
    least = sum(2.0 - 2.0 * np.cos(np.pi / (n + 1)) for n in (planes * (LANES // size_z), size_y, size_z))
    longest = 1.001 / (factor * least)
    remain = target
    image = packed_apply(remain, screen, factor, size_z)
    for step in range(COARSE_ITERS):
        more = step + 1 < COARSE_ITERS
        norm, bent = totals_of(remain * remain, remain * image)
        if more:
            ahead = packed_apply(image, screen, factor, size_z)
        if step == 0:
            length = norm / bent
            search, search_image, search_ahead = remain, image, ahead
            iterate = length * search
        else:
            ratio = norm / norm_before
            length = jnp.clip(norm / (bent - ratio * norm / length), 0.0, longest)
            search = remain + ratio * search
            iterate = iterate + length * search
            if more:
                search_image = image + ratio * search_image
                search_ahead = ahead + ratio * search_ahead
        if more:
            remain = remain - length * search_image
            image = image - length * search_ahead
        norm_before = norm
    return iterate


def add_lanes(rows_ref, planes, size_y, matrix):
    half = pair_rows(rows_ref, 0, planes * size_y).reshape(planes // 4, 4, size_y // 2, LANES)
    wide = jnp.concatenate([half[:, j].reshape(-1, LANES) for j in range(4)], 1)
    return gather_lanes(wide, matrix[...]).reshape(planes // 4, size_y // 2, LANES)


def copy_level(value, matrix):
    planes, size_y, _ = value.shape
    wide = spread_lanes(value.reshape(-1, LANES), matrix[...]).reshape(planes, size_y, 4 * LANES)
    return jnp.stack([wide[:, :, j * LANES : (j + 1) * LANES] for j in range(4)], 1).reshape(
        4 * planes, size_y, LANES
    )


class Sizes:
    def __init__(self, mesh_x, mesh_y, size_x, size_y):
        self.mesh_x, self.mesh_y = mesh_x, mesh_y
        self.own_x, self.own_y = size_x // 4, size_y // 2
        self.planes, self.rows = mesh_x * self.own_x, mesh_y * self.own_y
        self.stride = self.rows + 8
        self.flat = (self.planes + 8) * self.stride + 8
        self.pad_x = 4


def level_one(place, gathered, sizes, mats, refs, first):
    mat_1, mat_2 = mats
    given, inverse, diag, step, iterate, rows_ref, level_two, local_a, local_b, two_a, two_b = refs
    size_z = LANES // 2
    factor = 0.25
    planes, rows, stride, pad = sizes.planes, sizes.rows, sizes.stride, sizes.pad_x
    own_x, own_y = sizes.own_x, sizes.own_y

    def clear(ref):
        ref[0 : pad * stride + 8] = jnp.zeros((pad * stride + 8, LANES), F32)
        ref[(pad + planes) * stride :] = jnp.zeros((pad * stride + 8, LANES), F32)

        def gap(i):
            ref[pl.ds((pad + i) * stride, 8), :] = jnp.zeros((8, LANES), F32)

        for_planes(planes, gap)

    for ref in (given, step, iterate) + ((inverse, diag) if first else ()):
        clear(ref)

    core = place[1] % 2
    per_core = sizes.mesh_x * sizes.mesh_y // 2

    def block(b):
        source, side = (gathered[0], core) if b < per_core else (gathered[1], 1 - core)
        gx = b % per_core // (sizes.mesh_y // 2)
        gy = 2 * (b % (sizes.mesh_y // 2)) + side
        tiles = []
        for i in range(source.shape[1]):
            tile = source[b % per_core, i].astype(jnp.int32).astype(F32)
            tiles += [tile[:own_y], tile[own_y:]]
        scale = scale_of(tiles[own_x])
        for i in range(own_x):
            start = (pad + gx * own_x + i) * stride + 8 + gy * own_y
            at = pl.ds(pl.multiple_of(start, 8), own_y)
            value = tiles[i] * scale
            if first:
                d = 6.0 * factor + (screen_weight * 0.125) * tiles[own_x + 2 + i]
                diag[at, :] = d
                inv = 1.0 / d
                inverse[at, :] = inv
            else:
                inv = inverse[at, :]
            given[at, :] = value
            step[at, :] = value * inv * (1.0 / centre)

    for b in range(sizes.mesh_x * sizes.mesh_y):
        block(b)

    def second(i):
        base = (pad + i) * stride + 8
        at = pl.ds(base, rows)
        here, total = neighbours(step, base, rows, stride, size_z)
        fit = (given[at, :] + factor * total) * inverse[at, :]
        iterate[at, :] = here + (keep * here + gain * (fit - here))

    for_planes(planes, second)

    def residual(i):
        base = (pad + i) * stride + 8
        at = pl.ds(base, rows)
        here, total = neighbours(iterate, base, rows, stride, size_z)
        rows_ref[pl.ds(i * rows, rows), :] = given[at, :] + factor * total - diag[at, :] * here

    for_planes(planes, residual)
    target = 0.125 * add_lanes(rows_ref, planes, rows, mat_1)

    screen_two, screen_three = level_two
    if first:

        def screens(i):
            at = pl.ds((pad + i) * stride + 8, rows)
            rows_ref[pl.ds(i * rows, rows), :] = diag[at, :] - 6.0 * factor

        for_planes(planes, screens)
        screen_two[...] = 0.125 * add_lanes(rows_ref, planes, rows, mat_1)
    planes_2, rows_2 = planes // 4, rows // 2
    screen = screen_two[...]
    level = 6.0 * factor**2 + screen
    inv = 1.0 / level
    if first:
        rows_ref[0 : planes_2 * rows_2] = screen.reshape(-1, LANES)
        screen_three[...] = 0.125 * add_lanes(rows_ref, planes_2, rows_2, mat_2)
    stride_2 = rows_2 + 8

    def at_2(i):
        return (1 + i) * stride_2 + 8

    for ref in (two_a, two_b):
        for start, count in ((0, stride_2 + 8), ((planes_2 + 1) * stride_2, stride_2 + 8)):
            ref[start : start + count] = jnp.zeros((count, LANES), F32)
        for i in range(planes_2):
            ref[at_2(i) - 8 : at_2(i)] = jnp.zeros((8, LANES), F32)

    def fit_two(ref, i):
        here, total = neighbours(ref, at_2(i), rows_2, stride_2, LANES // 4)
        return here, (target[i] + factor**2 * total) * inv[i]

    for i in range(planes_2):
        two_a[pl.ds(at_2(i), rows_2), :] = target[i] * inv[i] * (1.0 / centre)
    for i in range(planes_2):
        here, fit = fit_two(two_a, i)
        two_b[pl.ds(at_2(i), rows_2), :] = here + (keep * here + gain * (fit - here))
    for i in range(planes_2):
        here, total = neighbours(two_b, at_2(i), rows_2, stride_2, LANES // 4)
        rows_ref[i * rows_2 : (i + 1) * rows_2] = target[i] + factor**2 * total - level[i] * here
    target_3 = 0.125 * add_lanes(rows_ref, planes_2, rows_2, mat_2)
    error = conjugate_gradients(target_3, screen_three[...], factor**3, LANES // 8)
    error = copy_level(error, mat_2).reshape(-1, LANES)
    count = planes_2 * rows_2
    rows_ref[pl.ds(0, count // 2, stride=2), :] = error
    rows_ref[pl.ds(1, count // 2, stride=2), :] = error
    for i in range(planes_2):
        two_a[pl.ds(at_2(i), rows_2), :] = two_b[pl.ds(at_2(i), rows_2), :] + rows_ref[i * rows_2 : (i + 1) * rows_2]
    for i in range(planes_2):
        here, fit = fit_two(two_a, i)
        two_b[pl.ds(at_2(i), rows_2), :] = here + (fit - here) * (1.0 / centre)

    rows_ref[0:rows_2] = jnp.zeros((rows_2, LANES), F32)
    rows_ref[(planes_2 + 1) * rows_2 : (planes_2 + 2) * rows_2] = jnp.zeros((rows_2, LANES), F32)
    for i in range(planes_2):
        here, fit = fit_two(two_b, i)
        before = two_a[pl.ds(at_2(i), rows_2), :]
        rows_ref[(i + 1) * rows_2 : (i + 2) * rows_2] = here + (keep * (here - before) + gain * (fit - here))
    near_2 = own_x // 4 + 2
    start = pl.multiple_of(place[0] * (own_x // 4) * rows_2, 8)
    near = rows_ref[pl.ds(start, near_2 * rows_2), :].reshape(near_2, rows_2, LANES)
    error = copy_level(near, mat_1)
    near_x, near_y = 4 * near_2, own_y + 16
    first_plane = place[0] * own_x
    for i in range(near_x):
        base = (first_plane + i) * stride + 8
        even, odd = pl.ds(base, rows_2, stride=2), pl.ds(base + 1, rows_2, stride=2)
        iterate[even, :] = iterate[even, :] + error[i]
        iterate[odd, :] = iterate[odd, :] + error[i]
    for i in range(near_x):
        at = pl.ds(pl.multiple_of((first_plane + i) * stride + place[1] * own_y, 8), near_y)
        local_a[pl.ds(8 + i * near_y, near_y), :] = iterate[at, :]
    for ref in (local_a, local_b):
        ref[0:8] = jnp.zeros((8, LANES), F32)
        ref[8 + near_x * near_y :] = jnp.zeros((8, LANES), F32)
    ends = pl.ds(8, near_y), pl.ds(8 + (near_x - 1) * near_y, near_y)
    for at in ends:
        local_b[at, :] = jnp.zeros((near_y, LANES), F32)

    def fit_of(ref, i):
        at = pl.ds(pl.multiple_of((first_plane + i) * stride + place[1] * own_y, 8), near_y)
        here, total = neighbours(ref, 8 + i * near_y, near_y, near_y, size_z)
        return here, (given[at, :] + factor * total) * inverse[at, :]

    for i in range(1, near_x - 1):
        here, fit = fit_of(local_a, i)
        local_b[pl.ds(8 + i * near_y, near_y), :] = here + (fit - here) * (1.0 / centre)
    for i in range(2, near_x - 2):
        here, fit = fit_of(local_b, i)
        at = pl.ds(8 + i * near_y, near_y)
        local_a[at, :] = here + (keep * (here - local_a[at, :]) + gain * (fit - here))


def add_correction(start, iterate, local, sizes, mat_0, plane):
    ends = pl.ds(0, 8), pl.ds(start.shape[0] - 8, 8)
    for at in ends:
        iterate[at, :] = start[at, :]
    near_y = sizes.own_y + 16
    half_y = plane // 2
    planes = sizes.own_x + 4
    value = jnp.concatenate(
        [local[pl.ds(8 + (2 + i) * near_y + 4, half_y), :] for i in range(planes)], 0
    )
    wide = spread_lanes(value, mat_0[...])
    for i in range(planes):
        for j in range(4):
            error = wide[i * half_y : (i + 1) * half_y, (j // 2) * LANES : (j // 2 + 1) * LANES]
            for side in (0, 1):
                at = pl.ds(8 + (4 * i + j) * plane + side, half_y, stride=2)
                iterate[at, :] = start[at, :] + error


def middle_kernel(sizes, place, near, far, start, field, scaled, count_x, mat_0, mat_1, mat_2, *rest):
    iterate, packet, inverse, diag, screen_two, screen_three = rest[:6]
    given, step, coarse, rows_ref, local_a, local_b, two_a, two_b, other, fine_rows = rest[6:]
    wide, size_y = count_x.shape[:2]
    size_x = wide - 2 * HALO
    plane = size_y + 2 * HALO
    refs = (given, inverse, diag, step, coarse, rows_ref, (screen_two, screen_three), local_a, local_b, two_a, two_b)
    level_one(place, (near, far), sizes, (mat_1, mat_2), refs, True)
    add_correction(start, iterate, local_a, sizes, mat_0, plane)
    finest_step_one(iterate, other, field, scaled, 6, wide, plane)
    finest_step_two(other, iterate, field, scaled, 5, wide, plane)
    finest_step_one(iterate, other, field, scaled, 4, wide, plane)
    finest_step_two(other, iterate, field, scaled, 3, wide, plane)

    def write(i, here, value):
        fine_rows[pl.ds(i * size_y, size_y), :] = value

    finest_residual(iterate, field, count_x, size_x, size_y, write)
    even, odd = restrict_finest(fine_rows, size_x, size_y, mat_0)
    send_coarse(packet, 0.125 * gather_lanes(jnp.concatenate([even, odd], 1), mat_0[...]), None, size_y // 2)


def last_kernel(sizes, place, near, far, start, field, scaled, count_x, inverse, diag, screen_two, screen_three, *rest):
    mat_0, mat_1, mat_2, solution_far, residual_far = rest[:5]
    given, step, coarse, rows_ref, local_a, local_b, two_a, two_b, iterate, other = rest[5:15]
    solution_out, residual_out, left = rest[15:]
    wide, size_y = count_x.shape[:2]
    size_x = wide - 2 * HALO
    plane = size_y + 2 * HALO
    refs = (given, inverse, diag, step, coarse, rows_ref, (screen_two, screen_three), local_a, local_b, two_a, two_b)
    level_one(place, (near, far), sizes, (mat_1, mat_2), refs, False)
    add_correction(start, iterate, local_a, sizes, mat_0, plane)
    finest_step_one(iterate, other, field, scaled, 2, wide, plane)
    finest_step_two(other, iterate, field, scaled, 1, wide, plane)

    def send(source, target, which):
        copy = pltpu.make_async_copy(source, target, left.at[which])
        copy.start()
        return copy

    for i in range(size_x):
        solution_out[i] = iterate[pl.ds(8 + (HALO + i) * plane + HALO, size_y), :]
    copies = [send(solution_out, solution_far, 0)]

    def write(i, here, value):
        residual_out[i] = value
        if (2 * i + 2) % size_x == 0:
            half = pl.ds(i + 1 - size_x // 2, size_x // 2)
            copies.append(send(residual_out.at[half], residual_far.at[half], 1 + (i + 1) * 2 // size_x))

    finest_residual(iterate, field, count_x, size_x, size_y, write)
    for copy in copies:
        copy.wait()


def exchange(first, second, axis):
    count = lax.axis_size(axis)

    def pairs(start):
        found = []
        for i in range(start, count - 1, 2):
            found += [(i, i + 1), (i + 1, i)]
        return found

    return lax.ppermute(first, axis, pairs(0)), lax.ppermute(second, axis, pairs(1))


def gather(packet):
    near = lax.all_to_all(packet, ("gx", "gy_chip"), 0, 0, tiled=True)
    return near, lax.ppermute(near, "gy_core", [(0, 1), (1, 0)])


def per_device(point_counts, face_counts):
    size_x, size_y, size_z = point_counts.shape
    assert size_z == LANES and size_x == 16 and size_y == 16
    mesh_x = lax.axis_size("gx")
    mesh_y = lax.axis_size("gy_chip") * lax.axis_size("gy_core")
    gx = lax.axis_index("gx")
    gy = lax.axis_index("gy_chip") * 2 + lax.axis_index("gy_core")
    place = jnp.stack([gx, gy]).astype(jnp.int32)
    wide, plane = size_x + 2 * HALO, size_y + 2 * HALO
    flat = 16 + wide * plane
    sizes = Sizes(mesh_x, mesh_y, size_x, size_y)
    copies = mesh_x * mesh_y // 2
    mats = [transfer_matrix(level) for level in range(3)]
    params = pltpu.CompilerParams(vmem_limit_bytes=(24 if sizes.flat < 4096 else 56) * 2**20)

    def call(kernel, outs, scratch, *args, copies=0, far_out=False, cost=None):
        return pl.pallas_call(
            kernel,
            out_shape=[jax.ShapeDtypeStruct(shape, dtype) for shape, dtype in outs],
            in_specs=[SMEM] + [VMEM] * (len(args) - 1),
            out_specs=[FAR if far_out else VMEM] * len(outs),
            scratch_shapes=[pltpu.VMEM(shape, dtype) for shape, dtype in scratch]
            + ([pltpu.SemaphoreType.DMA((copies,))] if copies else []),
            compiler_params=params,
            cost_estimate=cost,
        )(*args)

    cells = (size_x, size_y, LANES)
    packet = (2 * HALO + 2, size_y, LANES)
    first, second, part, count, edge = call(
        cells_kernel,
        [(packet, BF16), (packet, BF16), (cells, BF16), (cells, BF16), ((2, size_y, LANES), BF16)],
        [],
        place,
        pack_cell(face_counts, point_counts),
    )
    first, second = exchange(first, second, "gx")
    packet = (wide + wide // size_y, size_y, LANES)
    strip = (wide, size_y, LANES)
    first, second, part_x, count_x, edge_x = call(
        wide_kernel,
        [(packet, BF16), (packet, BF16), (strip, BF16), (strip, BF16), ((wide, LANES), F32)],
        [],
        place,
        first,
        second,
        part,
        count,
        edge,
    )
    first, second = exchange(first, second, ("gy_chip", "gy_core"))
    own = sizes.own_x
    received = (first, second, part_x, count_x, edge_x)
    flat_f32 = ((flat, LANES), F32)
    (packet,) = call(
        start_kernel,
        [((copies, own + 1, 2 * sizes.own_y, LANES), jnp.int16)],
        [flat_f32] * 4 + [((size_x * size_y, LANES), F32)],
        place,
        *received,
        mats[0],
    )
    near, far = gather(packet)
    iterate, field, scaled = call(
        surroundings_kernel,
        [flat_f32] * 3,
        [flat_f32],
        place,
        near,
        *received,
        cost=pl.CostEstimate(flops=1 << 22, bytes_accessed=4 << 20, transcendentals=0),
    )
    level = (sizes.flat, LANES)
    flat_two = ((sizes.planes // 4 + 2) * (sizes.rows // 2 + 8) + 8, LANES)
    around = (16 + (own + 8) * (sizes.own_y + 16), LANES)
    scratch = [
        (level, F32),
        (level, F32),
        (level, F32),
        ((sizes.planes * sizes.rows, LANES), F32),
        (around, F32),
        (around, F32),
        (flat_two, F32),
        (flat_two, F32),
        ((flat, LANES), F32),
    ]
    level_two = (sizes.planes // 4, sizes.rows // 2, LANES)
    level_three = (sizes.planes // 16, sizes.rows // 4, LANES)
    iterate, packet, inverse, diag, screen_two, screen_three = call(
        lambda *refs: middle_kernel(sizes, *refs),
        [
            ((flat, LANES), F32),
            ((copies, own // 2 + 1, 2 * sizes.own_y, LANES), jnp.int16),
            (level, F32),
            (level, F32),
            (level_two, F32),
            (level_three, F32),
        ],
        scratch + [((size_x * size_y, LANES), F32)],
        place,
        near,
        far,
        iterate,
        field,
        scaled,
        count_x,
        *mats,
    )
    solution_own, residual_own = call(
        lambda *refs: last_kernel(sizes, *refs),
        [(cells, F32), (cells, F32)],
        scratch + [((flat, LANES), F32), (cells, F32), (cells, F32)],
        place,
        *gather(packet),
        iterate,
        field,
        scaled,
        count_x,
        inverse,
        diag,
        screen_two,
        screen_three,
        *mats,
        copies=4,
        far_out=True,
    )
    return solution_own, residual_own


def solution(mesh):
    mesh_x, mesh_y = mesh.shape["gx"], mesh.shape["gy"]
    split = Mesh(mesh.devices.reshape(mesh_x, mesh_y // 2, 2), ("gx", "gy_chip", "gy_core"))
    rows = ("gy_chip", "gy_core")

    def run(point_counts, face_counts):
        return jax.shard_map(
            per_device,
            mesh=split,
            in_specs=(P("gx", rows, None), P(None, "gx", rows, None)),
            out_specs=(P("gx", rows, None), P("gx", rows, None)),
            check_vma=False,
        )(point_counts, face_counts)

    return run
```

```python
import numpy as np
import jax
import jax.numpy as jnp
from jax import lax
from jax.experimental import pallas as pl
from jax.experimental.pallas import tpu as pltpu
from jax.sharding import Mesh, PartitionSpec as P

F32 = jnp.float32
BF16 = jnp.bfloat16
LANES = 128
HALO = 8
COARSE_ITERS = 6

screen_weight = 0.25
flux_scale = 0.125
low_edge = 0.3
high_edge = 2.0
centre = 0.5 * (high_edge + low_edge)
radius = 0.5 * (high_edge - low_edge)
ratio = centre / radius
mom_first = 1.0 / ratio
mom_second = 1.0 / (2.0 * ratio - mom_first)
keep = mom_second * mom_first
gain = 2.0 * mom_second / radius

VMEM = pl.BlockSpec(memory_space=pltpu.VMEM)
SMEM = pl.BlockSpec(memory_space=pltpu.SMEM)
FAR = pl.BlockSpec(memory_space=pltpu.HBM)


def transfer_matrix(level):
    pack, size_z = 1 << level, LANES >> level
    planes = 2 if level == 0 else 4
    out = np.zeros((planes * LANES, LANES), np.float32)
    for j in range(planes):
        for q in range(pack):
            coarse = j if level == 0 else (j * pack + q) // 2
            for z in range(size_z):
                out[j * LANES + q * size_z + z, coarse * (size_z // 2) + z // 2] = 1.0
    return jnp.asarray(out, BF16)


def in_parts(value):
    high = value.astype(BF16)
    rest = value - high.astype(F32)
    middle = rest.astype(BF16)
    return jnp.concatenate([high, middle, (rest - middle.astype(F32)).astype(BF16)], 0)


def add_parts(value, rows):
    return value[:rows] + (value[rows : 2 * rows] + value[2 * rows :])


def gather_lanes(value, matrix):
    return add_parts(jnp.dot(in_parts(value), matrix, preferred_element_type=F32), value.shape[0])


def spread_lanes(value, matrix):
    dims = (((1,), (1,)), ((), ()))
    return add_parts(lax.dot_general(in_parts(value), matrix, dims, preferred_element_type=F32), value.shape[0])


def lane_index():
    return lax.broadcasted_iota(jnp.int32, (1, LANES), 1)


def z_sum(value, size_z):
    lane = lane_index() & (size_z - 1)
    inner_low = (lane != 0).astype(F32)
    inner_high = (lane != size_z - 1).astype(F32)
    return pltpu.roll(value, 1, 1) * inner_low + pltpu.roll(value, LANES - 1, 1) * inner_high


def x_sum(before, here, after, size_z):
    if size_z == LANES:
        return before + after
    lane = lax.broadcasted_iota(jnp.int32, here.shape, 1)
    if 2 * size_z == LANES:
        return pltpu.roll(here + jnp.where(lane < size_z, after, before), size_z, 1)
    up = pltpu.roll(jnp.where(lane < size_z, after, here), LANES - size_z, 1)
    down = pltpu.roll(jnp.where(lane >= LANES - size_z, before, here), size_z, 1)
    return up + down


def neighbours(ref, base, rows, stride, size_z):
    here = ref[pl.ds(base, rows), :]
    total = x_sum(ref[pl.ds(base - stride, rows), :], here, ref[pl.ds(base + stride, rows), :], size_z)
    total = total + (ref[pl.ds(base - 1, rows), :] + ref[pl.ds(base + 1, rows), :])
    return here, total + z_sum(here, size_z)


def for_planes(count, body, limit=64):
    if count <= limit:
        for i in range(count):
            body(i)
    else:
        step = 8

        def block(k, carry):
            for j in range(step):
                body(k * step + j)
            return carry

        lax.fori_loop(0, count // step, block, 0)


def pair_rows(ref, start, rows):
    return ref[pl.ds(start, rows // 2, stride=2), :] + ref[pl.ds(start + 1, rows // 2, stride=2), :]


def pack_cell(faces, points):
    word = points << 18
    for c in range(3):
        word = word + ((faces[c] + 32) << (6 * c))
    return word


def cells_kernel(place, words, first, second, part, count, edge):
    size_x, size_y = words.shape[:2]
    lane = lax.broadcasted_iota(jnp.int32, (size_y, LANES), 1)
    row = lax.broadcasted_iota(jnp.int32, (size_y, LANES), 0)
    last_x = None
    for i in range(size_x):
        word = words[i]
        along_x, along_y, along_z = [((word >> (6 * c)) & 63) - 32 for c in range(3)]
        total = jnp.where(row != 0, pltpu.roll(along_y, 1, 0), 0) - along_y
        total = total + (jnp.where(lane != 0, pltpu.roll(along_z, 1, 1), 0) - along_z) - along_x
        if last_x is not None:
            total = total + last_x
        last_x = along_x
        part[i] = total.astype(F32).astype(BF16)
        count[i] = ((word >> 18) + 1).astype(F32).astype(BF16)
    edge[0] = last_x.astype(F32).astype(BF16)
    edge[1] = (((words[:, size_y - 1, :] >> 6) & 63) - 32).astype(F32).astype(BF16)

    def write(up, down):
        for target, start in ((up, size_x - HALO), (down, 0)):
            target[0:HALO] = part[start : start + HALO]
            target[HALO : 2 * HALO] = count[start : start + HALO]
            target[2 * HALO : 2 * HALO + 2] = edge[...]

    odd = 1 - place[0] % 2

    @pl.when(odd == 0)
    def _():
        write(first, second)

    @pl.when(odd == 1)
    def _():
        write(second, first)


def wide_kernel(place, got_first, got_second, part, count, edge, first, second, part_x, count_x, edge_x):
    size_x, size_y = part.shape[:2]
    wide = size_x + 2 * HALO

    def fill(below, above):
        part_x[0:HALO] = below[0:HALO]
        part_x[HALO + size_x :] = above[0:HALO]
        count_x[0:HALO] = below[HALO : 2 * HALO]
        count_x[HALO + size_x :] = above[HALO : 2 * HALO]
        part_x[HALO : HALO + size_x] = part[...]
        count_x[HALO : HALO + size_x] = count[...]
        part_x[HALO] = (part[0].astype(F32) + below[2 * HALO].astype(F32)).astype(BF16)
        part_x[HALO + size_x] = (above[0].astype(F32) + edge[0].astype(F32)).astype(BF16)
        edge_x[0:HALO] = below[2 * HALO + 1].astype(F32)[size_x - HALO :]
        edge_x[HALO : HALO + size_x] = edge[1].astype(F32)
        edge_x[HALO + size_x :] = above[2 * HALO + 1].astype(F32)[:HALO]

    odd = 1 - place[0] % 2

    @pl.when(odd == 0)
    def _():
        fill(got_second, got_first)

    @pl.when(odd == 1)
    def _():
        fill(got_first, got_second)

    def write(up, down):
        for i in range(wide):
            cells = part_x[i].astype(F32)
            points = count_x[i].astype(F32)
            up[i] = jnp.concatenate([cells[size_y - HALO :], points[size_y - HALO :]], 0).astype(BF16)
            down[i] = jnp.concatenate([cells[:HALO], points[:HALO]], 0).astype(BF16)
        for target in (up, down):
            for j in range(wide // size_y):
                target[wide + j] = edge_x[j * size_y : (j + 1) * size_y].astype(BF16)

    odd_y = 1 - place[1] % 2

    @pl.when(odd_y == 0)
    def _():
        write(first, second)

    @pl.when(odd_y == 1)
    def _():
        write(second, first)


def finest_parts(margin, wide, plane):
    planes = range(HALO - margin, wide - HALO + margin)
    if margin > 4:
        return [(8 + i * plane, 2 * plane) for i in planes[::2]]
    return [(8 + i * plane + HALO - 4, plane - 2 * HALO + 8) for i in planes]


def finest_step_one(source, target, field, scaled, margin, wide, plane):
    for base, rows in finest_parts(margin, wide, plane):
        at = pl.ds(base, rows)
        here, total = neighbours(source, base, rows, plane, LANES)
        fit = (field[at, :] + total) * scaled[at, :]
        target[at, :] = here + (fit - here) * (1.0 / centre)


def finest_step_two(source, old, field, scaled, margin, wide, plane):
    for base, rows in finest_parts(margin, wide, plane):
        at = pl.ds(base, rows)
        here, total = neighbours(source, base, rows, plane, LANES)
        fit = (field[at, :] + total) * scaled[at, :]
        old[at, :] = here + (keep * (here - old[at, :]) + gain * (fit - here))


def finest_step_two_from_zero(source, target, field, scaled, margin, wide, plane):
    for base, rows in finest_parts(margin, wide, plane):
        at = pl.ds(base, rows)
        here, total = neighbours(source, base, rows, plane, LANES)
        fit = (field[at, :] + total) * scaled[at, :]
        target[at, :] = here + (keep * here + gain * (fit - here))


def finest_residual(iterate, field, count, size_x, size_y, write):
    plane = size_y + 2 * HALO
    for i in range(size_x):
        base = 8 + (HALO + i) * plane + HALO
        here, total = neighbours(iterate, base, size_y, plane, LANES)
        diag = 6.0 + screen_weight * (count[HALO + i].astype(F32) - 1.0)
        write(i, here, field[pl.ds(base, size_y), :] + total - diag * here)


def restrict_finest(rows_ref, size_x, size_y, matrix):
    half = pair_rows(rows_ref, 0, size_x * size_y).reshape(size_x // 4, 4, size_y // 2, LANES)
    even = (half[:, 0] + half[:, 1]).reshape(-1, LANES)
    odd = (half[:, 2] + half[:, 3]).reshape(-1, LANES)
    return even, odd


def first_step(place, got, part_x, count_x, edge_x, iterate, field, inverse, margin):
    wide, size_y = part_x.shape[:2]
    plane = size_y + 2 * HALO
    even = place[1] % 2 == 1
    top = lax.broadcasted_iota(jnp.int32, (HALO, LANES), 0) == 0
    under_rows = [jnp.where(even, got[1][wide + j], got[0][wide + j]).astype(F32) for j in range(wide // size_y)]
    for i in range(HALO - margin, wide - HALO + margin):
        below = jnp.where(even, got[1][i], got[0][i]).astype(F32)
        above = jnp.where(even, got[0][i], got[1][i]).astype(F32)
        own = part_x[i].astype(F32)
        under = under_rows[i // size_y][i % size_y : i % size_y + 1]
        over = edge_x[i : i + 1]
        cells = jnp.concatenate(
            [
                below[:HALO],
                own[:HALO] + jnp.where(top, under, 0.0),
                own[HALO:],
                above[:HALO] + jnp.where(top, over, 0.0),
            ],
            0,
        )
        points = jnp.concatenate([below[HALO:], count_x[i].astype(F32), above[HALO:]], 0)
        given = flux_scale * cells
        inv = jnp.where(points > 0.0, 1.0 / (6.0 - screen_weight + screen_weight * points), 0.0)
        at = pl.ds(8 + i * plane, plane)
        field[at, :] = given
        inverse[at, :] = inv
        iterate[at, :] = (given * inv) * (1.0 / centre)


def start_kernel(
    place, got_first, got_second, part_x, count_x, edge_x, matrix, packet, first, second, field, inverse, rows_ref
):
    wide, size_y = part_x.shape[:2]
    size_x = wide - 2 * HALO
    plane = size_y + 2 * HALO
    first_step(place, (got_first, got_second), part_x, count_x, edge_x, first, field, inverse, 2)
    finest_step_two_from_zero(first, second, field, inverse, 1, wide, plane)

    def write(i, here, value):
        rows_ref[pl.ds(i * size_y, size_y), :] = value

    finest_residual(second, field, count_x, size_x, size_y, write)
    even, odd = restrict_finest(rows_ref, size_x, size_y, matrix)
    coarse = 0.125 * gather_lanes(jnp.concatenate([even, odd], 1), matrix[...])
    for i in range(size_x):
        rows_ref[pl.ds(i * size_y, size_y), :] = count_x[HALO + i].astype(F32) - 1.0
    even, odd = restrict_finest(rows_ref, size_x, size_y, matrix)
    points = jnp.dot(jnp.concatenate([even, odd], 1).astype(BF16), matrix[...], preferred_element_type=F32)
    send_coarse(packet, coarse, points, size_y // 2)


def surroundings_kernel(
    place, after, got_first, got_second, part_x, count_x, edge_x, iterate, field, inverse, first
):
    wide, size_y = part_x.shape[:2]
    plane = size_y + 2 * HALO
    zero = jnp.zeros((8, LANES), F32)
    for ref in (iterate, field, inverse, first):
        ref[0:8] = zero
        ref[8 + wide * plane :] = zero
    first_step(place, (got_first, got_second), part_x, count_x, edge_x, first, field, inverse, HALO)
    for base, rows in ((8, plane), (8 + (wide - 1) * plane, plane)):
        iterate[pl.ds(base, rows), :] = first[pl.ds(base, rows), :]
    finest_step_two_from_zero(first, iterate, field, inverse, HALO - 1, wide, plane)


def scale_of(code):
    return jnp.exp2(code * (1.0 / 128.0))


def send_coarse(packet, coarse, points, size_y):
    copies = packet.shape[0]
    tiles = [coarse[i : i + size_y] for i in range(0, coarse.shape[0], size_y)]
    largest = jnp.abs(tiles[0])
    for tile in tiles[1:]:
        largest = jnp.maximum(largest, jnp.abs(tile))
    largest = jnp.maximum(jnp.max(largest, 1, keepdims=True), 1e-30)
    code = jnp.ceil(128.0 * jnp.log2(largest * (1.0 / 32766.0)))
    scale = scale_of(-code)
    rows = [jnp.round(tile * scale) for tile in tiles]
    rows += [jnp.broadcast_to(code, (size_y, LANES)), jnp.zeros((size_y, LANES), F32)]
    if points is not None:
        rows += [points[i : i + size_y] for i in range(0, points.shape[0], size_y)]
    for i in range(0, len(rows), 2):
        tile = jnp.concatenate(rows[i : i + 2], 0).astype(jnp.int32).astype(jnp.int16)
        for k in range(copies):
            packet[k, i // 2] = tile


def packed_apply(value, screen, factor, size_z):
    planes, size_y, _ = value.shape
    flat = value.reshape(planes * size_y, LANES)
    empty = jnp.zeros((1, size_y, LANES), F32)
    if planes > 1:
        before = jnp.concatenate([empty, value[:-1]], 0).reshape(flat.shape)
        after = jnp.concatenate([value[1:], empty], 0).reshape(flat.shape)
    else:
        before = after = jnp.zeros_like(flat)
    row = lax.broadcasted_iota(jnp.int32, value.shape, 1)
    along_y = jnp.where(row != 0, pltpu.roll(value, 1, 1), 0.0) + jnp.where(
        row != size_y - 1, pltpu.roll(value, size_y - 1, 1), 0.0
    )
    total = x_sum(before, flat, after, size_z) + z_sum(flat, size_z)
    return (6.0 * value - (total.reshape(value.shape) + along_y)) * factor + screen * value


def totals_of(*values):
    rows = jnp.concatenate([jnp.sum(value, 0) for value in values], 0)
    sums = jnp.sum(rows, 1, keepdims=True).reshape(len(values), -1, 1)
    sums = jnp.sum(sums, 1, keepdims=True)
    return [sums[i : i + 1] for i in range(len(values))]


def conjugate_gradients(target, screen, factor, size_z):
    planes, size_y, _ = target.shape
    least = sum(2.0 - 2.0 * np.cos(np.pi / (n + 1)) for n in (planes * (LANES // size_z), size_y, size_z))
    longest = 1.001 / (factor * least)
    remain = target
    image = packed_apply(remain, screen, factor, size_z)
    for step in range(COARSE_ITERS):
        more = step + 1 < COARSE_ITERS
        norm, bent = totals_of(remain * remain, remain * image)
        if more:
            ahead = packed_apply(image, screen, factor, size_z)
        if step == 0:
            length = norm / bent
            search, search_image, search_ahead = remain, image, ahead
            iterate = length * search
        else:
            ratio = norm / norm_before
            length = jnp.clip(norm / (bent - ratio * norm / length), 0.0, longest)
            search = remain + ratio * search
            iterate = iterate + length * search
            if more:
                search_image = image + ratio * search_image
                search_ahead = ahead + ratio * search_ahead
        if more:
            remain = remain - length * search_image
            image = image - length * search_ahead
        norm_before = norm
    return iterate


def add_lanes(rows_ref, planes, size_y, matrix):
    half = pair_rows(rows_ref, 0, planes * size_y).reshape(planes // 4, 4, size_y // 2, LANES)
    wide = jnp.concatenate([half[:, j].reshape(-1, LANES) for j in range(4)], 1)
    return gather_lanes(wide, matrix[...]).reshape(planes // 4, size_y // 2, LANES)


def copy_level(value, matrix):
    planes, size_y, _ = value.shape
    wide = spread_lanes(value.reshape(-1, LANES), matrix[...]).reshape(planes, size_y, 4 * LANES)
    return jnp.stack([wide[:, :, j * LANES : (j + 1) * LANES] for j in range(4)], 1).reshape(
        4 * planes, size_y, LANES
    )


class Sizes:
    def __init__(self, mesh_x, mesh_y, size_x, size_y):
        self.mesh_x, self.mesh_y = mesh_x, mesh_y
        self.own_x, self.own_y = size_x // 4, size_y // 2
        self.planes, self.rows = mesh_x * self.own_x, mesh_y * self.own_y
        self.stride = self.rows + 8
        self.flat = (self.planes + 8) * self.stride + 8
        self.pad_x = 4


def level_one(place, gathered, sizes, mats, refs, first):
    mat_1, mat_2 = mats
    given, inverse, diag, step, iterate, rows_ref, level_two, local_a, local_b, two_a, two_b = refs
    size_z = LANES // 2
    factor = 0.25
    planes, rows, stride, pad = sizes.planes, sizes.rows, sizes.stride, sizes.pad_x
    own_x, own_y = sizes.own_x, sizes.own_y

    def clear(ref):
        ref[0 : pad * stride + 8] = jnp.zeros((pad * stride + 8, LANES), F32)
        ref[(pad + planes) * stride :] = jnp.zeros((pad * stride + 8, LANES), F32)

        def gap(i):
            ref[pl.ds((pad + i) * stride, 8), :] = jnp.zeros((8, LANES), F32)

        for_planes(planes, gap)

    for ref in (given, step, iterate) + ((inverse, diag) if first else ()):
        clear(ref)

    core = place[1] % 2
    per_core = sizes.mesh_x * sizes.mesh_y // 2

    def block(b):
        source, side = (gathered[0], core) if b < per_core else (gathered[1], 1 - core)
        gx = b % per_core // (sizes.mesh_y // 2)
        gy = 2 * (b % (sizes.mesh_y // 2)) + side
        tiles = []
        for i in range(source.shape[1]):
            tile = source[b % per_core, i].astype(jnp.int32).astype(F32)
            tiles += [tile[:own_y], tile[own_y:]]
        scale = scale_of(tiles[own_x])
        for i in range(own_x):
            start = (pad + gx * own_x + i) * stride + 8 + gy * own_y
            at = pl.ds(pl.multiple_of(start, 8), own_y)
            value = tiles[i] * scale
            if first:
                d = 6.0 * factor + (screen_weight * 0.125) * tiles[own_x + 2 + i]
                diag[at, :] = d
                inv = 1.0 / d
                inverse[at, :] = inv
            else:
                inv = inverse[at, :]
            given[at, :] = value
            step[at, :] = value * inv * (1.0 / centre)

    for b in range(sizes.mesh_x * sizes.mesh_y):
        block(b)

    def second(i):
        base = (pad + i) * stride + 8
        at = pl.ds(base, rows)
        here, total = neighbours(step, base, rows, stride, size_z)
        fit = (given[at, :] + factor * total) * inverse[at, :]
        iterate[at, :] = here + (keep * here + gain * (fit - here))

    for_planes(planes, second)

    def residual(i):
        base = (pad + i) * stride + 8
        at = pl.ds(base, rows)
        here, total = neighbours(iterate, base, rows, stride, size_z)
        rows_ref[pl.ds(i * rows, rows), :] = given[at, :] + factor * total - diag[at, :] * here

    for_planes(planes, residual)
    target = 0.125 * add_lanes(rows_ref, planes, rows, mat_1)

    screen_two, screen_three = level_two
    if first:

        def screens(i):
            at = pl.ds((pad + i) * stride + 8, rows)
            rows_ref[pl.ds(i * rows, rows), :] = diag[at, :] - 6.0 * factor

        for_planes(planes, screens)
        screen_two[...] = 0.125 * add_lanes(rows_ref, planes, rows, mat_1)
    planes_2, rows_2 = planes // 4, rows // 2
    screen = screen_two[...]
    level = 6.0 * factor**2 + screen
    inv = 1.0 / level
    if first:
        rows_ref[0 : planes_2 * rows_2] = screen.reshape(-1, LANES)
        screen_three[...] = 0.125 * add_lanes(rows_ref, planes_2, rows_2, mat_2)
    stride_2 = rows_2 + 8

    def at_2(i):
        return (1 + i) * stride_2 + 8

    for ref in (two_a, two_b):
        for start, count in ((0, stride_2 + 8), ((planes_2 + 1) * stride_2, stride_2 + 8)):
            ref[start : start + count] = jnp.zeros((count, LANES), F32)
        for i in range(planes_2):
            ref[at_2(i) - 8 : at_2(i)] = jnp.zeros((8, LANES), F32)

    def fit_two(ref, i):
        here, total = neighbours(ref, at_2(i), rows_2, stride_2, LANES // 4)
        return here, (target[i] + factor**2 * total) * inv[i]

    for i in range(planes_2):
        two_a[pl.ds(at_2(i), rows_2), :] = target[i] * inv[i] * (1.0 / centre)
    for i in range(planes_2):
        here, fit = fit_two(two_a, i)
        two_b[pl.ds(at_2(i), rows_2), :] = here + (keep * here + gain * (fit - here))
    for i in range(planes_2):
        here, total = neighbours(two_b, at_2(i), rows_2, stride_2, LANES // 4)
        rows_ref[i * rows_2 : (i + 1) * rows_2] = target[i] + factor**2 * total - level[i] * here
    target_3 = 0.125 * add_lanes(rows_ref, planes_2, rows_2, mat_2)
    error = conjugate_gradients(target_3, screen_three[...], factor**3, LANES // 8)
    error = copy_level(error, mat_2).reshape(-1, LANES)
    count = planes_2 * rows_2
    rows_ref[pl.ds(0, count // 2, stride=2), :] = error
    rows_ref[pl.ds(1, count // 2, stride=2), :] = error
    for i in range(planes_2):
        two_a[pl.ds(at_2(i), rows_2), :] = two_b[pl.ds(at_2(i), rows_2), :] + rows_ref[i * rows_2 : (i + 1) * rows_2]
    for i in range(planes_2):
        here, fit = fit_two(two_a, i)
        two_b[pl.ds(at_2(i), rows_2), :] = here + (fit - here) * (1.0 / centre)

    rows_ref[0:rows_2] = jnp.zeros((rows_2, LANES), F32)
    rows_ref[(planes_2 + 1) * rows_2 : (planes_2 + 2) * rows_2] = jnp.zeros((rows_2, LANES), F32)
    for i in range(planes_2):
        here, fit = fit_two(two_b, i)
        before = two_a[pl.ds(at_2(i), rows_2), :]
        rows_ref[(i + 1) * rows_2 : (i + 2) * rows_2] = here + (keep * (here - before) + gain * (fit - here))
    near_2 = own_x // 4 + 2
    start = pl.multiple_of(place[0] * (own_x // 4) * rows_2, 8)
    near = rows_ref[pl.ds(start, near_2 * rows_2), :].reshape(near_2, rows_2, LANES)
    error = copy_level(near, mat_1)
    near_x, near_y = 4 * near_2, own_y + 16
    first_plane = place[0] * own_x
    for i in range(near_x):
        base = (first_plane + i) * stride + 8
        even, odd = pl.ds(base, rows_2, stride=2), pl.ds(base + 1, rows_2, stride=2)
        iterate[even, :] = iterate[even, :] + error[i]
        iterate[odd, :] = iterate[odd, :] + error[i]
    for i in range(near_x):
        at = pl.ds(pl.multiple_of((first_plane + i) * stride + place[1] * own_y, 8), near_y)
        local_a[pl.ds(8 + i * near_y, near_y), :] = iterate[at, :]
    for ref in (local_a, local_b):
        ref[0:8] = jnp.zeros((8, LANES), F32)
        ref[8 + near_x * near_y :] = jnp.zeros((8, LANES), F32)
    ends = pl.ds(8, near_y), pl.ds(8 + (near_x - 1) * near_y, near_y)
    for at in ends:
        local_b[at, :] = jnp.zeros((near_y, LANES), F32)

    def fit_of(ref, i):
        at = pl.ds(pl.multiple_of((first_plane + i) * stride + place[1] * own_y, 8), near_y)
        here, total = neighbours(ref, 8 + i * near_y, near_y, near_y, size_z)
        return here, (given[at, :] + factor * total) * inverse[at, :]

    for i in range(1, near_x - 1):
        here, fit = fit_of(local_a, i)
        local_b[pl.ds(8 + i * near_y, near_y), :] = here + (fit - here) * (1.0 / centre)
    for i in range(2, near_x - 2):
        here, fit = fit_of(local_b, i)
        at = pl.ds(8 + i * near_y, near_y)
        local_a[at, :] = here + (keep * (here - local_a[at, :]) + gain * (fit - here))


def add_correction(start, iterate, local, sizes, mat_0, plane):
    ends = pl.ds(0, 8), pl.ds(start.shape[0] - 8, 8)
    for at in ends:
        iterate[at, :] = start[at, :]
    near_y = sizes.own_y + 16
    half_y = plane // 2
    planes = sizes.own_x + 4
    value = jnp.concatenate(
        [local[pl.ds(8 + (2 + i) * near_y + 4, half_y), :] for i in range(planes)], 0
    )
    wide = spread_lanes(value, mat_0[...])
    for i in range(planes):
        for j in range(4):
            error = wide[i * half_y : (i + 1) * half_y, (j // 2) * LANES : (j // 2 + 1) * LANES]
            for side in (0, 1):
                at = pl.ds(8 + (4 * i + j) * plane + side, half_y, stride=2)
                iterate[at, :] = start[at, :] + error


def middle_kernel(sizes, place, near, far, start, field, scaled, count_x, mat_0, mat_1, mat_2, *rest):
    iterate, packet, inverse, diag, screen_two, screen_three = rest[:6]
    given, step, coarse, rows_ref, local_a, local_b, two_a, two_b, other, fine_rows = rest[6:]
    wide, size_y = count_x.shape[:2]
    size_x = wide - 2 * HALO
    plane = size_y + 2 * HALO
    refs = (given, inverse, diag, step, coarse, rows_ref, (screen_two, screen_three), local_a, local_b, two_a, two_b)
    level_one(place, (near, far), sizes, (mat_1, mat_2), refs, True)
    add_correction(start, iterate, local_a, sizes, mat_0, plane)
    finest_step_one(iterate, other, field, scaled, 6, wide, plane)
    finest_step_two(other, iterate, field, scaled, 5, wide, plane)
    finest_step_one(iterate, other, field, scaled, 4, wide, plane)
    finest_step_two(other, iterate, field, scaled, 3, wide, plane)

    def write(i, here, value):
        fine_rows[pl.ds(i * size_y, size_y), :] = value

    finest_residual(iterate, field, count_x, size_x, size_y, write)
    even, odd = restrict_finest(fine_rows, size_x, size_y, mat_0)
    send_coarse(packet, 0.125 * gather_lanes(jnp.concatenate([even, odd], 1), mat_0[...]), None, size_y // 2)


def last_kernel(sizes, place, near, far, start, field, scaled, count_x, inverse, diag, screen_two, screen_three, *rest):
    mat_0, mat_1, mat_2, solution_far, residual_far = rest[:5]
    given, step, coarse, rows_ref, local_a, local_b, two_a, two_b, iterate, other = rest[5:15]
    solution_out, residual_out, left = rest[15:]
    wide, size_y = count_x.shape[:2]
    size_x = wide - 2 * HALO
    plane = size_y + 2 * HALO
    refs = (given, inverse, diag, step, coarse, rows_ref, (screen_two, screen_three), local_a, local_b, two_a, two_b)
    level_one(place, (near, far), sizes, (mat_1, mat_2), refs, False)
    add_correction(start, iterate, local_a, sizes, mat_0, plane)
    finest_step_one(iterate, other, field, scaled, 2, wide, plane)
    finest_step_two(other, iterate, field, scaled, 1, wide, plane)

    def send(source, target, which):
        copy = pltpu.make_async_copy(source, target, left.at[which])
        copy.start()
        return copy

    for i in range(size_x):
        solution_out[i] = iterate[pl.ds(8 + (HALO + i) * plane + HALO, size_y), :]
    copies = [send(solution_out, solution_far, 0)]

    def write(i, here, value):
        residual_out[i] = value
        if (2 * i + 2) % size_x == 0:
            half = pl.ds(i + 1 - size_x // 2, size_x // 2)
            copies.append(send(residual_out.at[half], residual_far.at[half], 1 + (i + 1) * 2 // size_x))

    finest_residual(iterate, field, count_x, size_x, size_y, write)
    for copy in copies:
        copy.wait()


def exchange(first, second, axis):
    count = lax.axis_size(axis)

    def pairs(start):
        found = []
        for i in range(start, count - 1, 2):
            found += [(i, i + 1), (i + 1, i)]
        return found

    return lax.ppermute(first, axis, pairs(1)), lax.ppermute(second, axis, pairs(0))


def gather(packet):
    near = lax.all_to_all(packet, ("gx", "gy_chip"), 0, 0, tiled=True)
    return near, lax.ppermute(near, "gy_core", [(0, 1), (1, 0)])


def per_device(point_counts, face_counts):
    size_x, size_y, size_z = point_counts.shape
    assert size_z == LANES and size_x == 16 and size_y == 16
    mesh_x = lax.axis_size("gx")
    mesh_y = lax.axis_size("gy_chip") * lax.axis_size("gy_core")
    gx = lax.axis_index("gx")
    gy = lax.axis_index("gy_chip") * 2 + lax.axis_index("gy_core")
    place = jnp.stack([gx, gy]).astype(jnp.int32)
    wide, plane = size_x + 2 * HALO, size_y + 2 * HALO
    flat = 16 + wide * plane
    sizes = Sizes(mesh_x, mesh_y, size_x, size_y)
    copies = mesh_x * mesh_y // 2
    mats = [transfer_matrix(level) for level in range(3)]
    params = pltpu.CompilerParams(vmem_limit_bytes=(24 if sizes.flat < 4096 else 56) * 2**20)

    def call(kernel, outs, scratch, *args, copies=0, far_out=False, cost=None):
        return pl.pallas_call(
            kernel,
            out_shape=[jax.ShapeDtypeStruct(shape, dtype) for shape, dtype in outs],
            in_specs=[SMEM] + [VMEM] * (len(args) - 1),
            out_specs=[FAR if far_out else VMEM] * len(outs),
            scratch_shapes=[pltpu.VMEM(shape, dtype) for shape, dtype in scratch]
            + ([pltpu.SemaphoreType.DMA((copies,))] if copies else []),
            compiler_params=params,
            cost_estimate=cost,
        )(*args)

    cells = (size_x, size_y, LANES)
    packet = (2 * HALO + 2, size_y, LANES)
    first, second, part, count, edge = call(
        cells_kernel,
        [(packet, BF16), (packet, BF16), (cells, BF16), (cells, BF16), ((2, size_y, LANES), BF16)],
        [],
        place,
        pack_cell(face_counts, point_counts),
    )
    first, second = exchange(first, second, "gx")
    packet = (wide + wide // size_y, size_y, LANES)
    strip = (wide, size_y, LANES)
    first, second, part_x, count_x, edge_x = call(
        wide_kernel,
        [(packet, BF16), (packet, BF16), (strip, BF16), (strip, BF16), ((wide, LANES), F32)],
        [],
        place,
        first,
        second,
        part,
        count,
        edge,
    )
    first, second = exchange(first, second, ("gy_chip", "gy_core"))
    own = sizes.own_x
    received = (first, second, part_x, count_x, edge_x)
    flat_f32 = ((flat, LANES), F32)
    (packet,) = call(
        start_kernel,
        [((copies, own + 1, 2 * sizes.own_y, LANES), jnp.int16)],
        [flat_f32] * 4 + [((size_x * size_y, LANES), F32)],
        place,
        *received,
        mats[0],
    )
    near, far = gather(packet)
    iterate, field, scaled = call(
        surroundings_kernel,
        [flat_f32] * 3,
        [flat_f32],
        place,
        near,
        *received,
        cost=pl.CostEstimate(flops=1 << 22, bytes_accessed=4 << 20, transcendentals=0),
    )
    level = (sizes.flat, LANES)
    flat_two = ((sizes.planes // 4 + 2) * (sizes.rows // 2 + 8) + 8, LANES)
    around = (16 + (own + 8) * (sizes.own_y + 16), LANES)
    scratch = [
        (level, F32),
        (level, F32),
        (level, F32),
        ((sizes.planes * sizes.rows, LANES), F32),
        (around, F32),
        (around, F32),
        (flat_two, F32),
        (flat_two, F32),
        ((flat, LANES), F32),
    ]
    level_two = (sizes.planes // 4, sizes.rows // 2, LANES)
    level_three = (sizes.planes // 16, sizes.rows // 4, LANES)
    iterate, packet, inverse, diag, screen_two, screen_three = call(
        lambda *refs: middle_kernel(sizes, *refs),
        [
            ((flat, LANES), F32),
            ((copies, own // 2 + 1, 2 * sizes.own_y, LANES), jnp.int16),
            (level, F32),
            (level, F32),
            (level_two, F32),
            (level_three, F32),
        ],
        scratch + [((size_x * size_y, LANES), F32)],
        place,
        near,
        far,
        iterate,
        field,
        scaled,
        count_x,
        *mats,
    )
    solution_own, residual_own = call(
        lambda *refs: last_kernel(sizes, *refs),
        [(cells, F32), (cells, F32)],
        scratch + [((flat, LANES), F32), (cells, F32), (cells, F32)],
        place,
        *gather(packet),
        iterate,
        field,
        scaled,
        count_x,
        inverse,
        diag,
        screen_two,
        screen_three,
        *mats,
        copies=4,
        far_out=True,
    )
    return solution_own, residual_own


def solution(mesh):
    mesh_x, mesh_y = mesh.shape["gx"], mesh.shape["gy"]
    split = Mesh(mesh.devices.reshape(mesh_x, mesh_y // 2, 2), ("gx", "gy_chip", "gy_core"))
    rows = ("gy_chip", "gy_core")

    def run(point_counts, face_counts):
        return jax.shard_map(
            per_device,
            mesh=split,
            in_specs=(P("gx", rows, None), P(None, "gx", rows, None)),
            out_specs=(P("gx", rows, None), P("gx", rows, None)),
            check_vma=False,
        )(point_counts, face_counts)

    return run
```

```python
import numpy as np
import jax
import jax.numpy as jnp
from jax import lax
from jax.experimental import pallas as pl
from jax.experimental.pallas import tpu as pltpu
from jax.sharding import Mesh, PartitionSpec as P

F32 = jnp.float32
BF16 = jnp.bfloat16
LANES = 128
HALO = 8
COARSE_ITERS = 6

screen_weight = 0.25
flux_scale = 0.125
low_edge = 0.3
high_edge = 2.0
centre = 0.5 * (high_edge + low_edge)
radius = 0.5 * (high_edge - low_edge)
ratio = centre / radius
mom_first = 1.0 / ratio
mom_second = 1.0 / (2.0 * ratio - mom_first)
keep = mom_second * mom_first
gain = 2.0 * mom_second / radius

VMEM = pl.BlockSpec(memory_space=pltpu.VMEM)
SMEM = pl.BlockSpec(memory_space=pltpu.SMEM)
FAR = pl.BlockSpec(memory_space=pltpu.HBM)


def transfer_matrix(level):
    pack, size_z = 1 << level, LANES >> level
    planes = 2 if level == 0 else 4
    out = np.zeros((planes * LANES, LANES), np.float32)
    for j in range(planes):
        for q in range(pack):
            coarse = j if level == 0 else (j * pack + q) // 2
            for z in range(size_z):
                out[j * LANES + q * size_z + z, coarse * (size_z // 2) + z // 2] = 1.0
    return jnp.asarray(out, BF16)


def in_parts(value):
    high = value.astype(BF16)
    rest = value - high.astype(F32)
    middle = rest.astype(BF16)
    return jnp.concatenate([high, middle, (rest - middle.astype(F32)).astype(BF16)], 0)


def add_parts(value, rows):
    return value[:rows] + (value[rows : 2 * rows] + value[2 * rows :])


def gather_lanes(value, matrix):
    return add_parts(jnp.dot(in_parts(value), matrix, preferred_element_type=F32), value.shape[0])


def spread_lanes(value, matrix):
    dims = (((1,), (1,)), ((), ()))
    return add_parts(lax.dot_general(in_parts(value), matrix, dims, preferred_element_type=F32), value.shape[0])


def lane_index():
    return lax.broadcasted_iota(jnp.int32, (1, LANES), 1)


def z_sum(value, size_z):
    lane = lane_index() & (size_z - 1)
    inner_low = (lane != 0).astype(F32)
    inner_high = (lane != size_z - 1).astype(F32)
    return pltpu.roll(value, 1, 1) * inner_low + pltpu.roll(value, LANES - 1, 1) * inner_high


def x_sum(before, here, after, size_z):
    if size_z == LANES:
        return before + after
    lane = lax.broadcasted_iota(jnp.int32, here.shape, 1)
    if 2 * size_z == LANES:
        return pltpu.roll(here + jnp.where(lane < size_z, after, before), size_z, 1)
    up = pltpu.roll(jnp.where(lane < size_z, after, here), LANES - size_z, 1)
    down = pltpu.roll(jnp.where(lane >= LANES - size_z, before, here), size_z, 1)
    return up + down


def neighbours(ref, base, rows, stride, size_z):
    here = ref[pl.ds(base, rows), :]
    total = x_sum(ref[pl.ds(base - stride, rows), :], here, ref[pl.ds(base + stride, rows), :], size_z)
    total = total + (ref[pl.ds(base - 1, rows), :] + ref[pl.ds(base + 1, rows), :])
    return here, total + z_sum(here, size_z)


def for_planes(count, body, limit=64):
    if count <= limit:
        for i in range(count):
            body(i)
    else:
        step = 8

        def block(k, carry):
            for j in range(step):
                body(k * step + j)
            return carry

        lax.fori_loop(0, count // step, block, 0)


def pair_rows(ref, start, rows):
    return ref[pl.ds(start, rows // 2, stride=2), :] + ref[pl.ds(start + 1, rows // 2, stride=2), :]


def pack_cell(faces, points):
    word = points << 18
    for c in range(3):
        word = word + ((faces[c] + 32) << (6 * c))
    return word


def cells_kernel(place, words, first, second, part, count, edge):
    size_x, size_y = words.shape[:2]
    lane = lax.broadcasted_iota(jnp.int32, (size_y, LANES), 1)
    row = lax.broadcasted_iota(jnp.int32, (size_y, LANES), 0)
    last_x = None
    for i in range(size_x):
        word = words[i]
        along_x, along_y, along_z = [((word >> (6 * c)) & 63) - 32 for c in range(3)]
        total = jnp.where(row != 0, pltpu.roll(along_y, 1, 0), 0) - along_y
        total = total + (jnp.where(lane != 0, pltpu.roll(along_z, 1, 1), 0) - along_z) - along_x
        if last_x is not None:
            total = total + last_x
        last_x = along_x
        part[i] = total.astype(F32).astype(BF16)
        count[i] = ((word >> 18) + 1).astype(F32).astype(BF16)
    edge[0] = last_x.astype(F32).astype(BF16)
    edge[1] = (((words[:, size_y - 1, :] >> 6) & 63) - 32).astype(F32).astype(BF16)

    def write(up, down):
        for target, start in ((up, size_x - HALO), (down, 0)):
            target[0:HALO] = part[start : start + HALO]
            target[HALO : 2 * HALO] = count[start : start + HALO]
            target[2 * HALO : 2 * HALO + 2] = edge[...]

    odd = 1 - place[0] % 2

    @pl.when(odd == 0)
    def _():
        write(first, second)

    @pl.when(odd == 1)
    def _():
        write(second, first)


def plane_slot(i, wide):
    size_x = wide - 2 * HALO
    if HALO <= i < HALO + size_x:
        return i - HALO, None
    distance = HALO - i if i < HALO else i - HALO - size_x + 1
    near = min(distance, HALO + 1 - distance)
    slot = size_x + near - 1 + (0 if i < HALO else HALO // 2)
    return slot, (near if near != distance else None)


def wide_kernel(place, got_first, got_second, part, count, edge, first, second, part_x, count_x, edge_x):
    size_x, size_y = part.shape[:2]
    wide = size_x + 2 * HALO

    def fill(below, above):
        part_x[0:HALO] = below[0:HALO]
        part_x[HALO + size_x :] = above[0:HALO]
        count_x[0:HALO] = below[HALO : 2 * HALO]
        count_x[HALO + size_x :] = above[HALO : 2 * HALO]
        part_x[HALO : HALO + size_x] = part[...]
        count_x[HALO : HALO + size_x] = count[...]
        part_x[HALO] = (part[0].astype(F32) + below[2 * HALO].astype(F32)).astype(BF16)
        part_x[HALO + size_x] = (above[0].astype(F32) + edge[0].astype(F32)).astype(BF16)
        edge_x[0:HALO] = below[2 * HALO + 1].astype(F32)[size_x - HALO :]
        edge_x[HALO : HALO + size_x] = edge[1].astype(F32)
        edge_x[HALO + size_x :] = above[2 * HALO + 1].astype(F32)[:HALO]

    odd = 1 - place[0] % 2

    @pl.when(odd == 0)
    def _():
        fill(got_second, got_first)

    @pl.when(odd == 1)
    def _():
        fill(got_first, got_second)

    def write(up, down):
        row = lax.broadcasted_iota(jnp.int32, (HALO, LANES), 0)
        for i in range(wide):
            slot, far = plane_slot(i, wide)
            if far is not None:
                continue
            pairs = [(part_x[i].astype(F32), count_x[i].astype(F32))]
            for k in range(wide):
                other, d = plane_slot(k, wide)
                if other == slot and d is not None:
                    pairs.append((part_x[k].astype(F32), count_x[k].astype(F32)))
                    break
            tops = [[value[size_y - HALO :] for value in pair] for pair in pairs]
            ends = [[value[:HALO] for value in pair] for pair in pairs]
            if len(pairs) == 2:
                tops[0] = [jnp.where(row >= d, a, pltpu.roll(b, d - 1, 0)) for a, b in zip(*tops)]
                ends[0] = [jnp.where(row < HALO - d, a, pltpu.roll(b, HALO + 1 - d, 0)) for a, b in zip(*ends)]
            up[slot] = jnp.concatenate(tops[0], 0).astype(BF16)
            down[slot] = jnp.concatenate(ends[0], 0).astype(BF16)
        for target in (up, down):
            for j in range(wide // size_y):
                target[wide - HALO + j] = edge_x[j * size_y : (j + 1) * size_y].astype(BF16)

    odd_y = 1 - place[1] % 2

    @pl.when(odd_y == 0)
    def _():
        write(first, second)

    @pl.when(odd_y == 1)
    def _():
        write(second, first)


def finest_parts(margin, wide, plane):
    planes = range(HALO - margin, wide - HALO + margin)
    if margin > 4:
        return [(8 + i * plane, 2 * plane) for i in planes[::2]]
    return [(8 + i * plane + HALO - 4, plane - 2 * HALO + 8) for i in planes]


def finest_step_one(source, target, field, scaled, margin, wide, plane):
    for base, rows in finest_parts(margin, wide, plane):
        at = pl.ds(base, rows)
        here, total = neighbours(source, base, rows, plane, LANES)
        fit = (field[at, :] + total) * scaled[at, :]
        target[at, :] = here + (fit - here) * (1.0 / centre)


def finest_step_two(source, old, field, scaled, margin, wide, plane):
    for base, rows in finest_parts(margin, wide, plane):
        at = pl.ds(base, rows)
        here, total = neighbours(source, base, rows, plane, LANES)
        fit = (field[at, :] + total) * scaled[at, :]
        old[at, :] = here + (keep * (here - old[at, :]) + gain * (fit - here))


def finest_step_two_from_zero(source, target, field, scaled, margin, wide, plane):
    for base, rows in finest_parts(margin, wide, plane):
        at = pl.ds(base, rows)
        here, total = neighbours(source, base, rows, plane, LANES)
        fit = (field[at, :] + total) * scaled[at, :]
        target[at, :] = here + (keep * here + gain * (fit - here))


def finest_residual(iterate, field, count, size_x, size_y, write):
    plane = size_y + 2 * HALO
    for i in range(size_x):
        base = 8 + (HALO + i) * plane + HALO
        here, total = neighbours(iterate, base, size_y, plane, LANES)
        diag = 6.0 + screen_weight * (count[HALO + i].astype(F32) - 1.0)
        write(i, here, field[pl.ds(base, size_y), :] + total - diag * here)


def restrict_finest(rows_ref, size_x, size_y, matrix):
    half = pair_rows(rows_ref, 0, size_x * size_y).reshape(size_x // 4, 4, size_y // 2, LANES)
    even = (half[:, 0] + half[:, 1]).reshape(-1, LANES)
    odd = (half[:, 2] + half[:, 3]).reshape(-1, LANES)
    return even, odd


def first_step(place, got, part_x, count_x, edge_x, iterate, field, inverse, margin):
    wide, size_y = part_x.shape[:2]
    plane = size_y + 2 * HALO
    even = place[1] % 2 == 1
    top = lax.broadcasted_iota(jnp.int32, (HALO, LANES), 0) == 0
    under_rows = [
        jnp.where(even, got[1][wide - HALO + j], got[0][wide - HALO + j]).astype(F32) for j in range(wide // size_y)
    ]
    for i in range(HALO - margin, wide - HALO + margin):
        slot, d = plane_slot(i, wide)
        below = jnp.where(even, got[1][slot], got[0][slot]).astype(F32)
        above = jnp.where(even, got[0][slot], got[1][slot]).astype(F32)
        if d is not None:
            below = jnp.concatenate([pltpu.roll(part, HALO + 1 - d, 0) for part in (below[:HALO], below[HALO:])], 0)
            above = jnp.concatenate([pltpu.roll(part, d - 1, 0) for part in (above[:HALO], above[HALO:])], 0)
        own = part_x[i].astype(F32)
        under = under_rows[i // size_y][i % size_y : i % size_y + 1]
        over = edge_x[i : i + 1]
        cells = jnp.concatenate(
            [
                below[:HALO],
                own[:HALO] + jnp.where(top, under, 0.0),
                own[HALO:],
                above[:HALO] + jnp.where(top, over, 0.0),
            ],
            0,
        )
        points = jnp.concatenate([below[HALO:], count_x[i].astype(F32), above[HALO:]], 0)
        given = flux_scale * cells
        inv = jnp.where(points > 0.0, 1.0 / (6.0 - screen_weight + screen_weight * points), 0.0)
        at = pl.ds(8 + i * plane, plane)
        field[at, :] = given
        inverse[at, :] = inv
        iterate[at, :] = (given * inv) * (1.0 / centre)


def start_kernel(
    place, got_first, got_second, part_x, count_x, edge_x, matrix, packet, first, second, field, inverse, rows_ref
):
    wide, size_y = part_x.shape[:2]
    size_x = wide - 2 * HALO
    plane = size_y + 2 * HALO
    first_step(place, (got_first, got_second), part_x, count_x, edge_x, first, field, inverse, 2)
    finest_step_two_from_zero(first, second, field, inverse, 1, wide, plane)

    def write(i, here, value):
        rows_ref[pl.ds(i * size_y, size_y), :] = value

    finest_residual(second, field, count_x, size_x, size_y, write)
    even, odd = restrict_finest(rows_ref, size_x, size_y, matrix)
    coarse = 0.125 * gather_lanes(jnp.concatenate([even, odd], 1), matrix[...])
    for i in range(size_x):
        rows_ref[pl.ds(i * size_y, size_y), :] = count_x[HALO + i].astype(F32) - 1.0
    even, odd = restrict_finest(rows_ref, size_x, size_y, matrix)
    points = jnp.dot(jnp.concatenate([even, odd], 1).astype(BF16), matrix[...], preferred_element_type=F32)
    send_coarse(packet, coarse, points, size_y // 2)


def surroundings_kernel(
    place, after, got_first, got_second, part_x, count_x, edge_x, iterate, field, inverse, first
):
    wide, size_y = part_x.shape[:2]
    plane = size_y + 2 * HALO
    zero = jnp.zeros((8, LANES), F32)
    for ref in (iterate, field, inverse, first):
        ref[0:8] = zero
        ref[8 + wide * plane :] = zero
    first_step(place, (got_first, got_second), part_x, count_x, edge_x, first, field, inverse, HALO)
    for base, rows in ((8, plane), (8 + (wide - 1) * plane, plane)):
        iterate[pl.ds(base, rows), :] = first[pl.ds(base, rows), :]
    finest_step_two_from_zero(first, iterate, field, inverse, HALO - 1, wide, plane)


def scale_of(code):
    return jnp.exp2(code * (1.0 / 128.0))


def send_coarse(packet, coarse, points, size_y):
    copies = packet.shape[0]
    tiles = [coarse[i : i + size_y] for i in range(0, coarse.shape[0], size_y)]
    largest = jnp.abs(tiles[0])
    for tile in tiles[1:]:
        largest = jnp.maximum(largest, jnp.abs(tile))
    largest = jnp.maximum(jnp.max(largest, 1, keepdims=True), 1e-30)
    code = jnp.ceil(128.0 * jnp.log2(largest * (1.0 / 32766.0)))
    scale = scale_of(-code)
    rows = [jnp.round(tile * scale) for tile in tiles]
    rows += [jnp.broadcast_to(code, (size_y, LANES)), jnp.zeros((size_y, LANES), F32)]
    if points is not None:
        rows += [points[i : i + size_y] for i in range(0, points.shape[0], size_y)]
    for i in range(0, len(rows), 2):
        tile = jnp.concatenate(rows[i : i + 2], 0).astype(jnp.int32).astype(jnp.int16)
        for k in range(copies):
            packet[k, i // 2] = tile


def packed_apply(value, screen, factor, size_z):
    planes, size_y, _ = value.shape
    flat = value.reshape(planes * size_y, LANES)
    empty = jnp.zeros((1, size_y, LANES), F32)
    if planes > 1:
        before = jnp.concatenate([empty, value[:-1]], 0).reshape(flat.shape)
        after = jnp.concatenate([value[1:], empty], 0).reshape(flat.shape)
    else:
        before = after = jnp.zeros_like(flat)
    row = lax.broadcasted_iota(jnp.int32, value.shape, 1)
    along_y = jnp.where(row != 0, pltpu.roll(value, 1, 1), 0.0) + jnp.where(
        row != size_y - 1, pltpu.roll(value, size_y - 1, 1), 0.0
    )
    total = x_sum(before, flat, after, size_z) + z_sum(flat, size_z)
    return (6.0 * value - (total.reshape(value.shape) + along_y)) * factor + screen * value


def totals_of(*values):
    rows = jnp.concatenate([jnp.sum(value, 0) for value in values], 0)
    sums = jnp.sum(rows, 1, keepdims=True).reshape(len(values), -1, 1)
    sums = jnp.sum(sums, 1, keepdims=True)
    return [sums[i : i + 1] for i in range(len(values))]


def conjugate_gradients(target, screen, factor, size_z):
    planes, size_y, _ = target.shape
    least = sum(2.0 - 2.0 * np.cos(np.pi / (n + 1)) for n in (planes * (LANES // size_z), size_y, size_z))
    longest = 1.001 / (factor * least)
    remain = target
    image = packed_apply(remain, screen, factor, size_z)
    for step in range(COARSE_ITERS):
        more = step + 1 < COARSE_ITERS
        norm, bent = totals_of(remain * remain, remain * image)
        if more:
            ahead = packed_apply(image, screen, factor, size_z)
        if step == 0:
            length = norm / bent
            search, search_image, search_ahead = remain, image, ahead
            iterate = length * search
        else:
            ratio = norm / norm_before
            length = jnp.clip(norm / (bent - ratio * norm / length), 0.0, longest)
            search = remain + ratio * search
            iterate = iterate + length * search
            if more:
                search_image = image + ratio * search_image
                search_ahead = ahead + ratio * search_ahead
        if more:
            remain = remain - length * search_image
            image = image - length * search_ahead
        norm_before = norm
    return iterate


def add_lanes(rows_ref, planes, size_y, matrix):
    half = pair_rows(rows_ref, 0, planes * size_y).reshape(planes // 4, 4, size_y // 2, LANES)
    wide = jnp.concatenate([half[:, j].reshape(-1, LANES) for j in range(4)], 1)
    return gather_lanes(wide, matrix[...]).reshape(planes // 4, size_y // 2, LANES)


def copy_level(value, matrix):
    planes, size_y, _ = value.shape
    wide = spread_lanes(value.reshape(-1, LANES), matrix[...]).reshape(planes, size_y, 4 * LANES)
    return jnp.stack([wide[:, :, j * LANES : (j + 1) * LANES] for j in range(4)], 1).reshape(
        4 * planes, size_y, LANES
    )


class Sizes:
    def __init__(self, mesh_x, mesh_y, size_x, size_y):
        self.mesh_x, self.mesh_y = mesh_x, mesh_y
        self.own_x, self.own_y = size_x // 4, size_y // 2
        self.planes, self.rows = mesh_x * self.own_x, mesh_y * self.own_y
        self.stride = self.rows + 8
        self.flat = (self.planes + 8) * self.stride + 8
        self.pad_x = 4


def level_one(place, gathered, sizes, mats, refs, first):
    mat_1, mat_2 = mats
    given, inverse, diag, step, iterate, rows_ref, level_two, local_a, local_b, two_a, two_b = refs
    size_z = LANES // 2
    factor = 0.25
    planes, rows, stride, pad = sizes.planes, sizes.rows, sizes.stride, sizes.pad_x
    own_x, own_y = sizes.own_x, sizes.own_y

    def clear(ref):
        ref[0 : pad * stride + 8] = jnp.zeros((pad * stride + 8, LANES), F32)
        ref[(pad + planes) * stride :] = jnp.zeros((pad * stride + 8, LANES), F32)

        def gap(i):
            ref[pl.ds((pad + i) * stride, 8), :] = jnp.zeros((8, LANES), F32)

        for_planes(planes, gap)

    for ref in (given, step, iterate) + ((inverse, diag) if first else ()):
        clear(ref)

    core = place[1] % 2
    per_core = sizes.mesh_x * sizes.mesh_y // 2

    def block(b):
        source, side = (gathered[0], core) if b < per_core else (gathered[1], 1 - core)
        gx = b % per_core // (sizes.mesh_y // 2)
        gy = 2 * (b % (sizes.mesh_y // 2)) + side
        tiles = []
        for i in range(source.shape[1]):
            tile = source[b % per_core, i].astype(jnp.int32).astype(F32)
            tiles += [tile[:own_y], tile[own_y:]]
        scale = scale_of(tiles[own_x])
        for i in range(own_x):
            start = (pad + gx * own_x + i) * stride + 8 + gy * own_y
            at = pl.ds(pl.multiple_of(start, 8), own_y)
            value = tiles[i] * scale
            if first:
                d = 6.0 * factor + (screen_weight * 0.125) * tiles[own_x + 2 + i]
                diag[at, :] = d
                inv = 1.0 / d
                inverse[at, :] = inv
            else:
                inv = inverse[at, :]
            given[at, :] = value
            step[at, :] = value * inv * (1.0 / centre)

    for b in range(sizes.mesh_x * sizes.mesh_y):
        block(b)

    def second(i):
        base = (pad + i) * stride + 8
        at = pl.ds(base, rows)
        here, total = neighbours(step, base, rows, stride, size_z)
        fit = (given[at, :] + factor * total) * inverse[at, :]
        iterate[at, :] = here + (keep * here + gain * (fit - here))

    for_planes(planes, second)

    def residual(i):
        base = (pad + i) * stride + 8
        at = pl.ds(base, rows)
        here, total = neighbours(iterate, base, rows, stride, size_z)
        rows_ref[pl.ds(i * rows, rows), :] = given[at, :] + factor * total - diag[at, :] * here

    for_planes(planes, residual)
    target = 0.125 * add_lanes(rows_ref, planes, rows, mat_1)

    screen_two, screen_three = level_two
    if first:

        def screens(i):
            at = pl.ds((pad + i) * stride + 8, rows)
            rows_ref[pl.ds(i * rows, rows), :] = diag[at, :] - 6.0 * factor

        for_planes(planes, screens)
        screen_two[...] = 0.125 * add_lanes(rows_ref, planes, rows, mat_1)
    planes_2, rows_2 = planes // 4, rows // 2
    screen = screen_two[...]
    level = 6.0 * factor**2 + screen
    inv = 1.0 / level
    if first:
        rows_ref[0 : planes_2 * rows_2] = screen.reshape(-1, LANES)
        screen_three[...] = 0.125 * add_lanes(rows_ref, planes_2, rows_2, mat_2)
    stride_2 = rows_2 + 8

    def at_2(i):
        return (1 + i) * stride_2 + 8

    for ref in (two_a, two_b):
        for start, count in ((0, stride_2 + 8), ((planes_2 + 1) * stride_2, stride_2 + 8)):
            ref[start : start + count] = jnp.zeros((count, LANES), F32)
        for i in range(planes_2):
            ref[at_2(i) - 8 : at_2(i)] = jnp.zeros((8, LANES), F32)

    def fit_two(ref, i):
        here, total = neighbours(ref, at_2(i), rows_2, stride_2, LANES // 4)
        return here, (target[i] + factor**2 * total) * inv[i]

    for i in range(planes_2):
        two_a[pl.ds(at_2(i), rows_2), :] = target[i] * inv[i] * (1.0 / centre)
    for i in range(planes_2):
        here, fit = fit_two(two_a, i)
        two_b[pl.ds(at_2(i), rows_2), :] = here + (keep * here + gain * (fit - here))
    for i in range(planes_2):
        here, total = neighbours(two_b, at_2(i), rows_2, stride_2, LANES // 4)
        rows_ref[i * rows_2 : (i + 1) * rows_2] = target[i] + factor**2 * total - level[i] * here
    target_3 = 0.125 * add_lanes(rows_ref, planes_2, rows_2, mat_2)
    error = conjugate_gradients(target_3, screen_three[...], factor**3, LANES // 8)
    error = copy_level(error, mat_2).reshape(-1, LANES)
    count = planes_2 * rows_2
    rows_ref[pl.ds(0, count // 2, stride=2), :] = error
    rows_ref[pl.ds(1, count // 2, stride=2), :] = error
    for i in range(planes_2):
        two_a[pl.ds(at_2(i), rows_2), :] = two_b[pl.ds(at_2(i), rows_2), :] + rows_ref[i * rows_2 : (i + 1) * rows_2]
    for i in range(planes_2):
        here, fit = fit_two(two_a, i)
        two_b[pl.ds(at_2(i), rows_2), :] = here + (fit - here) * (1.0 / centre)

    rows_ref[0:rows_2] = jnp.zeros((rows_2, LANES), F32)
    rows_ref[(planes_2 + 1) * rows_2 : (planes_2 + 2) * rows_2] = jnp.zeros((rows_2, LANES), F32)
    for i in range(planes_2):
        here, fit = fit_two(two_b, i)
        before = two_a[pl.ds(at_2(i), rows_2), :]
        rows_ref[(i + 1) * rows_2 : (i + 2) * rows_2] = here + (keep * (here - before) + gain * (fit - here))
    near_2 = own_x // 4 + 2
    start = pl.multiple_of(place[0] * (own_x // 4) * rows_2, 8)
    near = rows_ref[pl.ds(start, near_2 * rows_2), :].reshape(near_2, rows_2, LANES)
    error = copy_level(near, mat_1)
    near_x, near_y = 4 * near_2, own_y + 16
    first_plane = place[0] * own_x
    for i in range(near_x):
        base = (first_plane + i) * stride + 8
        even, odd = pl.ds(base, rows_2, stride=2), pl.ds(base + 1, rows_2, stride=2)
        iterate[even, :] = iterate[even, :] + error[i]
        iterate[odd, :] = iterate[odd, :] + error[i]
    for i in range(near_x):
        at = pl.ds(pl.multiple_of((first_plane + i) * stride + place[1] * own_y, 8), near_y)
        local_a[pl.ds(8 + i * near_y, near_y), :] = iterate[at, :]
    for ref in (local_a, local_b):
        ref[0:8] = jnp.zeros((8, LANES), F32)
        ref[8 + near_x * near_y :] = jnp.zeros((8, LANES), F32)
    ends = pl.ds(8, near_y), pl.ds(8 + (near_x - 1) * near_y, near_y)
    for at in ends:
        local_b[at, :] = jnp.zeros((near_y, LANES), F32)

    def fit_of(ref, i):
        at = pl.ds(pl.multiple_of((first_plane + i) * stride + place[1] * own_y, 8), near_y)
        here, total = neighbours(ref, 8 + i * near_y, near_y, near_y, size_z)
        return here, (given[at, :] + factor * total) * inverse[at, :]

    for i in range(1, near_x - 1):
        here, fit = fit_of(local_a, i)
        local_b[pl.ds(8 + i * near_y, near_y), :] = here + (fit - here) * (1.0 / centre)
    for i in range(2, near_x - 2):
        here, fit = fit_of(local_b, i)
        at = pl.ds(8 + i * near_y, near_y)
        local_a[at, :] = here + (keep * (here - local_a[at, :]) + gain * (fit - here))


def add_correction(start, iterate, local, sizes, mat_0, plane):
    ends = pl.ds(0, 8), pl.ds(start.shape[0] - 8, 8)
    for at in ends:
        iterate[at, :] = start[at, :]
    near_y = sizes.own_y + 16
    half_y = plane // 2
    planes = sizes.own_x + 4
    value = jnp.concatenate(
        [local[pl.ds(8 + (2 + i) * near_y + 4, half_y), :] for i in range(planes)], 0
    )
    wide = spread_lanes(value, mat_0[...])
    for i in range(planes):
        for j in range(4):
            error = wide[i * half_y : (i + 1) * half_y, (j // 2) * LANES : (j // 2 + 1) * LANES]
            for side in (0, 1):
                at = pl.ds(8 + (4 * i + j) * plane + side, half_y, stride=2)
                iterate[at, :] = start[at, :] + error


def middle_kernel(sizes, place, near, far, start, field, scaled, count_x, mat_0, mat_1, mat_2, *rest):
    iterate, packet, inverse, diag, screen_two, screen_three = rest[:6]
    given, step, coarse, rows_ref, local_a, local_b, two_a, two_b, other, fine_rows = rest[6:]
    wide, size_y = count_x.shape[:2]
    size_x = wide - 2 * HALO
    plane = size_y + 2 * HALO
    refs = (given, inverse, diag, step, coarse, rows_ref, (screen_two, screen_three), local_a, local_b, two_a, two_b)
    level_one(place, (near, far), sizes, (mat_1, mat_2), refs, True)
    add_correction(start, iterate, local_a, sizes, mat_0, plane)
    finest_step_one(iterate, other, field, scaled, 6, wide, plane)
    finest_step_two(other, iterate, field, scaled, 5, wide, plane)
    finest_step_one(iterate, other, field, scaled, 4, wide, plane)
    finest_step_two(other, iterate, field, scaled, 3, wide, plane)

    def write(i, here, value):
        fine_rows[pl.ds(i * size_y, size_y), :] = value

    finest_residual(iterate, field, count_x, size_x, size_y, write)
    even, odd = restrict_finest(fine_rows, size_x, size_y, mat_0)
    send_coarse(packet, 0.125 * gather_lanes(jnp.concatenate([even, odd], 1), mat_0[...]), None, size_y // 2)


def last_kernel(sizes, place, near, far, start, field, scaled, count_x, inverse, diag, screen_two, screen_three, *rest):
    mat_0, mat_1, mat_2, solution_far, residual_far = rest[:5]
    given, step, coarse, rows_ref, local_a, local_b, two_a, two_b, iterate, other = rest[5:15]
    solution_out, residual_out, left = rest[15:]
    wide, size_y = count_x.shape[:2]
    size_x = wide - 2 * HALO
    plane = size_y + 2 * HALO
    refs = (given, inverse, diag, step, coarse, rows_ref, (screen_two, screen_three), local_a, local_b, two_a, two_b)
    level_one(place, (near, far), sizes, (mat_1, mat_2), refs, False)
    add_correction(start, iterate, local_a, sizes, mat_0, plane)
    finest_step_one(iterate, other, field, scaled, 2, wide, plane)
    finest_step_two(other, iterate, field, scaled, 1, wide, plane)

    def send(source, target, which):
        copy = pltpu.make_async_copy(source, target, left.at[which])
        copy.start()
        return copy

    for i in range(size_x):
        solution_out[i] = iterate[pl.ds(8 + (HALO + i) * plane + HALO, size_y), :]
    copies = [send(solution_out, solution_far, 0)]

    def write(i, here, value):
        residual_out[i] = value
        if (2 * i + 2) % size_x == 0:
            half = pl.ds(i + 1 - size_x // 2, size_x // 2)
            copies.append(send(residual_out.at[half], residual_far.at[half], 1 + (i + 1) * 2 // size_x))

    finest_residual(iterate, field, count_x, size_x, size_y, write)
    for copy in copies:
        copy.wait()


def exchange(first, second, axis):
    count = lax.axis_size(axis)

    def pairs(start):
        found = []
        for i in range(start, count - 1, 2):
            found += [(i, i + 1), (i + 1, i)]
        return found

    return lax.ppermute(first, axis, pairs(1)), lax.ppermute(second, axis, pairs(0))


def gather(packet):
    near = lax.all_to_all(packet, ("gx", "gy_chip"), 0, 0, tiled=True)
    return near, lax.ppermute(near, "gy_core", [(0, 1), (1, 0)])


def per_device(point_counts, face_counts):
    size_x, size_y, size_z = point_counts.shape
    assert size_z == LANES and size_x == 16 and size_y == 16
    mesh_x = lax.axis_size("gx")
    mesh_y = lax.axis_size("gy_chip") * lax.axis_size("gy_core")
    gx = lax.axis_index("gx")
    gy = lax.axis_index("gy_chip") * 2 + lax.axis_index("gy_core")
    place = jnp.stack([gx, gy]).astype(jnp.int32)
    wide, plane = size_x + 2 * HALO, size_y + 2 * HALO
    flat = 16 + wide * plane
    sizes = Sizes(mesh_x, mesh_y, size_x, size_y)
    copies = mesh_x * mesh_y // 2
    mats = [transfer_matrix(level) for level in range(3)]
    params = pltpu.CompilerParams(vmem_limit_bytes=(24 if sizes.flat < 4096 else 56) * 2**20)

    def call(kernel, outs, scratch, *args, copies=0, far_out=False, cost=None):
        return pl.pallas_call(
            kernel,
            out_shape=[jax.ShapeDtypeStruct(shape, dtype) for shape, dtype in outs],
            in_specs=[SMEM] + [VMEM] * (len(args) - 1),
            out_specs=[FAR if far_out else VMEM] * len(outs),
            scratch_shapes=[pltpu.VMEM(shape, dtype) for shape, dtype in scratch]
            + ([pltpu.SemaphoreType.DMA((copies,))] if copies else []),
            compiler_params=params,
            cost_estimate=cost,
        )(*args)

    cells = (size_x, size_y, LANES)
    packet = (2 * HALO + 2, size_y, LANES)
    first, second, part, count, edge = call(
        cells_kernel,
        [(packet, BF16), (packet, BF16), (cells, BF16), (cells, BF16), ((2, size_y, LANES), BF16)],
        [],
        place,
        pack_cell(face_counts, point_counts),
    )
    first, second = exchange(first, second, "gx")
    packet = (wide - HALO + wide // size_y, size_y, LANES)
    strip = (wide, size_y, LANES)
    first, second, part_x, count_x, edge_x = call(
        wide_kernel,
        [(packet, BF16), (packet, BF16), (strip, BF16), (strip, BF16), ((wide, LANES), F32)],
        [],
        place,
        first,
        second,
        part,
        count,
        edge,
    )
    first, second = exchange(first, second, ("gy_chip", "gy_core"))
    own = sizes.own_x
    received = (first, second, part_x, count_x, edge_x)
    flat_f32 = ((flat, LANES), F32)
    (packet,) = call(
        start_kernel,
        [((copies, own + 1, 2 * sizes.own_y, LANES), jnp.int16)],
        [flat_f32] * 4 + [((size_x * size_y, LANES), F32)],
        place,
        *received,
        mats[0],
    )
    near, far = gather(packet)
    iterate, field, scaled = call(
        surroundings_kernel,
        [flat_f32] * 3,
        [flat_f32],
        place,
        near,
        *received,
        cost=pl.CostEstimate(flops=1 << 22, bytes_accessed=4 << 20, transcendentals=0),
    )
    level = (sizes.flat, LANES)
    flat_two = ((sizes.planes // 4 + 2) * (sizes.rows // 2 + 8) + 8, LANES)
    around = (16 + (own + 8) * (sizes.own_y + 16), LANES)
    scratch = [
        (level, F32),
        (level, F32),
        (level, F32),
        ((sizes.planes * sizes.rows, LANES), F32),
        (around, F32),
        (around, F32),
        (flat_two, F32),
        (flat_two, F32),
        ((flat, LANES), F32),
    ]
    level_two = (sizes.planes // 4, sizes.rows // 2, LANES)
    level_three = (sizes.planes // 16, sizes.rows // 4, LANES)
    iterate, packet, inverse, diag, screen_two, screen_three = call(
        lambda *refs: middle_kernel(sizes, *refs),
        [
            ((flat, LANES), F32),
            ((copies, own // 2 + 1, 2 * sizes.own_y, LANES), jnp.int16),
            (level, F32),
            (level, F32),
            (level_two, F32),
            (level_three, F32),
        ],
        scratch + [((size_x * size_y, LANES), F32)],
        place,
        near,
        far,
        iterate,
        field,
        scaled,
        count_x,
        *mats,
    )
    solution_own, residual_own = call(
        lambda *refs: last_kernel(sizes, *refs),
        [(cells, F32), (cells, F32)],
        scratch + [((flat, LANES), F32), (cells, F32), (cells, F32)],
        place,
        *gather(packet),
        iterate,
        field,
        scaled,
        count_x,
        inverse,
        diag,
        screen_two,
        screen_three,
        *mats,
        copies=4,
        far_out=True,
    )
    return solution_own, residual_own


def solution(mesh):
    mesh_x, mesh_y = mesh.shape["gx"], mesh.shape["gy"]
    split = Mesh(mesh.devices.reshape(mesh_x, mesh_y // 2, 2), ("gx", "gy_chip", "gy_core"))
    rows = ("gy_chip", "gy_core")

    def run(point_counts, face_counts):
        return jax.shard_map(
            per_device,
            mesh=split,
            in_specs=(P("gx", rows, None), P(None, "gx", rows, None)),
            out_specs=(P("gx", rows, None), P("gx", rows, None)),
            check_vma=False,
        )(point_counts, face_counts)

    return run
```

```python
import numpy as np
import jax
import jax.numpy as jnp
from jax import lax
from jax.experimental import pallas as pl
from jax.experimental.pallas import tpu as pltpu
from jax.sharding import Mesh, PartitionSpec as P

F32 = jnp.float32
BF16 = jnp.bfloat16
LANES = 128
HALO = 8
COARSE_ITERS = 6

screen_weight = 0.25
flux_scale = 0.125
low_edge = 0.3
high_edge = 2.0
centre = 0.5 * (high_edge + low_edge)
radius = 0.5 * (high_edge - low_edge)
ratio = centre / radius
mom_first = 1.0 / ratio
mom_second = 1.0 / (2.0 * ratio - mom_first)
keep = mom_second * mom_first
gain = 2.0 * mom_second / radius

VMEM = pl.BlockSpec(memory_space=pltpu.VMEM)
SMEM = pl.BlockSpec(memory_space=pltpu.SMEM)
FAR = pl.BlockSpec(memory_space=pltpu.HBM)


def transfer_matrix(level):
    pack, size_z = 1 << level, LANES >> level
    planes = 2 if level == 0 else 4
    out = np.zeros((planes * LANES, LANES), np.float32)
    for j in range(planes):
        for q in range(pack):
            coarse = j if level == 0 else (j * pack + q) // 2
            for z in range(size_z):
                out[j * LANES + q * size_z + z, coarse * (size_z // 2) + z // 2] = 1.0
    return jnp.asarray(out, BF16)


def in_parts(value):
    high = value.astype(BF16)
    rest = value - high.astype(F32)
    middle = rest.astype(BF16)
    return jnp.concatenate([high, middle, (rest - middle.astype(F32)).astype(BF16)], 0)


def add_parts(value, rows):
    return value[:rows] + (value[rows : 2 * rows] + value[2 * rows :])


def gather_lanes(value, matrix):
    return add_parts(jnp.dot(in_parts(value), matrix, preferred_element_type=F32), value.shape[0])


def spread_lanes(value, matrix):
    dims = (((1,), (1,)), ((), ()))
    return add_parts(lax.dot_general(in_parts(value), matrix, dims, preferred_element_type=F32), value.shape[0])


def lane_index():
    return lax.broadcasted_iota(jnp.int32, (1, LANES), 1)


def z_sum(value, size_z):
    lane = lane_index() & (size_z - 1)
    inner_low = (lane != 0).astype(F32)
    inner_high = (lane != size_z - 1).astype(F32)
    return pltpu.roll(value, 1, 1) * inner_low + pltpu.roll(value, LANES - 1, 1) * inner_high


def x_sum(before, here, after, size_z):
    if size_z == LANES:
        return before + after
    lane = lax.broadcasted_iota(jnp.int32, here.shape, 1)
    if 2 * size_z == LANES:
        return pltpu.roll(here + jnp.where(lane < size_z, after, before), size_z, 1)
    up = pltpu.roll(jnp.where(lane < size_z, after, here), LANES - size_z, 1)
    down = pltpu.roll(jnp.where(lane >= LANES - size_z, before, here), size_z, 1)
    return up + down


def neighbours(ref, base, rows, stride, size_z):
    here = ref[pl.ds(base, rows), :]
    total = x_sum(ref[pl.ds(base - stride, rows), :], here, ref[pl.ds(base + stride, rows), :], size_z)
    total = total + (ref[pl.ds(base - 1, rows), :] + ref[pl.ds(base + 1, rows), :])
    return here, total + z_sum(here, size_z)


def for_planes(count, body, limit=64):
    if count <= limit:
        for i in range(count):
            body(i)
    else:
        step = 8

        def block(k, carry):
            for j in range(step):
                body(k * step + j)
            return carry

        lax.fori_loop(0, count // step, block, 0)


def pair_rows(ref, start, rows):
    return ref[pl.ds(start, rows // 2, stride=2), :] + ref[pl.ds(start + 1, rows // 2, stride=2), :]


def pack_cell(faces, points):
    word = points << 18
    for c in range(3):
        word = word + ((faces[c] + 32) << (6 * c))
    return word


def cells_kernel(place, words, first, second, part, count, edge):
    size_x, size_y = words.shape[:2]
    lane = lax.broadcasted_iota(jnp.int32, (size_y, LANES), 1)
    row = lax.broadcasted_iota(jnp.int32, (size_y, LANES), 0)
    last_x = None
    for i in range(size_x):
        word = words[i]
        along_x, along_y, along_z = [((word >> (6 * c)) & 63) - 32 for c in range(3)]
        total = jnp.where(row != 0, pltpu.roll(along_y, 1, 0), 0) - along_y
        total = total + (jnp.where(lane != 0, pltpu.roll(along_z, 1, 1), 0) - along_z) - along_x
        if last_x is not None:
            total = total + last_x
        last_x = along_x
        part[i] = total.astype(F32).astype(BF16)
        count[i] = ((word >> 18) + 1).astype(F32).astype(BF16)
    edge[0] = last_x.astype(F32).astype(BF16)
    edge[1] = (((words[:, size_y - 1, :] >> 6) & 63) - 32).astype(F32).astype(BF16)

    def write(up, down):
        for target, start in ((up, size_x - HALO), (down, 0)):
            target[0:HALO] = part[start : start + HALO]
            target[HALO : 2 * HALO] = count[start : start + HALO]
            target[2 * HALO : 2 * HALO + 2] = edge[...]

    odd = 1 - place[0] % 2

    @pl.when(odd == 0)
    def _():
        write(first, second)

    @pl.when(odd == 1)
    def _():
        write(second, first)


def plane_slot(i, wide):
    size_x = wide - 2 * HALO
    if HALO <= i < HALO + size_x:
        return i - HALO, None
    distance = HALO - i if i < HALO else i - HALO - size_x + 1
    near = min(distance, HALO + 1 - distance)
    slot = size_x + near - 1 + (0 if i < HALO else HALO // 2)
    return slot, (near if near != distance else None)


def wide_kernel(place, got_first, got_second, part, count, edge, first, second, part_x, count_x, edge_x):
    size_x, size_y = part.shape[:2]
    wide = size_x + 2 * HALO

    def fill(below, above):
        part_x[0:HALO] = below[0:HALO]
        part_x[HALO + size_x :] = above[0:HALO]
        count_x[0:HALO] = below[HALO : 2 * HALO]
        count_x[HALO + size_x :] = above[HALO : 2 * HALO]
        part_x[HALO : HALO + size_x] = part[...]
        count_x[HALO : HALO + size_x] = count[...]
        part_x[HALO] = (part[0].astype(F32) + below[2 * HALO].astype(F32)).astype(BF16)
        part_x[HALO + size_x] = (above[0].astype(F32) + edge[0].astype(F32)).astype(BF16)
        edge_x[0:HALO] = below[2 * HALO + 1].astype(F32)[size_x - HALO :]
        edge_x[HALO : HALO + size_x] = edge[1].astype(F32)
        edge_x[HALO + size_x :] = above[2 * HALO + 1].astype(F32)[:HALO]

    odd = 1 - place[0] % 2

    @pl.when(odd == 0)
    def _():
        fill(got_second, got_first)

    @pl.when(odd == 1)
    def _():
        fill(got_first, got_second)

    def write(up, down):
        row = lax.broadcasted_iota(jnp.int32, (HALO, LANES), 0)
        for i in range(wide):
            slot, far = plane_slot(i, wide)
            if far is not None:
                continue
            pairs = [(part_x[i].astype(F32), count_x[i].astype(F32))]
            for k in range(wide):
                other, d = plane_slot(k, wide)
                if other == slot and d is not None:
                    pairs.append((part_x[k].astype(F32), count_x[k].astype(F32)))
                    break
            tops = [[value[size_y - HALO :] for value in pair] for pair in pairs]
            ends = [[value[:HALO] for value in pair] for pair in pairs]
            if len(pairs) == 2:
                tops[0] = [jnp.where(row >= d, a, pltpu.roll(b, d - 1, 0)) for a, b in zip(*tops)]
                ends[0] = [jnp.where(row < HALO - d, a, pltpu.roll(b, HALO + 1 - d, 0)) for a, b in zip(*ends)]
            up[slot] = jnp.concatenate(tops[0], 0).astype(BF16)
            down[slot] = jnp.concatenate(ends[0], 0).astype(BF16)
        for target in (up, down):
            for j in range(wide // size_y):
                target[wide - HALO + j] = edge_x[j * size_y : (j + 1) * size_y].astype(BF16)

    odd_y = 1 - place[1] % 2

    @pl.when(odd_y == 0)
    def _():
        write(first, second)

    @pl.when(odd_y == 1)
    def _():
        write(second, first)


def finest_parts(margin, wide, plane):
    planes = range(HALO - margin, wide - HALO + margin)
    if margin > 4:
        return [(8 + i * plane, 2 * plane) for i in planes[::2]]
    return [(8 + i * plane + HALO - 4, plane - 2 * HALO + 8) for i in planes]


def finest_step_one(source, target, field, scaled, margin, wide, plane):
    for base, rows in finest_parts(margin, wide, plane):
        at = pl.ds(base, rows)
        here, total = neighbours(source, base, rows, plane, LANES)
        fit = (field[at, :] + total) * scaled[at, :]
        target[at, :] = here + (fit - here) * (1.0 / centre)


def finest_step_two(source, old, field, scaled, margin, wide, plane):
    for base, rows in finest_parts(margin, wide, plane):
        at = pl.ds(base, rows)
        here, total = neighbours(source, base, rows, plane, LANES)
        fit = (field[at, :] + total) * scaled[at, :]
        old[at, :] = here + (keep * (here - old[at, :]) + gain * (fit - here))


def finest_step_two_from_zero(source, target, field, scaled, margin, wide, plane):
    for base, rows in finest_parts(margin, wide, plane):
        at = pl.ds(base, rows)
        here, total = neighbours(source, base, rows, plane, LANES)
        fit = (field[at, :] + total) * scaled[at, :]
        target[at, :] = here + (keep * here + gain * (fit - here))


def finest_residual(iterate, field, count, size_x, size_y, write):
    plane = size_y + 2 * HALO
    for i in range(size_x):
        base = 8 + (HALO + i) * plane + HALO
        here, total = neighbours(iterate, base, size_y, plane, LANES)
        diag = 6.0 + screen_weight * (count[HALO + i].astype(F32) - 1.0)
        write(i, here, field[pl.ds(base, size_y), :] + total - diag * here)


def restrict_finest(rows_ref, size_x, size_y, matrix):
    half = pair_rows(rows_ref, 0, size_x * size_y).reshape(size_x // 4, 4, size_y // 2, LANES)
    even = (half[:, 0] + half[:, 1]).reshape(-1, LANES)
    odd = (half[:, 2] + half[:, 3]).reshape(-1, LANES)
    return even, odd


def inverse_diag(count):
    return jnp.where(count > 0.0, 1.0 / (6.0 - screen_weight + screen_weight * count), 0.0)


def columns_kernel(place, count_x, matrix, inverse_x, points, rows_ref):
    wide, size_y = count_x.shape[:2]
    size_x = wide - 2 * HALO
    for i in range(wide):
        inverse_x[i] = inverse_diag(count_x[i].astype(F32))
    for i in range(size_x):
        rows_ref[pl.ds(i * size_y, size_y), :] = count_x[HALO + i].astype(F32) - 1.0
    even, odd = restrict_finest(rows_ref, size_x, size_y, matrix)
    points[...] = jnp.dot(jnp.concatenate([even, odd], 1).astype(BF16), matrix[...], preferred_element_type=F32)


def first_step(place, got, part_x, inverse_x, edge_x, iterate, field, inverse, margin):
    wide, size_y = part_x.shape[:2]
    plane = size_y + 2 * HALO
    even = place[1] % 2 == 1
    top = lax.broadcasted_iota(jnp.int32, (HALO, LANES), 0) == 0
    under_rows = [
        jnp.where(even, got[1][wide - HALO + j], got[0][wide - HALO + j]).astype(F32) for j in range(wide // size_y)
    ]
    for i in range(HALO - margin, wide - HALO + margin):
        slot, d = plane_slot(i, wide)
        below = jnp.where(even, got[1][slot], got[0][slot]).astype(F32)
        above = jnp.where(even, got[0][slot], got[1][slot]).astype(F32)
        if d is not None:
            below = jnp.concatenate([pltpu.roll(part, HALO + 1 - d, 0) for part in (below[:HALO], below[HALO:])], 0)
            above = jnp.concatenate([pltpu.roll(part, d - 1, 0) for part in (above[:HALO], above[HALO:])], 0)
        own = part_x[i].astype(F32)
        under = under_rows[i // size_y][i % size_y : i % size_y + 1]
        over = edge_x[i : i + 1]
        cells = jnp.concatenate(
            [
                below[:HALO],
                own[:HALO] + jnp.where(top, under, 0.0),
                own[HALO:],
                above[:HALO] + jnp.where(top, over, 0.0),
            ],
            0,
        )
        given = flux_scale * cells
        inv = jnp.concatenate([inverse_diag(below[HALO:]), inverse_x[i], inverse_diag(above[HALO:])], 0)
        at = pl.ds(8 + i * plane, plane)
        field[at, :] = given
        inverse[at, :] = inv
        iterate[at, :] = (given * inv) * (1.0 / centre)


def start_kernel(
    place,
    got_first,
    got_second,
    part_x,
    inverse_x,
    edge_x,
    count_x,
    points,
    matrix,
    packet,
    first,
    second,
    field,
    inverse,
    rows_ref,
):
    wide, size_y = part_x.shape[:2]
    size_x = wide - 2 * HALO
    plane = size_y + 2 * HALO
    first_step(place, (got_first, got_second), part_x, inverse_x, edge_x, first, field, inverse, 2)
    finest_step_two_from_zero(first, second, field, inverse, 1, wide, plane)

    def write(i, here, value):
        rows_ref[pl.ds(i * size_y, size_y), :] = value

    finest_residual(second, field, count_x, size_x, size_y, write)
    even, odd = restrict_finest(rows_ref, size_x, size_y, matrix)
    coarse = 0.125 * gather_lanes(jnp.concatenate([even, odd], 1), matrix[...])
    send_coarse(packet, coarse, points[...], size_y // 2)


def surroundings_kernel(
    place, after, got_first, got_second, part_x, inverse_x, edge_x, iterate, field, inverse, first
):
    wide, size_y = part_x.shape[:2]
    plane = size_y + 2 * HALO
    zero = jnp.zeros((8, LANES), F32)
    for ref in (iterate, field, inverse, first):
        ref[0:8] = zero
        ref[8 + wide * plane :] = zero
    first_step(place, (got_first, got_second), part_x, inverse_x, edge_x, first, field, inverse, HALO)
    for base, rows in ((8, plane), (8 + (wide - 1) * plane, plane)):
        iterate[pl.ds(base, rows), :] = first[pl.ds(base, rows), :]
    finest_step_two_from_zero(first, iterate, field, inverse, HALO - 1, wide, plane)


def scale_of(code):
    return jnp.exp2(code * (1.0 / 128.0))


def send_coarse(packet, coarse, points, size_y):
    copies = packet.shape[0]
    tiles = [coarse[i : i + size_y] for i in range(0, coarse.shape[0], size_y)]
    largest = jnp.abs(tiles[0])
    for tile in tiles[1:]:
        largest = jnp.maximum(largest, jnp.abs(tile))
    largest = jnp.maximum(jnp.max(largest, 1, keepdims=True), 1e-30)
    code = jnp.ceil(128.0 * jnp.log2(largest * (1.0 / 32766.0)))
    scale = scale_of(-code)
    rows = [jnp.round(tile * scale) for tile in tiles]
    rows += [jnp.broadcast_to(code, (size_y, LANES)), jnp.zeros((size_y, LANES), F32)]
    if points is not None:
        rows += [points[i : i + size_y] for i in range(0, points.shape[0], size_y)]
    for i in range(0, len(rows), 2):
        tile = jnp.concatenate(rows[i : i + 2], 0).astype(jnp.int32).astype(jnp.int16)
        for k in range(copies):
            packet[k, i // 2] = tile


def packed_apply(value, screen, factor, size_z):
    planes, size_y, _ = value.shape
    flat = value.reshape(planes * size_y, LANES)
    empty = jnp.zeros((1, size_y, LANES), F32)
    if planes > 1:
        before = jnp.concatenate([empty, value[:-1]], 0).reshape(flat.shape)
        after = jnp.concatenate([value[1:], empty], 0).reshape(flat.shape)
    else:
        before = after = jnp.zeros_like(flat)
    row = lax.broadcasted_iota(jnp.int32, value.shape, 1)
    along_y = jnp.where(row != 0, pltpu.roll(value, 1, 1), 0.0) + jnp.where(
        row != size_y - 1, pltpu.roll(value, size_y - 1, 1), 0.0
    )
    total = x_sum(before, flat, after, size_z) + z_sum(flat, size_z)
    return (6.0 * value - (total.reshape(value.shape) + along_y)) * factor + screen * value


def totals_of(*values):
    rows = jnp.concatenate([jnp.sum(value, 0) for value in values], 0)
    sums = jnp.sum(rows, 1, keepdims=True).reshape(len(values), -1, 1)
    sums = jnp.sum(sums, 1, keepdims=True)
    return [sums[i : i + 1] for i in range(len(values))]


def conjugate_gradients(target, screen, factor, size_z):
    planes, size_y, _ = target.shape
    least = sum(2.0 - 2.0 * np.cos(np.pi / (n + 1)) for n in (planes * (LANES // size_z), size_y, size_z))
    longest = 1.001 / (factor * least)
    remain = target
    image = packed_apply(remain, screen, factor, size_z)
    for step in range(COARSE_ITERS):
        more = step + 1 < COARSE_ITERS
        norm, bent = totals_of(remain * remain, remain * image)
        if more:
            ahead = packed_apply(image, screen, factor, size_z)
        if step == 0:
            length = norm / bent
            search, search_image, search_ahead = remain, image, ahead
            iterate = length * search
        else:
            ratio = norm / norm_before
            length = jnp.clip(norm / (bent - ratio * norm / length), 0.0, longest)
            search = remain + ratio * search
            iterate = iterate + length * search
            if more:
                search_image = image + ratio * search_image
                search_ahead = ahead + ratio * search_ahead
        if more:
            remain = remain - length * search_image
            image = image - length * search_ahead
        norm_before = norm
    return iterate


def add_lanes(rows_ref, planes, size_y, matrix, first_plane=0):
    half = pair_rows(rows_ref, first_plane * size_y, planes * size_y).reshape(planes // 4, 4, size_y // 2, LANES)
    wide = jnp.concatenate([half[:, j].reshape(-1, LANES) for j in range(4)], 1)
    return gather_lanes(wide, matrix[...]).reshape(planes // 4, size_y // 2, LANES)


def copy_level(value, matrix):
    planes, size_y, _ = value.shape
    wide = spread_lanes(value.reshape(-1, LANES), matrix[...]).reshape(planes, size_y, 4 * LANES)
    return jnp.stack([wide[:, :, j * LANES : (j + 1) * LANES] for j in range(4)], 1).reshape(
        4 * planes, size_y, LANES
    )


class Sizes:
    def __init__(self, mesh_x, mesh_y, size_x, size_y):
        self.mesh_x, self.mesh_y = mesh_x, mesh_y
        self.own_x, self.own_y = size_x // 4, size_y // 2
        self.planes, self.rows = mesh_x * self.own_x, mesh_y * self.own_y
        self.stride = self.rows + 8
        self.flat = (self.planes + 8) * self.stride + 8
        self.pad_x = 4


def level_one(place, gathered, sizes, mats, refs, first):
    mat_1, mat_2 = mats
    given, inverse, diag, step, iterate, rows_ref, level_two, local_a, local_b, two_a, two_b = refs
    size_z = LANES // 2
    factor = 0.25
    planes, rows, stride, pad = sizes.planes, sizes.rows, sizes.stride, sizes.pad_x
    own_x, own_y = sizes.own_x, sizes.own_y

    def clear(ref):
        ref[0 : pad * stride + 8] = jnp.zeros((pad * stride + 8, LANES), F32)
        ref[(pad + planes) * stride :] = jnp.zeros((pad * stride + 8, LANES), F32)

        def gap(i):
            ref[pl.ds((pad + i) * stride, 8), :] = jnp.zeros((8, LANES), F32)

        for_planes(planes, gap)

    for ref in (given, step, iterate) + ((inverse, diag) if first else ()):
        clear(ref)

    core = place[1] % 2
    per_core = sizes.mesh_x * sizes.mesh_y // 2

    def block(b):
        source, side = (gathered[0], core) if b < per_core else (gathered[1], 1 - core)
        gx = b % per_core // (sizes.mesh_y // 2)
        gy = 2 * (b % (sizes.mesh_y // 2)) + side
        tiles = []
        for i in range(source.shape[1]):
            tile = source[b % per_core, i].astype(jnp.int32).astype(F32)
            tiles += [tile[:own_y], tile[own_y:]]
        scale = scale_of(tiles[own_x])
        for i in range(own_x):
            start = (pad + gx * own_x + i) * stride + 8 + gy * own_y
            at = pl.ds(pl.multiple_of(start, 8), own_y)
            value = tiles[i] * scale
            if first:
                d = 6.0 * factor + (screen_weight * 0.125) * tiles[own_x + 2 + i]
                diag[at, :] = d
                inv = 1.0 / d
                inverse[at, :] = inv
            else:
                inv = inverse[at, :]
            given[at, :] = value
            step[at, :] = value * inv * (1.0 / centre)

    for b in range(sizes.mesh_x * sizes.mesh_y):
        block(b)

    def second(i):
        base = (pad + i) * stride + 8
        at = pl.ds(base, rows)
        here, total = neighbours(step, base, rows, stride, size_z)
        fit = (given[at, :] + factor * total) * inverse[at, :]
        iterate[at, :] = here + (keep * here + gain * (fit - here))

    for_planes(planes, second)

    def residual(i):
        base = (pad + i) * stride + 8
        at = pl.ds(base, rows)
        here, total = neighbours(iterate, base, rows, stride, size_z)
        rows_ref[pl.ds(i * rows, rows), :] = given[at, :] + factor * total - diag[at, :] * here

    groups = 4 if planes <= 64 else 1
    if groups == 1:
        for_planes(planes, residual)
    targets = []
    for k in range(groups):
        for i in range(k * planes // groups, (k + 1) * planes // groups if groups > 1 else 0):
            residual(i)
        targets.append(add_lanes(rows_ref, planes // groups, rows, mat_1, k * planes // groups))
    target = 0.125 * jnp.concatenate(targets, 0)

    screen_two, screen_three = level_two
    if first:

        def screens(i):
            at = pl.ds((pad + i) * stride + 8, rows)
            rows_ref[pl.ds(i * rows, rows), :] = diag[at, :] - 6.0 * factor

        for_planes(planes, screens)
        screen_two[...] = 0.125 * add_lanes(rows_ref, planes, rows, mat_1)
    planes_2, rows_2 = planes // 4, rows // 2
    screen = screen_two[...]
    level = 6.0 * factor**2 + screen
    inv = 1.0 / level
    if first:
        rows_ref[0 : planes_2 * rows_2] = screen.reshape(-1, LANES)
        screen_three[...] = 0.125 * add_lanes(rows_ref, planes_2, rows_2, mat_2)
    stride_2 = rows_2 + 8

    def at_2(i):
        return (1 + i) * stride_2 + 8

    for ref in (two_a, two_b):
        for start, count in ((0, stride_2 + 8), ((planes_2 + 1) * stride_2, stride_2 + 8)):
            ref[start : start + count] = jnp.zeros((count, LANES), F32)
        for i in range(planes_2):
            ref[at_2(i) - 8 : at_2(i)] = jnp.zeros((8, LANES), F32)

    def fit_two(ref, i):
        here, total = neighbours(ref, at_2(i), rows_2, stride_2, LANES // 4)
        return here, (target[i] + factor**2 * total) * inv[i]

    for i in range(planes_2):
        two_a[pl.ds(at_2(i), rows_2), :] = target[i] * inv[i] * (1.0 / centre)
    for i in range(planes_2):
        here, fit = fit_two(two_a, i)
        two_b[pl.ds(at_2(i), rows_2), :] = here + (keep * here + gain * (fit - here))
    for i in range(planes_2):
        here, total = neighbours(two_b, at_2(i), rows_2, stride_2, LANES // 4)
        rows_ref[i * rows_2 : (i + 1) * rows_2] = target[i] + factor**2 * total - level[i] * here
    target_3 = 0.125 * add_lanes(rows_ref, planes_2, rows_2, mat_2)
    error = conjugate_gradients(target_3, screen_three[...], factor**3, LANES // 8)
    error = copy_level(error, mat_2).reshape(-1, LANES)
    count = planes_2 * rows_2
    rows_ref[pl.ds(0, count // 2, stride=2), :] = error
    rows_ref[pl.ds(1, count // 2, stride=2), :] = error
    for i in range(planes_2):
        two_a[pl.ds(at_2(i), rows_2), :] = two_b[pl.ds(at_2(i), rows_2), :] + rows_ref[i * rows_2 : (i + 1) * rows_2]
    for i in range(planes_2):
        here, fit = fit_two(two_a, i)
        two_b[pl.ds(at_2(i), rows_2), :] = here + (fit - here) * (1.0 / centre)

    rows_ref[0:rows_2] = jnp.zeros((rows_2, LANES), F32)
    rows_ref[(planes_2 + 1) * rows_2 : (planes_2 + 2) * rows_2] = jnp.zeros((rows_2, LANES), F32)
    for i in range(planes_2):
        here, fit = fit_two(two_b, i)
        before = two_a[pl.ds(at_2(i), rows_2), :]
        rows_ref[(i + 1) * rows_2 : (i + 2) * rows_2] = here + (keep * (here - before) + gain * (fit - here))
    near_2 = own_x // 4 + 2
    start = pl.multiple_of(place[0] * (own_x // 4) * rows_2, 8)
    near = rows_ref[pl.ds(start, near_2 * rows_2), :].reshape(near_2, rows_2, LANES)
    error = copy_level(near, mat_1)
    near_x, near_y = 4 * near_2, own_y + 16
    first_plane = place[0] * own_x
    for i in range(near_x):
        base = (first_plane + i) * stride + 8
        even, odd = pl.ds(base, rows_2, stride=2), pl.ds(base + 1, rows_2, stride=2)
        iterate[even, :] = iterate[even, :] + error[i]
        iterate[odd, :] = iterate[odd, :] + error[i]
    for i in range(near_x):
        at = pl.ds(pl.multiple_of((first_plane + i) * stride + place[1] * own_y, 8), near_y)
        local_a[pl.ds(8 + i * near_y, near_y), :] = iterate[at, :]
    for ref in (local_a, local_b):
        ref[0:8] = jnp.zeros((8, LANES), F32)
        ref[8 + near_x * near_y :] = jnp.zeros((8, LANES), F32)
    ends = pl.ds(8, near_y), pl.ds(8 + (near_x - 1) * near_y, near_y)
    for at in ends:
        local_b[at, :] = jnp.zeros((near_y, LANES), F32)

    def fit_of(ref, i):
        at = pl.ds(pl.multiple_of((first_plane + i) * stride + place[1] * own_y, 8), near_y)
        here, total = neighbours(ref, 8 + i * near_y, near_y, near_y, size_z)
        return here, (given[at, :] + factor * total) * inverse[at, :]

    for i in range(1, near_x - 1):
        here, fit = fit_of(local_a, i)
        local_b[pl.ds(8 + i * near_y, near_y), :] = here + (fit - here) * (1.0 / centre)
    for i in range(2, near_x - 2):
        here, fit = fit_of(local_b, i)
        at = pl.ds(8 + i * near_y, near_y)
        local_a[at, :] = here + (keep * (here - local_a[at, :]) + gain * (fit - here))


def add_correction(start, iterate, local, sizes, mat_0, plane):
    ends = pl.ds(0, 8), pl.ds(start.shape[0] - 8, 8)
    for at in ends:
        iterate[at, :] = start[at, :]
    near_y = sizes.own_y + 16
    half_y = plane // 2
    planes = sizes.own_x + 4
    value = jnp.concatenate(
        [local[pl.ds(8 + (2 + i) * near_y + 4, half_y), :] for i in range(planes)], 0
    )
    wide = spread_lanes(value, mat_0[...])
    for i in range(planes):
        for j in range(4):
            error = wide[i * half_y : (i + 1) * half_y, (j // 2) * LANES : (j // 2 + 1) * LANES]
            for side in (0, 1):
                at = pl.ds(8 + (4 * i + j) * plane + side, half_y, stride=2)
                iterate[at, :] = start[at, :] + error


def middle_kernel(sizes, place, near, far, start, field, scaled, count_x, mat_0, mat_1, mat_2, *rest):
    iterate, packet, inverse, diag, screen_two, screen_three = rest[:6]
    given, step, coarse, rows_ref, local_a, local_b, two_a, two_b, other, fine_rows = rest[6:]
    wide, size_y = count_x.shape[:2]
    size_x = wide - 2 * HALO
    plane = size_y + 2 * HALO
    refs = (given, inverse, diag, step, coarse, rows_ref, (screen_two, screen_three), local_a, local_b, two_a, two_b)
    level_one(place, (near, far), sizes, (mat_1, mat_2), refs, True)
    add_correction(start, iterate, local_a, sizes, mat_0, plane)
    finest_step_one(iterate, other, field, scaled, 6, wide, plane)
    finest_step_two(other, iterate, field, scaled, 5, wide, plane)
    finest_step_one(iterate, other, field, scaled, 4, wide, plane)
    finest_step_two(other, iterate, field, scaled, 3, wide, plane)

    def write(i, here, value):
        fine_rows[pl.ds(i * size_y, size_y), :] = value

    finest_residual(iterate, field, count_x, size_x, size_y, write)
    even, odd = restrict_finest(fine_rows, size_x, size_y, mat_0)
    send_coarse(packet, 0.125 * gather_lanes(jnp.concatenate([even, odd], 1), mat_0[...]), None, size_y // 2)


def last_kernel(sizes, place, near, far, start, field, scaled, count_x, inverse, diag, screen_two, screen_three, *rest):
    mat_0, mat_1, mat_2, solution_far, residual_far = rest[:5]
    given, step, coarse, rows_ref, local_a, local_b, two_a, two_b, iterate, other = rest[5:15]
    solution_out, residual_out, left = rest[15:]
    wide, size_y = count_x.shape[:2]
    size_x = wide - 2 * HALO
    plane = size_y + 2 * HALO
    refs = (given, inverse, diag, step, coarse, rows_ref, (screen_two, screen_three), local_a, local_b, two_a, two_b)
    level_one(place, (near, far), sizes, (mat_1, mat_2), refs, False)
    add_correction(start, iterate, local_a, sizes, mat_0, plane)
    finest_step_one(iterate, other, field, scaled, 2, wide, plane)
    finest_step_two(other, iterate, field, scaled, 1, wide, plane)

    def send(source, target, which):
        copy = pltpu.make_async_copy(source, target, left.at[which])
        copy.start()
        return copy

    for i in range(size_x):
        solution_out[i] = iterate[pl.ds(8 + (HALO + i) * plane + HALO, size_y), :]
    copies = [send(solution_out, solution_far, 0)]

    def write(i, here, value):
        residual_out[i] = value
        if (2 * i + 2) % size_x == 0:
            half = pl.ds(i + 1 - size_x // 2, size_x // 2)
            copies.append(send(residual_out.at[half], residual_far.at[half], 1 + (i + 1) * 2 // size_x))

    finest_residual(iterate, field, count_x, size_x, size_y, write)
    for copy in copies:
        copy.wait()


def exchange(first, second, axis):
    count = lax.axis_size(axis)

    def pairs(start):
        found = []
        for i in range(start, count - 1, 2):
            found += [(i, i + 1), (i + 1, i)]
        return found

    return lax.ppermute(first, axis, pairs(1)), lax.ppermute(second, axis, pairs(0))


def gather(packet):
    near = lax.all_to_all(packet, ("gx", "gy_chip"), 0, 0, tiled=True)
    return near, lax.ppermute(near, "gy_core", [(0, 1), (1, 0)])


def per_device(point_counts, face_counts):
    size_x, size_y, size_z = point_counts.shape
    assert size_z == LANES and size_x == 16 and size_y == 16
    mesh_x = lax.axis_size("gx")
    mesh_y = lax.axis_size("gy_chip") * lax.axis_size("gy_core")
    gx = lax.axis_index("gx")
    gy = lax.axis_index("gy_chip") * 2 + lax.axis_index("gy_core")
    place = jnp.stack([gx, gy]).astype(jnp.int32)
    wide, plane = size_x + 2 * HALO, size_y + 2 * HALO
    flat = 16 + wide * plane
    sizes = Sizes(mesh_x, mesh_y, size_x, size_y)
    copies = mesh_x * mesh_y // 2
    mats = [transfer_matrix(level) for level in range(3)]
    params = pltpu.CompilerParams(vmem_limit_bytes=(24 if sizes.flat < 4096 else 56) * 2**20)

    def call(kernel, outs, scratch, *args, copies=0, far_out=False, cost=None):
        return pl.pallas_call(
            kernel,
            out_shape=[jax.ShapeDtypeStruct(shape, dtype) for shape, dtype in outs],
            in_specs=[SMEM] + [VMEM] * (len(args) - 1),
            out_specs=[FAR if far_out else VMEM] * len(outs),
            scratch_shapes=[pltpu.VMEM(shape, dtype) for shape, dtype in scratch]
            + ([pltpu.SemaphoreType.DMA((copies,))] if copies else []),
            compiler_params=params,
            cost_estimate=cost,
        )(*args)

    beside = pl.CostEstimate(flops=1 << 22, bytes_accessed=4 << 20, transcendentals=0)
    cells = (size_x, size_y, LANES)
    packet = (2 * HALO + 2, size_y, LANES)
    first, second, part, count, edge = call(
        cells_kernel,
        [(packet, BF16), (packet, BF16), (cells, BF16), (cells, BF16), ((2, size_y, LANES), BF16)],
        [],
        place,
        pack_cell(face_counts, point_counts),
    )
    first, second = exchange(first, second, "gx")
    packet = (wide - HALO + wide // size_y, size_y, LANES)
    strip = (wide, size_y, LANES)
    first, second, part_x, count_x, edge_x = call(
        wide_kernel,
        [(packet, BF16), (packet, BF16), (strip, BF16), (strip, BF16), ((wide, LANES), F32)],
        [],
        place,
        first,
        second,
        part,
        count,
        edge,
    )
    first, second = exchange(first, second, ("gy_chip", "gy_core"))
    own = sizes.own_x
    flat_f32 = ((flat, LANES), F32)
    inverse_x, points = call(
        columns_kernel,
        [(strip, F32), ((own * sizes.own_y, LANES), F32)],
        [((size_x * size_y, LANES), F32)],
        place,
        count_x,
        mats[0],
        cost=beside,
    )
    received = (first, second, part_x, inverse_x, edge_x)
    (packet,) = call(
        start_kernel,
        [((copies, own + 1, 2 * sizes.own_y, LANES), jnp.int16)],
        [flat_f32] * 4 + [((size_x * size_y, LANES), F32)],
        place,
        *received,
        count_x,
        points,
        mats[0],
    )
    near, far = gather(packet)
    iterate, field, scaled = call(
        surroundings_kernel,
        [flat_f32] * 3,
        [flat_f32],
        place,
        near,
        *received,
        cost=beside,
    )
    level = (sizes.flat, LANES)
    flat_two = ((sizes.planes // 4 + 2) * (sizes.rows // 2 + 8) + 8, LANES)
    around = (16 + (own + 8) * (sizes.own_y + 16), LANES)
    scratch = [
        (level, F32),
        (level, F32),
        (level, F32),
        ((sizes.planes * sizes.rows, LANES), F32),
        (around, F32),
        (around, F32),
        (flat_two, F32),
        (flat_two, F32),
        ((flat, LANES), F32),
    ]
    level_two = (sizes.planes // 4, sizes.rows // 2, LANES)
    level_three = (sizes.planes // 16, sizes.rows // 4, LANES)
    iterate, packet, inverse, diag, screen_two, screen_three = call(
        lambda *refs: middle_kernel(sizes, *refs),
        [
            ((flat, LANES), F32),
            ((copies, own // 2 + 1, 2 * sizes.own_y, LANES), jnp.int16),
            (level, F32),
            (level, F32),
            (level_two, F32),
            (level_three, F32),
        ],
        scratch + [((size_x * size_y, LANES), F32)],
        place,
        near,
        far,
        iterate,
        field,
        scaled,
        count_x,
        *mats,
    )
    solution_own, residual_own = call(
        lambda *refs: last_kernel(sizes, *refs),
        [(cells, F32), (cells, F32)],
        scratch + [((flat, LANES), F32), (cells, F32), (cells, F32)],
        place,
        *gather(packet),
        iterate,
        field,
        scaled,
        count_x,
        inverse,
        diag,
        screen_two,
        screen_three,
        *mats,
        copies=4,
        far_out=True,
    )
    return solution_own, residual_own


def solution(mesh):
    mesh_x, mesh_y = mesh.shape["gx"], mesh.shape["gy"]
    split = Mesh(mesh.devices.reshape(mesh_x, mesh_y // 2, 2), ("gx", "gy_chip", "gy_core"))
    rows = ("gy_chip", "gy_core")

    def run(point_counts, face_counts):
        return jax.shard_map(
            per_device,
            mesh=split,
            in_specs=(P("gx", rows, None), P(None, "gx", rows, None)),
            out_specs=(P("gx", rows, None), P("gx", rows, None)),
            check_vma=False,
        )(point_counts, face_counts)

    return run
```

```python
import numpy as np
import jax
import jax.numpy as jnp
from jax import lax
from jax.experimental import pallas as pl
from jax.experimental.pallas import tpu as pltpu
from jax.sharding import Mesh, PartitionSpec as P

F32 = jnp.float32
BF16 = jnp.bfloat16
LANES = 128
HALO = 8
COARSE_ITERS = 6

screen_weight = 0.25
flux_scale = 0.125
low_edge = 0.3
high_edge = 2.0
centre = 0.5 * (high_edge + low_edge)
radius = 0.5 * (high_edge - low_edge)
ratio = centre / radius
mom_first = 1.0 / ratio
mom_second = 1.0 / (2.0 * ratio - mom_first)
keep = mom_second * mom_first
gain = 2.0 * mom_second / radius

VMEM = pl.BlockSpec(memory_space=pltpu.VMEM)
SMEM = pl.BlockSpec(memory_space=pltpu.SMEM)
FAR = pl.BlockSpec(memory_space=pltpu.HBM)


def transfer_matrix(level):
    pack, size_z = 1 << level, LANES >> level
    planes = 2 if level == 0 else 4
    out = np.zeros((planes * LANES, LANES), np.float32)
    for j in range(planes):
        for q in range(pack):
            coarse = j if level == 0 else (j * pack + q) // 2
            for z in range(size_z):
                out[j * LANES + q * size_z + z, coarse * (size_z // 2) + z // 2] = 1.0
    return jnp.asarray(out, BF16)


def in_parts(value):
    high = value.astype(BF16)
    rest = value - high.astype(F32)
    middle = rest.astype(BF16)
    return jnp.concatenate([high, middle, (rest - middle.astype(F32)).astype(BF16)], 0)


def add_parts(value, rows):
    return value[:rows] + (value[rows : 2 * rows] + value[2 * rows :])


def gather_lanes(value, matrix):
    return add_parts(jnp.dot(in_parts(value), matrix, preferred_element_type=F32), value.shape[0])


def spread_lanes(value, matrix):
    dims = (((1,), (1,)), ((), ()))
    return add_parts(lax.dot_general(in_parts(value), matrix, dims, preferred_element_type=F32), value.shape[0])


def lane_index():
    return lax.broadcasted_iota(jnp.int32, (1, LANES), 1)


def z_sum(value, size_z):
    lane = lane_index() & (size_z - 1)
    inner_low = (lane != 0).astype(F32)
    inner_high = (lane != size_z - 1).astype(F32)
    return pltpu.roll(value, 1, 1) * inner_low + pltpu.roll(value, LANES - 1, 1) * inner_high


def x_sum(before, here, after, size_z):
    if size_z == LANES:
        return before + after
    lane = lax.broadcasted_iota(jnp.int32, here.shape, 1)
    if 2 * size_z == LANES:
        return pltpu.roll(here + jnp.where(lane < size_z, after, before), size_z, 1)
    up = pltpu.roll(jnp.where(lane < size_z, after, here), LANES - size_z, 1)
    down = pltpu.roll(jnp.where(lane >= LANES - size_z, before, here), size_z, 1)
    return up + down


def neighbours(ref, base, rows, stride, size_z):
    here = ref[pl.ds(base, rows), :]
    total = x_sum(ref[pl.ds(base - stride, rows), :], here, ref[pl.ds(base + stride, rows), :], size_z)
    total = total + (ref[pl.ds(base - 1, rows), :] + ref[pl.ds(base + 1, rows), :])
    return here, total + z_sum(here, size_z)


def for_planes(count, body, limit=64):
    if count <= limit:
        for i in range(count):
            body(i)
    else:
        step = 8

        def block(k, carry):
            for j in range(step):
                body(k * step + j)
            return carry

        lax.fori_loop(0, count // step, block, 0)


def pair_rows(ref, start, rows):
    return ref[pl.ds(start, rows // 2, stride=2), :] + ref[pl.ds(start + 1, rows // 2, stride=2), :]


def pack_cell(faces, points):
    word = points << 18
    for c in range(3):
        word = word + ((faces[c] + 32) << (6 * c))
    return word


def cells_kernel(place, words, first, second, part, count, edge):
    size_x, size_y = words.shape[:2]
    lane = lax.broadcasted_iota(jnp.int32, (size_y, LANES), 1)
    row = lax.broadcasted_iota(jnp.int32, (size_y, LANES), 0)
    last_x = None
    for i in range(size_x):
        word = words[i]
        along_x, along_y, along_z = [((word >> (6 * c)) & 63) - 32 for c in range(3)]
        total = jnp.where(row != 0, pltpu.roll(along_y, 1, 0), 0) - along_y
        total = total + (jnp.where(lane != 0, pltpu.roll(along_z, 1, 1), 0) - along_z) - along_x
        if last_x is not None:
            total = total + last_x
        last_x = along_x
        part[i] = total.astype(F32).astype(BF16)
        count[i] = ((word >> 18) + 1).astype(F32).astype(BF16)
    edge[0] = last_x.astype(F32).astype(BF16)
    edge[1] = (((words[:, size_y - 1, :] >> 6) & 63) - 32).astype(F32).astype(BF16)

    def write(up, down):
        for target, start in ((up, size_x - HALO), (down, 0)):
            target[0:HALO] = part[start : start + HALO]
            target[HALO : 2 * HALO] = count[start : start + HALO]
            target[2 * HALO : 2 * HALO + 2] = edge[...]

    odd = 1 - place[0] % 2

    @pl.when(odd == 0)
    def _():
        write(first, second)

    @pl.when(odd == 1)
    def _():
        write(second, first)


def plane_slot(i, wide):
    size_x = wide - 2 * HALO
    if HALO <= i < HALO + size_x:
        return i - HALO, None
    distance = HALO - i if i < HALO else i - HALO - size_x + 1
    near = min(distance, HALO + 1 - distance)
    slot = size_x + near - 1 + (0 if i < HALO else HALO // 2)
    return slot, (near if near != distance else None)


def wide_kernel(place, got_first, got_second, part, count, edge, first, second, part_x, count_x, edge_x):
    size_x, size_y = part.shape[:2]
    wide = size_x + 2 * HALO

    def fill(below, above):
        part_x[0:HALO] = below[0:HALO]
        part_x[HALO + size_x :] = above[0:HALO]
        count_x[0:HALO] = below[HALO : 2 * HALO]
        count_x[HALO + size_x :] = above[HALO : 2 * HALO]
        part_x[HALO : HALO + size_x] = part[...]
        count_x[HALO : HALO + size_x] = count[...]
        part_x[HALO] = (part[0].astype(F32) + below[2 * HALO].astype(F32)).astype(BF16)
        part_x[HALO + size_x] = (above[0].astype(F32) + edge[0].astype(F32)).astype(BF16)
        edge_x[0:HALO] = below[2 * HALO + 1].astype(F32)[size_x - HALO :]
        edge_x[HALO : HALO + size_x] = edge[1].astype(F32)
        edge_x[HALO + size_x :] = above[2 * HALO + 1].astype(F32)[:HALO]

    odd = 1 - place[0] % 2

    @pl.when(odd == 0)
    def _():
        fill(got_second, got_first)

    @pl.when(odd == 1)
    def _():
        fill(got_first, got_second)

    def write(up, down):
        row = lax.broadcasted_iota(jnp.int32, (HALO, LANES), 0)
        for i in range(wide):
            slot, far = plane_slot(i, wide)
            if far is not None:
                continue
            pairs = [(part_x[i].astype(F32), count_x[i].astype(F32))]
            for k in range(wide):
                other, d = plane_slot(k, wide)
                if other == slot and d is not None:
                    pairs.append((part_x[k].astype(F32), count_x[k].astype(F32)))
                    break
            tops = [[value[size_y - HALO :] for value in pair] for pair in pairs]
            ends = [[value[:HALO] for value in pair] for pair in pairs]
            if len(pairs) == 2:
                tops[0] = [jnp.where(row >= d, a, pltpu.roll(b, d - 1, 0)) for a, b in zip(*tops)]
                ends[0] = [jnp.where(row < HALO - d, a, pltpu.roll(b, HALO + 1 - d, 0)) for a, b in zip(*ends)]
            up[slot] = jnp.concatenate(tops[0], 0).astype(BF16)
            down[slot] = jnp.concatenate(ends[0], 0).astype(BF16)
        for target in (up, down):
            for j in range(wide // size_y):
                target[wide - HALO + j] = edge_x[j * size_y : (j + 1) * size_y].astype(BF16)

    odd_y = 1 - place[1] % 2

    @pl.when(odd_y == 0)
    def _():
        write(first, second)

    @pl.when(odd_y == 1)
    def _():
        write(second, first)


def finest_parts(margin, wide, plane):
    planes = range(HALO - margin, wide - HALO + margin)
    if margin > 4:
        return [(8 + i * plane, 2 * plane) for i in planes[::2]]
    return [(8 + i * plane + HALO - 4, plane - 2 * HALO + 8) for i in planes]


def finest_step_one(source, target, field, scaled, margin, wide, plane):
    for base, rows in finest_parts(margin, wide, plane):
        at = pl.ds(base, rows)
        here, total = neighbours(source, base, rows, plane, LANES)
        fit = (field[at, :] + total) * scaled[at, :]
        target[at, :] = here + (fit - here) * (1.0 / centre)


def finest_step_two(source, old, field, scaled, margin, wide, plane):
    for base, rows in finest_parts(margin, wide, plane):
        at = pl.ds(base, rows)
        here, total = neighbours(source, base, rows, plane, LANES)
        fit = (field[at, :] + total) * scaled[at, :]
        old[at, :] = here + (keep * (here - old[at, :]) + gain * (fit - here))


def finest_step_two_from_zero(source, target, field, scaled, margin, wide, plane):
    for base, rows in finest_parts(margin, wide, plane):
        at = pl.ds(base, rows)
        here, total = neighbours(source, base, rows, plane, LANES)
        fit = (field[at, :] + total) * scaled[at, :]
        target[at, :] = here + (keep * here + gain * (fit - here))


def finest_residual(iterate, field, count, size_x, size_y, write):
    plane = size_y + 2 * HALO
    for i in range(size_x):
        base = 8 + (HALO + i) * plane + HALO
        here, total = neighbours(iterate, base, size_y, plane, LANES)
        diag = 6.0 + screen_weight * (count[HALO + i].astype(F32) - 1.0)
        write(i, here, field[pl.ds(base, size_y), :] + total - diag * here)


def restrict_finest(rows_ref, size_x, size_y, matrix):
    half = pair_rows(rows_ref, 0, size_x * size_y).reshape(size_x // 4, 4, size_y // 2, LANES)
    even = (half[:, 0] + half[:, 1]).reshape(-1, LANES)
    odd = (half[:, 2] + half[:, 3]).reshape(-1, LANES)
    return even, odd


def inverse_diag(count):
    return jnp.where(count > 0.0, 1.0 / (6.0 - screen_weight + screen_weight * count), 0.0)


def columns_kernel(place, count_x, matrix, inverse_x, points, rows_ref):
    wide, size_y = count_x.shape[:2]
    size_x = wide - 2 * HALO
    for i in range(wide):
        inverse_x[i] = inverse_diag(count_x[i].astype(F32))
    for i in range(size_x):
        rows_ref[pl.ds(i * size_y, size_y), :] = count_x[HALO + i].astype(F32) - 1.0
    even, odd = restrict_finest(rows_ref, size_x, size_y, matrix)
    points[...] = jnp.dot(jnp.concatenate([even, odd], 1).astype(BF16), matrix[...], preferred_element_type=F32)


def first_step(place, got, part_x, inverse_x, edge_x, iterate, field, inverse, margin):
    wide, size_y = part_x.shape[:2]
    plane = size_y + 2 * HALO
    even = place[1] % 2 == 1
    top = lax.broadcasted_iota(jnp.int32, (HALO, LANES), 0) == 0
    under_rows = [
        jnp.where(even, got[1][wide - HALO + j], got[0][wide - HALO + j]).astype(F32) for j in range(wide // size_y)
    ]
    for i in range(HALO - margin, wide - HALO + margin):
        slot, d = plane_slot(i, wide)
        below = jnp.where(even, got[1][slot], got[0][slot]).astype(F32)
        above = jnp.where(even, got[0][slot], got[1][slot]).astype(F32)
        if d is not None:
            below = jnp.concatenate([pltpu.roll(part, HALO + 1 - d, 0) for part in (below[:HALO], below[HALO:])], 0)
            above = jnp.concatenate([pltpu.roll(part, d - 1, 0) for part in (above[:HALO], above[HALO:])], 0)
        own = part_x[i].astype(F32)
        under = under_rows[i // size_y][i % size_y : i % size_y + 1]
        over = edge_x[i : i + 1]
        cells = jnp.concatenate(
            [
                below[:HALO],
                own[:HALO] + jnp.where(top, under, 0.0),
                own[HALO:],
                above[:HALO] + jnp.where(top, over, 0.0),
            ],
            0,
        )
        given = flux_scale * cells
        inv = jnp.concatenate([inverse_diag(below[HALO:]), inverse_x[i], inverse_diag(above[HALO:])], 0)
        at = pl.ds(8 + i * plane, plane)
        field[at, :] = given
        inverse[at, :] = inv
        iterate[at, :] = (given * inv) * (1.0 / centre)


def start_kernel(
    place,
    got_first,
    got_second,
    part_x,
    inverse_x,
    edge_x,
    count_x,
    points,
    matrix,
    packet,
    first,
    second,
    field,
    inverse,
    rows_ref,
):
    wide, size_y = part_x.shape[:2]
    size_x = wide - 2 * HALO
    plane = size_y + 2 * HALO
    first_step(place, (got_first, got_second), part_x, inverse_x, edge_x, first, field, inverse, 2)
    finest_step_two_from_zero(first, second, field, inverse, 1, wide, plane)

    def write(i, here, value):
        rows_ref[pl.ds(i * size_y, size_y), :] = value

    finest_residual(second, field, count_x, size_x, size_y, write)
    even, odd = restrict_finest(rows_ref, size_x, size_y, matrix)
    coarse = 0.125 * gather_lanes(jnp.concatenate([even, odd], 1), matrix[...])
    send_coarse(packet, coarse, points[...], size_y // 2)


def surroundings_kernel(
    place, after, got_first, got_second, part_x, inverse_x, edge_x, iterate, field, inverse, first
):
    wide, size_y = part_x.shape[:2]
    plane = size_y + 2 * HALO
    zero = jnp.zeros((8, LANES), F32)
    for ref in (iterate, field, inverse, first):
        ref[0:8] = zero
        ref[8 + wide * plane :] = zero
    first_step(place, (got_first, got_second), part_x, inverse_x, edge_x, first, field, inverse, HALO)
    for base, rows in ((8, plane), (8 + (wide - 1) * plane, plane)):
        iterate[pl.ds(base, rows), :] = first[pl.ds(base, rows), :]
    finest_step_two_from_zero(first, iterate, field, inverse, HALO - 1, wide, plane)


def scale_of(code):
    return jnp.exp2(code * (1.0 / 128.0))


def send_coarse(packet, coarse, points, size_y):
    copies = packet.shape[0]
    tiles = [coarse[i : i + size_y] for i in range(0, coarse.shape[0], size_y)]
    largest = jnp.abs(tiles[0])
    for tile in tiles[1:]:
        largest = jnp.maximum(largest, jnp.abs(tile))
    largest = jnp.maximum(jnp.max(largest, 1, keepdims=True), 1e-30)
    code = jnp.ceil(128.0 * jnp.log2(largest * (1.0 / 32766.0)))
    scale = scale_of(-code)
    rows = [jnp.round(tile * scale) for tile in tiles]
    rows += [jnp.broadcast_to(code, (size_y, LANES)), jnp.zeros((size_y, LANES), F32)]
    if points is not None:
        rows += [points[i : i + size_y] for i in range(0, points.shape[0], size_y)]
    for i in range(0, len(rows), 2):
        tile = jnp.concatenate(rows[i : i + 2], 0).astype(jnp.int32).astype(jnp.int16)
        for k in range(copies):
            packet[k, i // 2] = tile


def packed_apply(value, screen, factor, size_z):
    planes, size_y, _ = value.shape
    flat = value.reshape(planes * size_y, LANES)
    empty = jnp.zeros((1, size_y, LANES), F32)
    if planes > 1:
        before = jnp.concatenate([empty, value[:-1]], 0).reshape(flat.shape)
        after = jnp.concatenate([value[1:], empty], 0).reshape(flat.shape)
    else:
        before = after = jnp.zeros_like(flat)
    row = lax.broadcasted_iota(jnp.int32, value.shape, 1)
    along_y = jnp.where(row != 0, pltpu.roll(value, 1, 1), 0.0) + jnp.where(
        row != size_y - 1, pltpu.roll(value, size_y - 1, 1), 0.0
    )
    total = x_sum(before, flat, after, size_z) + z_sum(flat, size_z)
    return (6.0 * value - (total.reshape(value.shape) + along_y)) * factor + screen * value


def totals_of(*values):
    rows = jnp.concatenate([jnp.sum(value, 0) for value in values], 0)
    sums = jnp.sum(rows, 1, keepdims=True).reshape(len(values), -1, 1)
    sums = jnp.sum(sums, 1, keepdims=True)
    return [sums[i : i + 1] for i in range(len(values))]


def conjugate_gradients(target, screen, factor, size_z):
    planes, size_y, _ = target.shape
    least = sum(2.0 - 2.0 * np.cos(np.pi / (n + 1)) for n in (planes * (LANES // size_z), size_y, size_z))
    longest = 1.001 / (factor * least)
    remain = target
    image = packed_apply(remain, screen, factor, size_z)
    for step in range(COARSE_ITERS):
        more = step + 1 < COARSE_ITERS
        norm, bent = totals_of(remain * remain, remain * image)
        if more:
            ahead = packed_apply(image, screen, factor, size_z)
        if step == 0:
            length = norm / bent
            search, search_image, search_ahead = remain, image, ahead
            iterate = length * search
        else:
            ratio = norm / norm_before
            length = jnp.clip(norm / (bent - ratio * norm / length), 0.0, longest)
            search = remain + ratio * search
            iterate = iterate + length * search
            if more:
                search_image = image + ratio * search_image
                search_ahead = ahead + ratio * search_ahead
        if more:
            remain = remain - length * search_image
            image = image - length * search_ahead
        norm_before = norm
    return iterate


def add_lanes(rows_ref, planes, size_y, matrix, first_plane=0):
    half = pair_rows(rows_ref, first_plane * size_y, planes * size_y).reshape(planes // 4, 4, size_y // 2, LANES)
    wide = jnp.concatenate([half[:, j].reshape(-1, LANES) for j in range(4)], 1)
    return gather_lanes(wide, matrix[...]).reshape(planes // 4, size_y // 2, LANES)


def copy_level(value, matrix):
    planes, size_y, _ = value.shape
    wide = spread_lanes(value.reshape(-1, LANES), matrix[...]).reshape(planes, size_y, 4 * LANES)
    return jnp.stack([wide[:, :, j * LANES : (j + 1) * LANES] for j in range(4)], 1).reshape(
        4 * planes, size_y, LANES
    )


class Sizes:
    def __init__(self, mesh_x, mesh_y, size_x, size_y):
        self.mesh_x, self.mesh_y = mesh_x, mesh_y
        self.own_x, self.own_y = size_x // 4, size_y // 2
        self.planes, self.rows = mesh_x * self.own_x, mesh_y * self.own_y
        self.stride = self.rows + 8
        self.flat = (self.planes + 8) * self.stride + 8
        self.pad_x = 4


def level_one(place, gathered, sizes, mats, refs, first):
    mat_1, mat_2 = mats
    given, inverse, diag, step, iterate, rows_ref, level_two, local_a, local_b, two_a, two_b = refs
    size_z = LANES // 2
    factor = 0.25
    planes, rows, stride, pad = sizes.planes, sizes.rows, sizes.stride, sizes.pad_x
    own_x, own_y = sizes.own_x, sizes.own_y

    def clear(ref):
        ref[0 : pad * stride + 8] = jnp.zeros((pad * stride + 8, LANES), F32)
        ref[(pad + planes) * stride :] = jnp.zeros((pad * stride + 8, LANES), F32)

        def gap(i):
            ref[pl.ds((pad + i) * stride, 8), :] = jnp.zeros((8, LANES), F32)

        for_planes(planes, gap)

    for ref in (given, step, iterate) + ((inverse, diag) if first else ()):
        clear(ref)

    core = place[1] % 2
    per_core = sizes.mesh_x * sizes.mesh_y // 2

    def block(b):
        source, side = (gathered[0], core) if b < per_core else (gathered[1], 1 - core)
        gx = b % per_core // (sizes.mesh_y // 2)
        gy = 2 * (b % (sizes.mesh_y // 2)) + side
        tiles = []
        for i in range(source.shape[1]):
            tile = source[b % per_core, i].astype(jnp.int32).astype(F32)
            tiles += [tile[:own_y], tile[own_y:]]
        scale = scale_of(tiles[own_x])
        for i in range(own_x):
            start = (pad + gx * own_x + i) * stride + 8 + gy * own_y
            at = pl.ds(pl.multiple_of(start, 8), own_y)
            value = tiles[i] * scale
            if first:
                d = 6.0 * factor + (screen_weight * 0.125) * tiles[own_x + 2 + i]
                diag[at, :] = d
                inv = 1.0 / d
                inverse[at, :] = inv
            else:
                inv = inverse[at, :]
            given[at, :] = value
            step[at, :] = value * inv * (1.0 / centre)

    for b in range(sizes.mesh_x * sizes.mesh_y):
        block(b)

    def second(i):
        base = (pad + i) * stride + 8
        at = pl.ds(base, rows)
        here, total = neighbours(step, base, rows, stride, size_z)
        fit = (given[at, :] + factor * total) * inverse[at, :]
        iterate[at, :] = here + (keep * here + gain * (fit - here))

    for_planes(planes, second)

    def residual(i):
        base = (pad + i) * stride + 8
        at = pl.ds(base, rows)
        here, total = neighbours(iterate, base, rows, stride, size_z)
        rows_ref[pl.ds(i * rows, rows), :] = given[at, :] + factor * total - diag[at, :] * here

    groups = 4 if planes <= 64 else 1
    if groups == 1:
        for_planes(planes, residual)
    targets = []
    for k in range(groups):
        for i in range(k * planes // groups, (k + 1) * planes // groups if groups > 1 else 0):
            residual(i)
        targets.append(add_lanes(rows_ref, planes // groups, rows, mat_1, k * planes // groups))
    target = 0.125 * jnp.concatenate(targets, 0)

    screen_two, screen_three = level_two
    if first:

        def screens(i):
            at = pl.ds((pad + i) * stride + 8, rows)
            rows_ref[pl.ds(i * rows, rows), :] = diag[at, :] - 6.0 * factor

        for_planes(planes, screens)
        screen_two[...] = 0.125 * add_lanes(rows_ref, planes, rows, mat_1)
    planes_2, rows_2 = planes // 4, rows // 2
    screen = screen_two[...]
    level = 6.0 * factor**2 + screen
    inv = 1.0 / level
    if first:
        rows_ref[0 : planes_2 * rows_2] = screen.reshape(-1, LANES)
        screen_three[...] = 0.125 * add_lanes(rows_ref, planes_2, rows_2, mat_2)
    stride_2 = rows_2 + 8

    def at_2(i):
        return (1 + i) * stride_2 + 8

    for ref in (two_a, two_b):
        for start, count in ((0, stride_2 + 8), ((planes_2 + 1) * stride_2, stride_2 + 8)):
            ref[start : start + count] = jnp.zeros((count, LANES), F32)
        for i in range(planes_2):
            ref[at_2(i) - 8 : at_2(i)] = jnp.zeros((8, LANES), F32)

    def fit_two(ref, i):
        here, total = neighbours(ref, at_2(i), rows_2, stride_2, LANES // 4)
        return here, (target[i] + factor**2 * total) * inv[i]

    for i in range(planes_2):
        two_a[pl.ds(at_2(i), rows_2), :] = target[i] * inv[i] * (1.0 / centre)
    for i in range(planes_2):
        here, fit = fit_two(two_a, i)
        two_b[pl.ds(at_2(i), rows_2), :] = here + (keep * here + gain * (fit - here))
    for i in range(planes_2):
        here, total = neighbours(two_b, at_2(i), rows_2, stride_2, LANES // 4)
        rows_ref[i * rows_2 : (i + 1) * rows_2] = target[i] + factor**2 * total - level[i] * here
    target_3 = 0.125 * add_lanes(rows_ref, planes_2, rows_2, mat_2)
    error = conjugate_gradients(target_3, screen_three[...], factor**3, LANES // 8)
    error = copy_level(error, mat_2).reshape(-1, LANES)
    count = planes_2 * rows_2
    rows_ref[pl.ds(0, count // 2, stride=2), :] = error
    rows_ref[pl.ds(1, count // 2, stride=2), :] = error
    for i in range(planes_2):
        two_a[pl.ds(at_2(i), rows_2), :] = two_b[pl.ds(at_2(i), rows_2), :] + rows_ref[i * rows_2 : (i + 1) * rows_2]
    for i in range(planes_2):
        here, fit = fit_two(two_a, i)
        two_b[pl.ds(at_2(i), rows_2), :] = here + (fit - here) * (1.0 / centre)

    rows_ref[0:rows_2] = jnp.zeros((rows_2, LANES), F32)
    rows_ref[(planes_2 + 1) * rows_2 : (planes_2 + 2) * rows_2] = jnp.zeros((rows_2, LANES), F32)
    for i in range(planes_2):
        here, fit = fit_two(two_b, i)
        before = two_a[pl.ds(at_2(i), rows_2), :]
        rows_ref[(i + 1) * rows_2 : (i + 2) * rows_2] = here + (keep * (here - before) + gain * (fit - here))
    near_2 = own_x // 4 + 2
    start = pl.multiple_of(place[0] * (own_x // 4) * rows_2, 8)
    near = rows_ref[pl.ds(start, near_2 * rows_2), :].reshape(near_2, rows_2, LANES)
    error = copy_level(near, mat_1)
    near_x, near_y = 4 * near_2, own_y + 16
    first_plane = place[0] * own_x
    for i in range(near_x):
        base = (first_plane + i) * stride + 8
        even, odd = pl.ds(base, rows_2, stride=2), pl.ds(base + 1, rows_2, stride=2)
        iterate[even, :] = iterate[even, :] + error[i]
        iterate[odd, :] = iterate[odd, :] + error[i]
    for i in range(near_x):
        at = pl.ds(pl.multiple_of((first_plane + i) * stride + place[1] * own_y, 8), near_y)
        local_a[pl.ds(8 + i * near_y, near_y), :] = iterate[at, :]
    for ref in (local_a, local_b):
        ref[0:8] = jnp.zeros((8, LANES), F32)
        ref[8 + near_x * near_y :] = jnp.zeros((8, LANES), F32)
    ends = pl.ds(8, near_y), pl.ds(8 + (near_x - 1) * near_y, near_y)
    for at in ends:
        local_b[at, :] = jnp.zeros((near_y, LANES), F32)

    def fit_of(ref, i):
        at = pl.ds(pl.multiple_of((first_plane + i) * stride + place[1] * own_y, 8), near_y)
        here, total = neighbours(ref, 8 + i * near_y, near_y, near_y, size_z)
        return here, (given[at, :] + factor * total) * inverse[at, :]

    for i in range(1, near_x - 1):
        here, fit = fit_of(local_a, i)
        local_b[pl.ds(8 + i * near_y, near_y), :] = here + (fit - here) * (1.0 / centre)
    for i in range(2, near_x - 2):
        here, fit = fit_of(local_b, i)
        at = pl.ds(8 + i * near_y, near_y)
        local_a[at, :] = here + (keep * (here - local_a[at, :]) + gain * (fit - here))


def add_correction(start, iterate, local, sizes, mat_0, plane):
    ends = pl.ds(0, 8), pl.ds(start.shape[0] - 8, 8)
    for at in ends:
        iterate[at, :] = start[at, :]
    near_y = sizes.own_y + 16
    half_y = plane // 2
    planes = sizes.own_x + 4
    value = jnp.concatenate(
        [local[pl.ds(8 + (2 + i) * near_y + 4, half_y), :] for i in range(planes)], 0
    )
    wide = spread_lanes(value, mat_0[...])
    for i in range(planes):
        for j in range(4):
            error = wide[i * half_y : (i + 1) * half_y, (j // 2) * LANES : (j // 2 + 1) * LANES]
            for side in (0, 1):
                at = pl.ds(8 + (4 * i + j) * plane + side, half_y, stride=2)
                iterate[at, :] = start[at, :] + error


def middle_kernel(sizes, place, near, far, start, field, scaled, count_x, mat_0, mat_1, mat_2, *rest):
    iterate, packet, inverse, diag, screen_two, screen_three = rest[:6]
    given, step, coarse, rows_ref, local_a, local_b, two_a, two_b, other, fine_rows = rest[6:]
    wide, size_y = count_x.shape[:2]
    size_x = wide - 2 * HALO
    plane = size_y + 2 * HALO
    refs = (given, inverse, diag, step, coarse, rows_ref, (screen_two, screen_three), local_a, local_b, two_a, two_b)
    level_one(place, (near, far), sizes, (mat_1, mat_2), refs, True)
    add_correction(start, iterate, local_a, sizes, mat_0, plane)
    finest_step_one(iterate, other, field, scaled, 6, wide, plane)
    finest_step_two(other, iterate, field, scaled, 5, wide, plane)
    finest_step_one(iterate, other, field, scaled, 4, wide, plane)
    finest_step_two(other, iterate, field, scaled, 3, wide, plane)

    def write(i, here, value):
        fine_rows[pl.ds(i * size_y, size_y), :] = value

    finest_residual(iterate, field, count_x, size_x, size_y, write)
    even, odd = restrict_finest(fine_rows, size_x, size_y, mat_0)
    send_coarse(packet, 0.125 * gather_lanes(jnp.concatenate([even, odd], 1), mat_0[...]), None, size_y // 2)


def last_kernel(sizes, place, near, far, start, field, scaled, count_x, inverse, diag, screen_two, screen_three, *rest):
    mat_0, mat_1, mat_2, solution_far, residual_far = rest[:5]
    given, step, coarse, rows_ref, local_a, local_b, two_a, two_b, iterate, other = rest[5:15]
    solution_out, residual_out, left = rest[15:]
    wide, size_y = count_x.shape[:2]
    size_x = wide - 2 * HALO
    plane = size_y + 2 * HALO
    refs = (given, inverse, diag, step, coarse, rows_ref, (screen_two, screen_three), local_a, local_b, two_a, two_b)
    level_one(place, (near, far), sizes, (mat_1, mat_2), refs, False)
    add_correction(start, iterate, local_a, sizes, mat_0, plane)
    finest_step_one(iterate, other, field, scaled, 2, wide, plane)
    finest_step_two(other, iterate, field, scaled, 1, wide, plane)

    def send(source, target, which):
        copy = pltpu.make_async_copy(source, target, left.at[which])
        copy.start()
        return copy

    copies = []

    def write(i, here, value):
        solution_out[i] = here
        residual_out[i] = value
        if (4 * i + 4) % size_x == 0:
            part = pl.ds(i + 1 - size_x // 4, size_x // 4)
            number = (i + 1) * 4 // size_x - 1
            copies.append(send(solution_out.at[part], solution_far.at[part], 2 * number))
            copies.append(send(residual_out.at[part], residual_far.at[part], 2 * number + 1))

    finest_residual(iterate, field, count_x, size_x, size_y, write)
    for copy in copies:
        copy.wait()


def exchange(first, second, axis):
    count = lax.axis_size(axis)

    def pairs(start):
        found = []
        for i in range(start, count - 1, 2):
            found += [(i, i + 1), (i + 1, i)]
        return found

    return lax.ppermute(first, axis, pairs(1)), lax.ppermute(second, axis, pairs(0))


def gather(packet):
    near = lax.all_to_all(packet, ("gx", "gy_chip"), 0, 0, tiled=True)
    return near, lax.ppermute(near, "gy_core", [(0, 1), (1, 0)])


def per_device(point_counts, face_counts):
    size_x, size_y, size_z = point_counts.shape
    assert size_z == LANES and size_x == 16 and size_y == 16
    mesh_x = lax.axis_size("gx")
    mesh_y = lax.axis_size("gy_chip") * lax.axis_size("gy_core")
    gx = lax.axis_index("gx")
    gy = lax.axis_index("gy_chip") * 2 + lax.axis_index("gy_core")
    place = jnp.stack([gx, gy]).astype(jnp.int32)
    wide, plane = size_x + 2 * HALO, size_y + 2 * HALO
    flat = 16 + wide * plane
    sizes = Sizes(mesh_x, mesh_y, size_x, size_y)
    copies = mesh_x * mesh_y // 2
    mats = [transfer_matrix(level) for level in range(3)]
    params = pltpu.CompilerParams(vmem_limit_bytes=(24 if sizes.flat < 4096 else 56) * 2**20)

    def call(kernel, outs, scratch, *args, copies=0, far_out=False, cost=None):
        return pl.pallas_call(
            kernel,
            out_shape=[jax.ShapeDtypeStruct(shape, dtype) for shape, dtype in outs],
            in_specs=[SMEM] + [VMEM] * (len(args) - 1),
            out_specs=[FAR if far_out else VMEM] * len(outs),
            scratch_shapes=[pltpu.VMEM(shape, dtype) for shape, dtype in scratch]
            + ([pltpu.SemaphoreType.DMA((copies,))] if copies else []),
            compiler_params=params,
            cost_estimate=cost,
        )(*args)

    beside = pl.CostEstimate(flops=1 << 22, bytes_accessed=4 << 20, transcendentals=0)
    cells = (size_x, size_y, LANES)
    packet = (2 * HALO + 2, size_y, LANES)
    first, second, part, count, edge = call(
        cells_kernel,
        [(packet, BF16), (packet, BF16), (cells, BF16), (cells, BF16), ((2, size_y, LANES), BF16)],
        [],
        place,
        pack_cell(face_counts, point_counts),
    )
    first, second = exchange(first, second, "gx")
    packet = (wide - HALO + wide // size_y, size_y, LANES)
    strip = (wide, size_y, LANES)
    first, second, part_x, count_x, edge_x = call(
        wide_kernel,
        [(packet, BF16), (packet, BF16), (strip, BF16), (strip, BF16), ((wide, LANES), F32)],
        [],
        place,
        first,
        second,
        part,
        count,
        edge,
    )
    first, second = exchange(first, second, ("gy_chip", "gy_core"))
    own = sizes.own_x
    flat_f32 = ((flat, LANES), F32)
    inverse_x, points = call(
        columns_kernel,
        [(strip, F32), ((own * sizes.own_y, LANES), F32)],
        [((size_x * size_y, LANES), F32)],
        place,
        count_x,
        mats[0],
        cost=beside,
    )
    received = (first, second, part_x, inverse_x, edge_x)
    (packet,) = call(
        start_kernel,
        [((copies, own + 1, 2 * sizes.own_y, LANES), jnp.int16)],
        [flat_f32] * 4 + [((size_x * size_y, LANES), F32)],
        place,
        *received,
        count_x,
        points,
        mats[0],
    )
    near, far = gather(packet)
    iterate, field, scaled = call(
        surroundings_kernel,
        [flat_f32] * 3,
        [flat_f32],
        place,
        near,
        *received,
        cost=beside,
    )
    level = (sizes.flat, LANES)
    flat_two = ((sizes.planes // 4 + 2) * (sizes.rows // 2 + 8) + 8, LANES)
    around = (16 + (own + 8) * (sizes.own_y + 16), LANES)
    scratch = [
        (level, F32),
        (level, F32),
        (level, F32),
        ((sizes.planes * sizes.rows, LANES), F32),
        (around, F32),
        (around, F32),
        (flat_two, F32),
        (flat_two, F32),
        ((flat, LANES), F32),
    ]
    level_two = (sizes.planes // 4, sizes.rows // 2, LANES)
    level_three = (sizes.planes // 16, sizes.rows // 4, LANES)
    iterate, packet, inverse, diag, screen_two, screen_three = call(
        lambda *refs: middle_kernel(sizes, *refs),
        [
            ((flat, LANES), F32),
            ((copies, own // 2 + 1, 2 * sizes.own_y, LANES), jnp.int16),
            (level, F32),
            (level, F32),
            (level_two, F32),
            (level_three, F32),
        ],
        scratch + [((size_x * size_y, LANES), F32)],
        place,
        near,
        far,
        iterate,
        field,
        scaled,
        count_x,
        *mats,
    )
    solution_own, residual_own = call(
        lambda *refs: last_kernel(sizes, *refs),
        [(cells, F32), (cells, F32)],
        scratch + [((flat, LANES), F32), (cells, F32), (cells, F32)],
        place,
        *gather(packet),
        iterate,
        field,
        scaled,
        count_x,
        inverse,
        diag,
        screen_two,
        screen_three,
        *mats,
        copies=8,
        far_out=True,
    )
    return solution_own, residual_own


def solution(mesh):
    mesh_x, mesh_y = mesh.shape["gx"], mesh.shape["gy"]
    split = Mesh(mesh.devices.reshape(mesh_x, mesh_y // 2, 2), ("gx", "gy_chip", "gy_core"))
    rows = ("gy_chip", "gy_core")

    def run(point_counts, face_counts):
        return jax.shard_map(
            per_device,
            mesh=split,
            in_specs=(P("gx", rows, None), P(None, "gx", rows, None)),
            out_specs=(P("gx", rows, None), P("gx", rows, None)),
            check_vma=False,
        )(point_counts, face_counts)

    return run
```
